32 devices in a mesh: vol: 8 (over z, y), dsg: 4 (over x, core).
Axes of the slice: x: 2, y: 2, z: 4, core: 2. Of those that a mesh axis runs over, the one named last changes fastest.
Arguments:
- fields: float32 [32768, 128], P('vol'), may hold values from -6 to 6
- far_geom: float32 [8, 16384], P(None, ('vol', 'dsg')), may hold values from -6 to 6, as said below
- far_block: int32 [16384, 1], P(('vol', 'dsg')), may hold values from 0 to 7; in each aligned block of 512 rows (0 to 511, 512 to 1023, ...) at most 160 rows name the same one
- far_cell: int32 [16384], P(('vol', 'dsg')), may hold values from 0 to 4095
- far_patch: int32 [16384], P(('vol', 'dsg')), may hold values from 0 to 95, as said below
- near_geom: float32 [8, 65536], P(None, ('vol', 'dsg')), may hold values from -6 to 6, as said below
- near_cell: int32 [65536], P(('vol', 'dsg')), may hold values from 0 to 4095
- near_patch: int32 [65536], P(('vol', 'dsg')), may hold values from 0 to 95, as said below
- adjacency: int32 [96, 4], replicated, may hold values from -1 to 95, as said below
Outputs:
- far_density: float32 [16384], P(('vol', 'dsg'))
- design_grad: float32 [96, 64, 64], P('dsg')
The draws below stay inside these ranges and needn't reach their ends.
Inputs may be any that keep to these rules, and one draw needn't show every extreme that they name: `far_geom`: rows 0-2 and 6-7 lie in [0, 1). `near_geom`: rows 0-2 and 6-7 lie in [0, 1). `far_block`: the 512 far points of one device name each block at most 160 times. `far_patch`: the far and near points of one device lie on at most 4 design patches, the same set for both. `near_patch`: the far and near points of one device lie on at most 4 design patches, the same set for both. -1 marks a free side; where adjacency[k, s] = m >= 0, adjacency[m, s xor 1] = k.
All inputs are finite; a program needn't handle non-finite values.
Results may differ from the reference program's by a relative error of at most 0.0003.
Values sent between devices are 32-bit elements; how exact they have to be, the bound alone decides.
No kernel may reach another device: no remote copies, remote signals or barrier semaphores. Data moves between devices by JAX's collectives and lax.ppermute only.
A program may use at most 128 MiB of HBM per device.

```python
import math
import jax
import jax.numpy as jnp
import numpy as np
from jax import lax

BASIS = 64
CELLS_DEV = 4096
PTS_DEV = 512
NEAR_DEV = 2048
CTRL = 64
CHORD_PATCHES = 12
SPAN_PATCHES = 8
PATCH_GRP = 4
SMOOTH_ITERS = 3
CAP = 160
CELLS = 32768
POINTS = 16384
NEAR = 65536
PATCHES = 96
N_VOL = 8
N_DSG = 4


def geometry(key, salt_value, point_total):
    base_key = jax.random.fold_in(key, salt_value)
    inside = jax.random.uniform(jax.random.fold_in(base_key, 1), (3, point_total), jnp.float32)
    normals = jnp.clip(1.5 * jax.random.normal(jax.random.fold_in(base_key, 2), (3, point_total), jnp.float32), -6.0, 6.0)
    surface = jax.random.uniform(jax.random.fold_in(base_key, 3), (2, point_total), jnp.float32)
    return jnp.concatenate([inside, normals, surface], 0)


def draw_far_geom(key, part):
    return geometry(key, 21, POINTS)


def draw_near_geom(key, part):
    return geometry(key, 22, NEAR)


def patch_choice(key, salt_value, per_device):
    device_keys = jax.random.split(jax.random.fold_in(key, 31), POINTS // PTS_DEV)
    groups = jax.vmap(lambda one_key: jax.random.permutation(one_key, PATCHES)[:PATCH_GRP])(device_keys)
    member = jax.random.randint(jax.random.fold_in(key, salt_value), (POINTS // PTS_DEV, per_device), 0, PATCH_GRP)
    return jnp.take_along_axis(groups.astype(jnp.int32), member, 1).reshape(-1).astype(jnp.int32)


def draw_far_patch(key, part):
    return patch_choice(key, 32, PTS_DEV)


def draw_near_patch(key, part):
    return patch_choice(key, 33, NEAR_DEV)


def draw_adjacency(key, part):
    placing = jax.random.permutation(jax.random.fold_in(key, 41), PATCHES).astype(jnp.int32)
    layout = placing.reshape(CHORD_PATCHES, SPAN_PATCHES)
    previous = jnp.roll(layout, 1, 0)
    following = jnp.roll(layout, -1, 0)
    free_side = jnp.full((CHORD_PATCHES, 1), -1, jnp.int32)
    lower_span = jnp.concatenate([free_side, layout[:, :-1]], 1)
    upper_span = jnp.concatenate([layout[:, 1:], free_side], 1)
    neighbour_ids = jnp.stack([previous, following, lower_span, upper_span], -1).reshape(PATCHES, 4)
    return jnp.zeros((PATCHES, 4), jnp.int32).at[placing].set(neighbour_ids)


def set_ends(result, key, low, top_value):
    extent = result.shape
    place = [jax.random.randint(jax.random.fold_in(key, axis), (), 0, extent[axis]) for axis in range(len(extent))]
    result = result.at[tuple(place)].set(low)
    longest = extent.index(max(extent))
    place[longest] = (place[longest] + 1) % extent[longest]
    return result.at[tuple(place)].set(top_value)


def levels(key, shape, pieces, smallest, high):
    def one(dim, shards_of):
        steps = jax.random.uniform(jax.random.fold_in(jax.random.fold_in(key, 6), dim), (shards_of,), jnp.float32, smallest / len(pieces), high / len(pieces))
        return jnp.repeat(jnp.exp(steps), shape[dim] // shards_of).reshape((-1,) + (1,) * (len(shape) - dim - 1))

    factor_of = one(*pieces[0])
    for cut in pieces[1:]:
        factor_of = factor_of * one(*cut)
    return factor_of


def shared_out(stream_key, own, number, rows, number_of, top, bound, skew):
    ranking = jax.random.permutation(stream_key, number_of)
    packed, common = portions_of(number_of, rows * top, bound, skew, True), portions_of(number_of, rows * top, bound, skew, False)
    places = jnp.arange(number_of)

    def named(tallies, offset_by):
        used = int((tallies > 0).sum())
        fixed = max(1, used // 4)
        moved = fixed + (places - fixed + offset_by * (used - fixed)) % max(1, number_of - fixed)
        return jnp.zeros((number_of,), jnp.int32).at[ranking[jnp.where(places < fixed, places, moved)]].set(jnp.asarray(tallies, jnp.int32))

    tallies = jnp.where(number % 4 == 0, named(packed, number // 4), named(common, number - number // 4 - 1))
    mixed = jax.random.permutation(jax.random.fold_in(own, 3), number_of)
    giver, receiver = mixed[0:number_of // 2 * 2:2], mixed[1:number_of // 2 * 2:2]
    margin = jnp.minimum(tallies[giver] - 1, bound - tallies[receiver]) // 2
    margin = jnp.where((giver == ranking[0]) | (receiver == ranking[0]) | (tallies[receiver] == 0), 0, jnp.maximum(margin, 0))
    moved = jax.random.randint(jax.random.fold_in(own, 4), (number_of // 2,), 0, 1 << 20) % (margin + 1)
    tallies = tallies.at[giver].add(-moved).at[receiver].add(moved)
    items = jnp.searchsorted(jnp.cumsum(tallies), jnp.arange(rows * top), side="right").astype(jnp.int32)
    table = items.reshape(top, rows).T
    table = table[jax.random.permutation(jax.random.fold_in(own, 1), rows)]
    offset_by = jax.random.randint(jax.random.fold_in(own, 2), (rows, 1), 0, top)
    return jnp.take_along_axis(table, (jnp.arange(top)[None, :] + offset_by) % top, axis=1)


def portions_of(number_of, total, limit, slope, full):
    weights = [(1 << 20) // math.isqrt(grade ** slope) + 1 for grade in range(1, number_of + 1)]
    largest = limit if full else min(limit, max(-(-total // number_of), total * weights[0] // sum(weights)))
    least = 1 if total - largest >= number_of - 1 else 0
    holding, rest = [largest] + [least] * (number_of - 1), total - largest - least * (number_of - 1)
    while rest > 0:
        free = [i for i in range(1, number_of) if holding[i] < largest] or [i for i in range(1, number_of) if holding[i] < limit]
        pool, remaining = sum([weights[i] for i in free]), rest
        for i in free:
            extra = min(limit - holding[i], max(1, remaining * weights[i] // pool), rest)
            holding[i] = holding[i] + extra
            rest = rest - extra
    return np.array(holding)


def gaussian(rng, extent, scale, most, cuts=(), held_as=jnp.bfloat16):
    drawn = scale * jax.random.normal(rng, extent, jnp.float32)
    if cuts:
        drawn = drawn * levels(rng, extent, cuts, -0.22, 0.18)
    return jnp.clip(drawn, -most, most).astype(held_as)


def setup_inputs(seed: int = 0) -> dict:
    key_of = jax.random.split(jax.random.key(seed), 10)
    fields = gaussian(key_of[0], (CELLS, 2 * BASIS), 1.0, 6.0, ((0, 8),), jnp.float32)
    far_geom = draw_far_geom(jax.random.fold_in(key_of[9], 71), 0)
    far_block_keys = jax.random.split(jax.random.fold_in(key_of[2], 1), POINTS // PTS_DEV)
    far_block_turns = jax.random.permutation(jax.random.fold_in(key_of[2], 3), POINTS // PTS_DEV)
    far_block = jax.vmap(lambda own, number: shared_out(jax.random.fold_in(key_of[2], 2), own, number, PTS_DEV, N_VOL, 1, CAP, 2))(far_block_keys, far_block_turns).reshape((POINTS, 1))
    far_cell = set_ends(jax.random.randint(key_of[3], (POINTS,), 0, CELLS_DEV), jax.random.fold_in(key_of[3], 1), 0, CELLS_DEV - 1).astype(jnp.int32)
    far_patch = draw_far_patch(jax.random.fold_in(key_of[9], 71), 0)
    near_geom = draw_near_geom(jax.random.fold_in(key_of[9], 71), 0)
    near_cell = set_ends(jax.random.randint(key_of[6], (NEAR,), 0, CELLS_DEV), jax.random.fold_in(key_of[6], 1), 0, CELLS_DEV - 1).astype(jnp.int32)
    near_patch = draw_near_patch(jax.random.fold_in(key_of[9], 71), 0)
    adjacency = draw_adjacency(jax.random.fold_in(key_of[9], 71), 0)
    return dict(fields=fields, far_geom=far_geom, far_block=far_block, far_cell=far_cell, far_patch=far_patch, near_geom=near_geom, near_cell=near_cell, near_patch=near_patch, adjacency=adjacency)


PENALTY = 4.0
SMOOTHING = 16.0
FLIPPED = np.array([1, 0, 3, 2], dtype=np.int32)

def bernstein(position):
    complement = 1.0 - position
    values = jnp.stack([complement * complement * complement, 3.0 * position * complement * complement, 3.0 * position * position * complement, position * position * position])
    slopes = jnp.stack([-3.0 * complement * complement, 3.0 * complement * complement - 6.0 * position * complement, 6.0 * position * complement - 3.0 * position * position, 3.0 * position * position])
    return (values, slopes)

def tensor_basis(factor_x, factor_y, factor_z):
    product = factor_x[:, None, None, :] * factor_y[None, :, None, :] * factor_z[None, None, :, :]
    return product.reshape(-1, factor_x.shape[-1])

def evaluate(columns, coords):
    value_x, slope_x = bernstein(coords[0])
    value_y, slope_y = bernstein(coords[1])
    value_z, slope_z = bernstein(coords[2])
    basis_set = [tensor_basis(value_x, value_y, value_z), tensor_basis(slope_x, value_y, value_z), tensor_basis(value_x, slope_y, value_z), tensor_basis(value_x, value_y, slope_z)]
    half_width = columns.shape[0] // 2
    state_part = columns[:half_width]
    adjoint_part = columns[half_width:]
    results = [jnp.sum(state_part * basis_kind, 0) for basis_kind in basis_set]
    results = results + [jnp.sum(adjoint_part * basis_kind, 0) for basis_kind in basis_set]
    return jnp.stack(results)

def density(values, normals):
    grad_state = values[1:4]
    grad_adjoint = values[5:8]
    normal_sq = jnp.sum(normals * normals, 0)
    inner_sum = jnp.sum(grad_state * grad_adjoint, 0)
    along_state = jnp.sum(grad_state * normals, 0)
    along_adjoint = jnp.sum(grad_adjoint * normals, 0)
    return normal_sq * inner_sum - 2.0 * along_state * along_adjoint + PENALTY * normal_sq * values[0] * values[4]

def spline_weights(param, span_count):
    scaled = param * span_count
    first_span = jnp.clip(jnp.floor(scaled), 0, span_count - 1)
    offset_in = scaled - first_span
    complement = 1.0 - offset_in
    cubed = offset_in * offset_in * offset_in
    squared = offset_in * offset_in
    weights = jnp.stack([complement * complement * complement / 6.0, (3.0 * cubed - 6.0 * squared + 4.0) / 6.0, (-3.0 * cubed + 3.0 * squared + 3.0 * offset_in + 1.0) / 6.0, cubed / 6.0])
    return (first_span.astype(jnp.int32), weights)

def spread(grid_flat, strength, spline_params, patch_ids, control):
    span_count = control - 3
    start_s, weights_s = spline_weights(spline_params[0], span_count)
    start_t, weights_t = spline_weights(spline_params[1], span_count)
    offsets = jnp.arange(4, dtype=jnp.int32)
    row_index = patch_ids[None, :] * control + start_s[None, :] + offsets[:, None]
    flat_index = (row_index[:, None, :] * control + start_t[None, None, :] + offsets[None, :, None]).reshape(-1)
    additions = (strength[None, None, :] * weights_s[:, None, :] * weights_t[None, :, :]).reshape(-1)
    return grid_flat.at[flat_index].add(additions)

def edge_table(iterate):
    return jnp.stack([iterate[:, 0, :], iterate[:, -1, :], iterate[:, :, 0], iterate[:, :, -1]], 1)

def lookup(edge_rows, neighbours):
    safe_ids = jnp.maximum(neighbours, 0)
    picked = edge_rows[safe_ids, FLIPPED[None, :]]
    return jnp.where((neighbours >= 0)[:, :, None], picked, jnp.zeros_like(picked))

def apply_operator(iterate, halo_rows):
    patch_count, edge_size = (iterate.shape[0], iterate.shape[1])
    padded = jnp.zeros((patch_count, edge_size + 2, edge_size + 2), iterate.dtype)
    padded = padded.at[:, 1:-1, 1:-1].set(iterate)
    padded = padded.at[:, 0, 1:-1].set(halo_rows[:, 0])
    padded = padded.at[:, -1, 1:-1].set(halo_rows[:, 1])
    padded = padded.at[:, 1:-1, 0].set(halo_rows[:, 2])
    padded = padded.at[:, 1:-1, -1].set(halo_rows[:, 3])
    beside = padded[:, :-2, 1:-1] + padded[:, 2:, 1:-1] + padded[:, 1:-1, :-2] + padded[:, 1:-1, 2:]
    return iterate + SMOOTHING * (4.0 * iterate - beside)

def precondition(residual):
    patch_count, edge_size = (residual.shape[0], residual.shape[1])
    below_diag = jnp.full((patch_count, edge_size), -SMOOTHING, residual.dtype).at[:, 0].set(0.0)
    main_diag = jnp.full((patch_count, edge_size), 1.0 + 2.0 * SMOOTHING, residual.dtype)
    above_diag = jnp.full((patch_count, edge_size), -SMOOTHING, residual.dtype).at[:, -1].set(0.0)
    along_rows = lax.linalg.tridiagonal_solve(below_diag, main_diag, above_diag, residual)
    along_cols = lax.linalg.tridiagonal_solve(below_diag, main_diag, above_diag, jnp.swapaxes(along_rows, 1, 2))
    return jnp.swapaxes(along_cols, 1, 2)

def smooth(summed, neighbours):
    iterate = precondition(summed)
    for sweep_index in range(SMOOTH_ITERS):
        halo_rows = lookup(edge_table(iterate), neighbours)
        iterate = iterate + precondition(summed - apply_operator(iterate, halo_rows))
    return iterate

def reference(fields, far_geom, far_block, far_cell, far_patch, near_geom, near_cell, near_patch, adjacency):
    columns_all = fields.T
    devices_count = POINTS // PTS_DEV
    grid_flat = jnp.zeros((PATCHES * CTRL * CTRL,), fields.dtype)
    far_cells = (far_block[:, 0] * CELLS_DEV + far_cell).astype(jnp.int32)
    owner_block = jnp.arange(devices_count, dtype=jnp.int32) // N_DSG * CELLS_DEV
    near_cells = (near_cell.reshape(devices_count, NEAR_DEV) + owner_block[:, None]).astype(jnp.int32)

    def point_step(carried, inputs):
        geom_part, cells_part, patch_part = inputs
        values = evaluate(jnp.take(columns_all, cells_part, axis=1), geom_part[0:3])
        strength = density(values, geom_part[3:6])
        return (spread(carried, strength, geom_part[6:8], patch_part, CTRL), strength)
    grid_flat, far_values = lax.scan(point_step, grid_flat, (far_geom.reshape(8, devices_count, PTS_DEV).transpose(1, 0, 2), far_cells.reshape(devices_count, PTS_DEV), far_patch.reshape(devices_count, PTS_DEV)))
    grid_flat, unused = lax.scan(point_step, grid_flat, (near_geom.reshape(8, devices_count, NEAR_DEV).transpose(1, 0, 2), near_cells, near_patch.reshape(devices_count, NEAR_DEV)))
    design = smooth(grid_flat.reshape(PATCHES, CTRL, CTRL), adjacency)
    return (far_values.reshape(-1), design)
```

```python
import functools

import jax
import jax.numpy as jnp
import numpy as np
from jax import lax
from jax.experimental import pallas as pl
from jax.experimental.pallas import tpu as pltpu
from jax.sharding import PartitionSpec as P

CTRL = 64
GROUP = 4
LANES = 128
PENALTY = 4.0
SMOOTHING = 16.0
NO_PATCH = 1.0e6
GRID_ROWS = GROUP // 2 * CTRL
PAYLOAD_ROWS = GRID_ROWS + GROUP * 8
F32 = jnp.float32
BF16 = jnp.bfloat16
EXACT = lax.Precision.HIGHEST
VMEM = pl.BlockSpec(memory_space=pltpu.VMEM)
SMEM = pl.BlockSpec(memory_space=pltpu.SMEM)
ANY = pl.BlockSpec(memory_space=pl.ANY)


def params(megabytes):
    return pltpu.CompilerParams(vmem_limit_bytes=megabytes << 20)


def constants():
    order = np.arange(1, CTRL + 1)
    basis = np.sqrt(2.0 / (CTRL + 1)) * np.sin(np.pi * np.outer(order, order) / (CTRL + 1))
    eigen = 1.0 + SMOOTHING * (2.0 - 2.0 * np.cos(np.pi * order / (CTRL + 1)))
    damp = 1.0 / eigen
    keep = 1.0 - damp
    powers = [keep**k * damp for k in range(3)]
    ends = [basis[:, 0], basis[:, CTRL - 1]]
    edge_rows = np.zeros((8, CTRL))
    scale_rows = np.zeros((8, CTRL))
    for k in range(3):
        for side in range(2):
            edge_rows[2 * k + side] = powers[k] * ends[side]
            scale_rows[2 * k + side] = powers[k]
    series = sum(np.outer(keep**k * damp, keep**k * damp) for k in range(4))

    def coupling(k):
        f = powers[k]
        lane = [0, 2, 1, 3]
        out = np.zeros((4 * CTRL, 4 * CTRL))
        for a, side_in in enumerate(lane):
            for b, side_out in enumerate(lane):
                q_in, q_out = ends[side_in % 2], ends[side_out % 2]
                if side_in // 2 == side_out // 2:
                    block = np.diag(f * np.sum(q_in * q_out * f))
                else:
                    block = np.outer(q_out * f, q_in * f)
                out[a * CTRL : (a + 1) * CTRL, b * CTRL : (b + 1) * CTRL] = SMOOTHING * block
        return out

    return dict(
        basis=np.float32(basis),
        basis_pair=np.float32(np.kron(np.eye(2), basis)),
        edge_rows=np.float32(edge_rows),
        scale_rows=np.float32(scale_rows),
        series=np.float32(series),
        coupling=np.float32(np.concatenate([coupling(0), coupling(1)], 1)),
    )


def split3(x):
    high = x.astype(BF16).astype(F32)
    rest = x - high
    mid = rest.astype(BF16).astype(F32)
    return high, mid, rest - mid


def nt(a, b, **kw):
    return lax.dot_general(a, b, (((1,), (1,)), ((), ())), preferred_element_type=F32, **kw)


def nn(a, b, **kw):
    return lax.dot_general(a, b, (((1,), (0,)), ((), ())), preferred_element_type=F32, **kw)


def tn(a, b, **kw):
    return lax.dot_general(a, b, (((0,), (0,)), ((), ())), preferred_element_type=F32, **kw)


def iota(shape, axis):
    return lax.broadcasted_iota(jnp.int32, shape, axis)


def pack_kernel(capacity, geom_ref, block_ref, cell_ref, request_ref, place_ref):
    owners = request_ref.shape[0]
    count = geom_ref.shape[1]
    block = block_ref[...]
    owner_id = iota((owners, count), 0)
    chosen = jnp.where(owner_id == block, 1.0, 0.0).astype(F32)
    earlier = jnp.where(iota((count, count), 0) < iota((count, count), 1), 1.0, 0.0).astype(BF16)
    rank = nn(chosen.astype(BF16), earlier)
    place = jnp.sum(chosen * (rank + (capacity * owner_id).astype(F32)), axis=0, keepdims=True)
    place = place.astype(jnp.int32)
    place_ref[...] = place
    row = iota((8, count), 0)
    values = jnp.where(row < 6, geom_ref[...], jnp.where(row == 6, cell_ref[...].astype(F32), 0.0))
    high, mid, low = split3(values)
    parts = jnp.concatenate([high, mid, low], 0).astype(BF16)
    put = jnp.where(iota((owners * capacity, count), 0) == place, 1.0, 0.0).astype(BF16)
    packed = nt(parts, put)
    packed = (packed[16:24] + packed[8:16]) + packed[0:8]
    for owner in range(owners):
        request_ref[owner] = packed[:, owner * capacity : (owner + 1) * capacity]


def pack_requests(far_geom, far_block, far_cell, owners, capacity):
    count = far_geom.shape[1]
    return pl.pallas_call(
        functools.partial(pack_kernel, capacity),
        out_shape=(
            jax.ShapeDtypeStruct((owners, 8, capacity), F32),
            jax.ShapeDtypeStruct((1, count), jnp.int32),
        ),
        in_specs=[VMEM] * 3,
        out_specs=(VMEM, VMEM),
        compiler_params=params(16),
        name="pack_requests",
    )(far_geom, far_block, far_cell)


def gather_rows(cells, fields_ref, rows_ref, count):
    unroll = 16

    def step(i, carry):
        for u in range(unroll):
            p = i * unroll + u
            rows_ref[pl.ds(p, 1), :] = fields_ref[pl.ds(cells(p), 1), :]
        return carry

    lax.fori_loop(0, count // unroll, step, 0)


def bernstein(t):
    u = 1.0 - t
    uu, tt = u * u, t * t
    values = [uu * u, 3.0 * t * uu, 3.0 * tt * u, tt * t]
    tu = 6.0 * t * u
    slopes = [-3.0 * uu, 3.0 * uu - tu, tu - 3.0 * tt, 3.0 * tt]
    return values, slopes


def tile_density(columns, geom):
    row = iota((8, LANES), 0)
    wide = [jnp.broadcast_to(geom[r : r + 1], (8, LANES)) for r in range(3)]
    x_val, x_der = bernstein(wide[0])
    y_val, y_der = bernstein(wide[1])
    z_val, z_der = bernstein(wide[2])
    k = row % 4

    def by_k(v):
        return jnp.where(k == 0, v[0], jnp.where(k == 1, v[1], jnp.where(k == 2, v[2], v[3])))

    def by_j(v, m):
        return jnp.where(row < 4, v[2 * m], v[2 * m + 1])

    z_v, z_d = by_k(z_val), by_k(z_der)
    yz = [by_j(y_val, m) * z_v for m in range(2)]
    dyz = [by_j(y_der, m) * z_v for m in range(2)]
    ydz = [by_j(y_val, m) * z_d for m in range(2)]
    sums = []
    for half in range(2):
        total = [None] * 4
        for i in range(4):
            at = half * 64 + i * 16
            first, second = columns[at : at + 8], columns[at + 8 : at + 16]
            plain = first * yz[0] + second * yz[1]
            along_y = first * dyz[0] + second * dyz[1]
            along_z = first * ydz[0] + second * ydz[1]
            terms = [x_val[i] * plain, x_der[i] * plain, x_val[i] * along_y, x_val[i] * along_z]
            total = [t if s is None else s + t for s, t in zip(total, terms)]
        sums.append([jnp.sum(t, axis=0, keepdims=True) for t in total])
    state, adjoint = sums
    n = [geom[3 + r : 4 + r] for r in range(3)]
    normal_sq = n[0] * n[0] + n[1] * n[1] + n[2] * n[2]
    inner = state[1] * adjoint[1] + state[2] * adjoint[2] + state[3] * adjoint[3]
    along_s = state[1] * n[0] + state[2] * n[1] + state[3] * n[2]
    along_a = adjoint[1] * n[0] + adjoint[2] * n[1] + adjoint[3] * n[2]
    return normal_sq * inner - 2.0 * along_s * along_a + PENALTY * normal_sq * state[0] * adjoint[0]


def densities(rows_ref, geom_ref, out_ref, count):
    def step(tile, carry):
        at = pl.multiple_of(tile * LANES, LANES)
        columns = rows_ref[pl.ds(at, LANES), :].T
        out_ref[:, pl.ds(at, LANES)] = tile_density(columns, geom_ref[:, pl.ds(at, LANES)])
        return carry

    lax.fori_loop(0, count // LANES, step, 0)


def near_kernel(cell_ref, fields_ref, geom_ref, out_ref, rows_ref):
    count = geom_ref.shape[1]
    gather_rows(lambda p: cell_ref[p], fields_ref, rows_ref, count)
    densities(rows_ref, geom_ref, out_ref, count)


def near_densities(near_cell, fields, near_geom):
    count = near_geom.shape[1]
    return pl.pallas_call(
        near_kernel,
        out_shape=jax.ShapeDtypeStruct((1, count), F32),
        in_specs=[SMEM, VMEM, VMEM],
        out_specs=VMEM,
        scratch_shapes=[pltpu.VMEM((count, LANES), F32)],
        compiler_params=params(24),
        cost_estimate=pl.CostEstimate(flops=40_000_000, bytes_accessed=4_000_000, transcendentals=0),
        name="near_densities",
    )(near_cell, fields, near_geom)


def far_kernel(request_ref, fields_ref, out_ref, query_ref, cell_v, cell_s, rows_ref, dens_ref, sem):
    owners, _, capacity = request_ref.shape
    count = owners * capacity
    for o in range(owners):
        query_ref[:, o * capacity : (o + 1) * capacity] = request_ref[o]
    cell_v[...] = query_ref[6:7, :].astype(jnp.int32)
    copy = pltpu.make_async_copy(cell_v, cell_s, sem)
    copy.start()
    copy.wait()
    gather_rows(lambda p: cell_s[0, p], fields_ref, rows_ref, count)
    densities(rows_ref, query_ref, dens_ref, count)
    for o in range(owners):
        out_ref[o] = dens_ref[:, o * capacity : (o + 1) * capacity]


def far_answers(requests, fields):
    owners, _, capacity = requests.shape
    count = owners * capacity
    return pl.pallas_call(
        far_kernel,
        out_shape=jax.ShapeDtypeStruct((owners, 1, capacity), F32),
        in_specs=[VMEM, VMEM],
        out_specs=VMEM,
        scratch_shapes=[
            pltpu.VMEM((8, count), F32),
            pltpu.VMEM((1, count), jnp.int32),
            pltpu.SMEM((1, count), jnp.int32),
            pltpu.VMEM((count, LANES), F32),
            pltpu.VMEM((1, count), F32),
            pltpu.SemaphoreType.DMA,
        ],
        compiler_params=params(24),
        name="far_answers",
    )(requests, fields)


def spline_columns(param):
    scaled = param * float(CTRL - 3)
    start = jnp.clip(jnp.floor(scaled), 0.0, float(CTRL - 4))
    x = scaled - start
    u = 1.0 - x
    cubed, squared = x * x * x, x * x
    weights = [
        u * u * u * (1.0 / 6.0),
        (3.0 * cubed - 6.0 * squared + 4.0) * (1.0 / 6.0),
        (-3.0 * cubed + 3.0 * squared + 3.0 * x + 1.0) * (1.0 / 6.0),
        cubed * (1.0 / 6.0),
    ]
    off = iota((CTRL, param.shape[1]), 0) - start.astype(jnp.int32)
    out = jnp.zeros(off.shape, F32)
    for m in range(4):
        out = jnp.where(off == m, weights[m], out)
    return out


def halves(x):
    high = x.astype(BF16)
    return high, (x - high.astype(F32)).astype(BF16)


def slot_grids(density, s, t, patch, slots):
    left_high, left_low = halves(spline_columns(s))
    right_high, right_low = halves(spline_columns(t) * density)
    masks = [jnp.where(patch == slot, 1.0, 0.0).astype(BF16) for slot in slots]
    high = jnp.concatenate([left_high * m for m in masks], 0)
    low = jnp.concatenate([left_low * m for m in masks], 0)
    return nt(high, right_high) + (nt(high, right_low) + nt(low, right_high))


def near_grid_kernel(dens_ref, geom_ref, near_ref, far_ref, grid_ref, slot_ref):
    near, far = near_ref[...].astype(F32), far_ref[...].astype(F32)
    slots = []
    last = jnp.full((1, 1), -1.0, F32)
    for _ in range(GROUP):
        a = jnp.min(jnp.where(near > last, near, NO_PATCH), axis=1, keepdims=True)
        b = jnp.min(jnp.where(far > last, far, NO_PATCH), axis=1, keepdims=True)
        last = jnp.minimum(a, b)
        slots.append(last)
    slot_ref[...] = jnp.concatenate([jnp.broadcast_to(s, (1, LANES)) for s in slots + slots], 0)
    grid_ref[...] = slot_grids(dens_ref[...], geom_ref[6:7, :], geom_ref[7:8, :], near, slots)


def near_grids(dens, near_geom, near_patch, far_patch):
    return pl.pallas_call(
        near_grid_kernel,
        out_shape=(
            jax.ShapeDtypeStruct((GROUP * CTRL, CTRL), F32),
            jax.ShapeDtypeStruct((8, LANES), F32),
        ),
        in_specs=[VMEM] * 4,
        out_specs=(VMEM, VMEM),
        compiler_params=params(24),
        cost_estimate=pl.CostEstimate(flops=80_000_000, bytes_accessed=1_000_000, transcendentals=0),
        name="near_grids",
    )(dens, near_geom, near_patch, far_patch)


def payload_kernel(
    reply_ref, place_ref, geom_ref, far_ref, slot_ref, near_ref,
    basis_ref, pair_ref, edge_ref, scale_ref,
    dens_ref, out_ref, flat_ref,
):
    owners, _, capacity = reply_ref.shape
    count = geom_ref.shape[1]
    for o in range(owners):
        flat_ref[:, o * capacity : (o + 1) * capacity] = reply_ref[o]
    high, mid, low = split3(flat_ref[...])
    parts = jnp.concatenate([high, mid, low, jnp.zeros((5, owners * capacity), F32)], 0).astype(BF16)
    put = jnp.where(iota((owners * capacity, count), 0) == place_ref[...], 1.0, 0.0).astype(BF16)
    got = nn(parts, put)
    dens = (got[2:3] + got[1:2]) + got[0:1]
    dens_ref[...] = dens
    slots = [slot_ref[s : s + 1, 0:1] for s in range(GROUP)]
    grids = near_ref[...] + slot_grids(
        dens, geom_ref[6:7, :], geom_ref[7:8, :], far_ref[...].astype(F32), slots
    )
    lane = iota((1, LANES), 1)
    names = jnp.zeros((1, LANES), F32)
    for s in range(GROUP):
        names = jnp.where(lane == s, slot_ref[s : s + 1, :], names)
    edge = edge_ref[...]
    scale = scale_ref[...]
    blank = jnp.zeros((8, CTRL), F32)
    both = jnp.concatenate(
        [jnp.concatenate([edge, blank], 1), jnp.concatenate([blank, edge], 1)], 0
    )
    row = iota((8, LANES), 0)
    for pair in range(GROUP // 2):
        a, b = 2 * pair, 2 * pair + 1
        both_grids = jnp.concatenate(
            [grids[a * CTRL : (a + 1) * CTRL], grids[b * CTRL : (b + 1) * CTRL]], 1
        )
        spectral = nn(nn(basis_ref[...], both_grids, precision=EXACT), pair_ref[...], precision=EXACT)
        out_ref[pair * CTRL : (pair + 1) * CTRL, :] = spectral
        along_rows = nn(edge, spectral, precision=EXACT)
        along_cols = nt(both, spectral, precision=EXACT)
        for side, slot in enumerate((a, b)):
            block = jnp.concatenate(
                [
                    along_rows[:, side * CTRL : (side + 1) * CTRL] * scale,
                    along_cols[8 * side : 8 * side + 8] * scale,
                ],
                1,
            )
            block = jnp.where(row == 6, slot_ref[slot : slot + 1, :], jnp.where(row == 7, names, block))
            out_ref[GRID_ROWS + slot * 8 : GRID_ROWS + slot * 8 + 8, :] = block


def make_payload(reply, place, far_geom, far_patch, slots, near_grid, const):
    owners, _, capacity = reply.shape
    count = far_geom.shape[1]
    return pl.pallas_call(
        payload_kernel,
        out_shape=(
            jax.ShapeDtypeStruct((1, count), F32),
            jax.ShapeDtypeStruct((PAYLOAD_ROWS, LANES), F32),
        ),
        in_specs=[VMEM] * 10,
        out_specs=(VMEM, VMEM),
        scratch_shapes=[pltpu.VMEM((1, owners * capacity), F32)],
        compiler_params=params(24),
        name="make_payload",
    )(
        reply, place, far_geom, far_patch, slots, near_grid,
        const["basis"], const["basis_pair"], const["edge_rows"], const["scale_rows"],
    )


def smooth_kernel(
    sources, per_owner, where_ref, adj_ref, coupling_ref, basis_ref, series_ref, edge_ref, scale_ref, *rest
):
    n_in = len(sources)
    payload = rest[:n_in]
    out_ref, buf, name_v, name_s, own, halo_rows, sem, name_sem = rest[n_in:]
    devices = buf.shape[0] // PAYLOAD_ROWS
    copies = []
    for a, (source, ref) in enumerate(zip(sources, payload)):
        rows = ref.shape[0]
        copies.append(
            pltpu.make_async_copy(
                ref, buf.at[pl.ds(pl.multiple_of(where_ref[1 + a] * PAYLOAD_ROWS, 8), rows)], sem.at[a]
            )
        )
        copies[-1].start()
    own[...] = jnp.zeros(own.shape, F32)
    for copy in copies:
        copy.wait()
    name_v[...] = buf[pl.ds(PAYLOAD_ROWS - 1, devices, stride=PAYLOAD_ROWS), :].astype(jnp.int32)
    names = pltpu.make_async_copy(name_v, name_s, name_sem)
    names.start()

    patches = adj_ref.shape[0]
    lane = iota((devices, LANES), 1)

    def edge_rows(r):
        return [
            buf[pl.ds(GRID_ROWS + 8 * s + r, devices, stride=PAYLOAD_ROWS), :] for s in range(GROUP)
        ]

    places = [jnp.where(lane == n.astype(jnp.int32), 1.0, 0.0) for n in edge_rows(6)]
    place = jnp.concatenate(places, 0).astype(BF16)
    sums = []
    for r in range(6):
        parts = [p.astype(BF16) for p in split3(jnp.concatenate(edge_rows(r), 0))]
        sums.append(tn(place, parts[0]) + (tn(place, parts[1]) + tn(place, parts[2])))
    base = [jnp.concatenate([sums[2 * k], sums[2 * k + 1]], 1)[:patches] for k in range(3)]

    adjacency = adj_ref[...]
    column = iota((patches, patches), 1)
    facing = [
        jnp.where(adjacency[:, s : s + 1] == column, 1.0, 0.0).astype(BF16) for s in range(4)
    ]
    low_lane = iota((patches, LANES), 1) < CTRL

    def halo(edges):
        parts = [p.astype(BF16) for p in split3(edges)]

        def look(side, at):
            pieces = [nn(facing[side], p[:, at : at + LANES]) for p in parts]
            return pieces[0] + (pieces[1] + pieces[2])

        first = jnp.where(low_lane, look(0, LANES), look(2, LANES))
        second = jnp.where(low_lane, look(1, 0), look(3, 0))
        return jnp.concatenate([first, second], 1)

    wide = 4 * CTRL
    halo0 = halo(base[0])
    effect0 = nn(halo0, coupling_ref[...], precision=EXACT)
    edges1 = base[0] + base[1] + effect0[:, :wide]
    halo1 = halo(edges1)
    effect1 = nn(halo1, coupling_ref[:, :wide], precision=EXACT)
    edges2 = base[0] + base[1] + base[2] + effect0[:, wide:] + effect1
    halo2 = halo(edges2)

    first_own = where_ref[0] * per_owner
    mine = jnp.where(
        iota((per_owner, patches), 1) == iota((per_owner, patches), 0) + first_own, 1.0, 0.0
    ).astype(BF16)
    scale = scale_ref[...]
    for k, h in enumerate((halo2, halo1, halo0)):
        picked = [nn(mine, p.astype(BF16)) for p in split3(h)]
        picked = picked[0] + (picked[1] + picked[2])
        factor = SMOOTHING * jnp.concatenate([scale[2 * k : 2 * k + 1]] * 2, 1)
        for side in range(2):
            halo_rows[pl.ds(2 * k + side, per_owner, stride=8), :] = (
                picked[:, side * LANES : (side + 1) * LANES] * factor
            )
    zero = jnp.zeros((per_owner, LANES), F32)
    for r in (6, 7):
        halo_rows[pl.ds(r, per_owner, stride=8), :] = zero

    names.wait()

    def add_slot(device, carry):
        for s in range(GROUP):
            patch = name_s[device, s] - first_own

            @pl.when((patch >= 0) & (patch < per_owner))
            def _():
                at = pl.multiple_of(device * PAYLOAD_ROWS + (s // 2) * CTRL, 8)
                block = buf[pl.ds(at, CTRL), :]
                if s % 2:
                    block = pltpu.roll(block, CTRL, 1)
                own_at = pl.multiple_of(patch * CTRL, CTRL)
                own[pl.ds(own_at, CTRL), :] = own[pl.ds(own_at, CTRL), :] + block

        return carry

    lax.fori_loop(0, devices, add_slot, 0)

    basis = basis_ref[...]
    series = series_ref[...]
    edge = edge_ref[...]

    def finish(patch, carry):
        at = pl.multiple_of(patch * CTRL, CTRL)
        rows = halo_rows[pl.ds(pl.multiple_of(patch * 8, 8), 8), :]
        left = jnp.concatenate([edge, rows[:, CTRL:]], 0)
        right = jnp.concatenate([rows[:, :CTRL], edge], 0)
        spectral = own[pl.ds(at, CTRL), :][:, :CTRL] * series + tn(left, right, precision=EXACT)
        out_ref[patch] = nn(nn(basis, spectral, precision=EXACT), basis, precision=EXACT)
        return carry

    lax.fori_loop(0, per_owner, finish, 0, unroll=4)


def smooth(payloads, sources, where, adjacency, owners, devices, const):
    per_owner = adjacency.shape[0] // owners
    return pl.pallas_call(
        functools.partial(smooth_kernel, sources, per_owner),
        out_shape=jax.ShapeDtypeStruct((per_owner, CTRL, CTRL), F32),
        in_specs=[SMEM] + [VMEM] * 6 + [ANY] * len(payloads),
        out_specs=VMEM,
        scratch_shapes=[
            pltpu.VMEM((devices * PAYLOAD_ROWS, LANES), F32),
            pltpu.VMEM((devices, LANES), jnp.int32),
            pltpu.SMEM((devices, LANES), jnp.int32),
            pltpu.VMEM((per_owner * CTRL, LANES), F32),
            pltpu.VMEM((per_owner * 8, LANES), F32),
            pltpu.SemaphoreType.DMA((len(payloads),)),
            pltpu.SemaphoreType.DMA,
        ],
        compiler_params=params(48),
        name="smooth",
    )(
        where, adjacency, const["coupling"], const["basis"], const["series"], const["edge_rows"],
        const["scale_rows"], *payloads,
    )


def spread_payload(payload, vol_count, dsg_count):
    if vol_count > 8 or dsg_count != 4:
        whole = lax.all_gather(payload, ("vol", "dsg"), axis=0, tiled=True)
        return [None], [whole]
    sources, arrays = [(0, 0)], [payload]
    for k in range(1, vol_count):
        sources.append((k, 0))
        arrays.append(lax.ppermute(payload, "vol", [(i, i ^ k) for i in range(vol_count)]))
    for offset in (2, 1):
        pairs = [(i, i ^ offset) for i in range(dsg_count)]
        for (a, b), array in list(zip(sources, arrays)):
            sources.append((a, b ^ offset))
            arrays.append(lax.ppermute(array, "dsg", pairs))
    return sources, arrays


def per_device(
    fields, far_geom, far_block, far_cell, far_patch, near_geom, near_cell, near_patch, adjacency
):
    vol_count, dsg_count = lax.axis_size("vol"), lax.axis_size("dsg")
    vol_at, dsg_at = lax.axis_index("vol"), lax.axis_index("dsg")
    far_count = far_cell.shape[0]
    capacity = 5 * far_count // (2 * vol_count)
    const = {name: jnp.asarray(value) for name, value in constants().items()}

    request, place = pack_requests(
        far_geom, far_block.reshape(1, -1), far_cell.reshape(1, -1), vol_count, capacity
    )
    asked = lax.all_to_all(request, "vol", split_axis=0, concat_axis=0, tiled=True)
    near_dens = near_densities(near_cell, fields, near_geom)
    answer = far_answers(asked, fields)
    reply = lax.all_to_all(answer, "vol", split_axis=0, concat_axis=0, tiled=True)
    near_patch, far_patch = near_patch.reshape(1, -1), far_patch.reshape(1, -1)
    near_grid, slots = near_grids(near_dens, near_geom, near_patch, far_patch)
    far_dens, payload = make_payload(reply, place, far_geom, far_patch, slots, near_grid, const)

    sources, arrays = spread_payload(payload, vol_count, dsg_count)
    where = [dsg_at]
    for source in sources:
        if source is None:
            where.append(jnp.int32(0))
        else:
            where.append((vol_at ^ source[0]) * dsg_count + (dsg_at ^ source[1]))
    where = jnp.stack([w.astype(jnp.int32) for w in where])
    design = smooth(arrays, sources, where, adjacency, dsg_count, vol_count * dsg_count, const)
    return far_dens.reshape(-1), design


def solution(mesh):
    return jax.shard_map(
        per_device,
        mesh=mesh,
        in_specs=(
            P("vol", None),
            P(None, ("vol", "dsg")),
            P(("vol", "dsg"), None),
            P(("vol", "dsg")),
            P(("vol", "dsg")),
            P(None, ("vol", "dsg")),
            P(("vol", "dsg")),
            P(("vol", "dsg")),
            P(),
        ),
        out_specs=(P(("vol", "dsg")), P("dsg", None, None)),
        check_vma=False,
    )
```

```python
import functools

import jax
import jax.numpy as jnp
import numpy as np
from jax import lax
from jax.experimental import pallas as pl
from jax.experimental.pallas import tpu as pltpu
from jax.sharding import PartitionSpec as P

CTRL = 64
GROUP = 4
LANES = 128
PENALTY = 4.0
SMOOTHING = 16.0
NO_PATCH = 1.0e6
GRID_ROWS = GROUP // 2 * CTRL
PAYLOAD_ROWS = GRID_ROWS + GROUP * 8
F32 = jnp.float32
BF16 = jnp.bfloat16
EXACT = lax.Precision.HIGHEST
VMEM = pl.BlockSpec(memory_space=pltpu.VMEM)
SMEM = pl.BlockSpec(memory_space=pltpu.SMEM)
ANY = pl.BlockSpec(memory_space=pl.ANY)
WHOLE = pl.BlockSpec()


def params(megabytes):
    return pltpu.CompilerParams(vmem_limit_bytes=megabytes << 20)


def constants():
    order = np.arange(1, CTRL + 1)
    basis = np.sqrt(2.0 / (CTRL + 1)) * np.sin(np.pi * np.outer(order, order) / (CTRL + 1))
    eigen = 1.0 + SMOOTHING * (2.0 - 2.0 * np.cos(np.pi * order / (CTRL + 1)))
    damp = 1.0 / eigen
    keep = 1.0 - damp
    powers = [keep**k * damp for k in range(3)]
    ends = [basis[:, 0], basis[:, CTRL - 1]]
    edge_rows = np.zeros((8, CTRL))
    scale_rows = np.zeros((8, CTRL))
    for k in range(3):
        for side in range(2):
            edge_rows[2 * k + side] = powers[k] * ends[side]
            scale_rows[2 * k + side] = powers[k]
    series = sum(np.outer(keep**k * damp, keep**k * damp) for k in range(4))

    def coupling(k):
        f = powers[k]
        lane = [0, 2, 1, 3]
        out = np.zeros((4 * CTRL, 4 * CTRL))
        for a, side_in in enumerate(lane):
            for b, side_out in enumerate(lane):
                q_in, q_out = ends[side_in % 2], ends[side_out % 2]
                if side_in // 2 == side_out // 2:
                    block = np.diag(f * np.sum(q_in * q_out * f))
                else:
                    block = np.outer(q_out * f, q_in * f)
                out[a * CTRL : (a + 1) * CTRL, b * CTRL : (b + 1) * CTRL] = SMOOTHING * block
        return out

    return dict(
        basis=np.float32(basis),
        basis_pair=np.float32(np.kron(np.eye(2), basis)),
        edge_rows=np.float32(edge_rows),
        scale_rows=np.float32(scale_rows),
        series=np.float32(np.concatenate([series, series], 1)),
        coupling=np.float32(np.concatenate([coupling(0), coupling(1)], 1)),
    )


def split3(x):
    high = x.astype(BF16).astype(F32)
    rest = x - high
    mid = rest.astype(BF16).astype(F32)
    return high, mid, rest - mid


def nt(a, b, **kw):
    return lax.dot_general(a, b, (((1,), (1,)), ((), ())), preferred_element_type=F32, **kw)


def nn(a, b, **kw):
    return lax.dot_general(a, b, (((1,), (0,)), ((), ())), preferred_element_type=F32, **kw)


def tn(a, b, **kw):
    return lax.dot_general(a, b, (((0,), (0,)), ((), ())), preferred_element_type=F32, **kw)


def iota(shape, axis):
    return lax.broadcasted_iota(jnp.int32, shape, axis)


def pack_kernel(capacity, geom_ref, block_ref, cell_ref, request_ref, place_ref):
    owners = request_ref.shape[0]
    count = geom_ref.shape[1]
    block = block_ref[...]
    owner_id = iota((owners, count), 0)
    chosen = jnp.where(owner_id == block, 1.0, 0.0).astype(F32)
    earlier = jnp.where(iota((count, count), 0) < iota((count, count), 1), 1.0, 0.0).astype(BF16)
    rank = nn(chosen.astype(BF16), earlier)
    place = jnp.sum(chosen * (rank + (capacity * owner_id).astype(F32)), axis=0, keepdims=True)
    place = place.astype(jnp.int32)
    place_ref[...] = place
    row = iota((8, count), 0)
    values = jnp.where(row < 6, geom_ref[...], jnp.where(row == 6, cell_ref[...].astype(F32), 0.0))
    high, mid, low = split3(values)
    parts = jnp.concatenate([high, mid, low], 0).astype(BF16)
    put = jnp.where(iota((owners * capacity, count), 0) == place, 1.0, 0.0).astype(BF16)
    packed = nt(parts, put)
    packed = (packed[16:24] + packed[8:16]) + packed[0:8]
    for owner in range(owners):
        request_ref[owner] = packed[:, owner * capacity : (owner + 1) * capacity]


def pack_requests(far_geom, far_block, far_cell, owners, capacity):
    count = far_geom.shape[1]
    return pl.pallas_call(
        functools.partial(pack_kernel, capacity),
        out_shape=(
            jax.ShapeDtypeStruct((owners, 8, capacity), F32),
            jax.ShapeDtypeStruct((1, count), jnp.int32),
        ),
        in_specs=[WHOLE] * 3,
        out_specs=(VMEM, VMEM),
        compiler_params=params(16),
        name="pack_requests",
    )(far_geom, far_block, far_cell)


def gather_rows(cells, fields_ref, rows_ref, count):
    unroll = 16

    def step(i, carry):
        for u in range(unroll):
            p = i * unroll + u
            rows_ref[pl.ds(p, 1), :] = fields_ref[pl.ds(cells(p), 1), :]
        return carry

    lax.fori_loop(0, count // unroll, step, 0)


def bernstein(t):
    u = 1.0 - t
    uu, tt = u * u, t * t
    values = [uu * u, 3.0 * t * uu, 3.0 * tt * u, tt * t]
    tu = 6.0 * t * u
    slopes = [-3.0 * uu, 3.0 * uu - tu, tu - 3.0 * tt, 3.0 * tt]
    return values, slopes


def tile_density(columns, geom):
    row = iota((8, LANES), 0)
    wide = [jnp.broadcast_to(geom[r : r + 1], (8, LANES)) for r in range(3)]
    x_val, x_der = bernstein(wide[0])
    y_val, y_der = bernstein(wide[1])
    z_val, z_der = bernstein(wide[2])
    k = row % 4

    def by_k(v):
        return jnp.where(k == 0, v[0], jnp.where(k == 1, v[1], jnp.where(k == 2, v[2], v[3])))

    def by_j(v, m):
        return jnp.where(row < 4, v[2 * m], v[2 * m + 1])

    z_v, z_d = by_k(z_val), by_k(z_der)
    yz = [by_j(y_val, m) * z_v for m in range(2)]
    dyz = [by_j(y_der, m) * z_v for m in range(2)]
    ydz = [by_j(y_val, m) * z_d for m in range(2)]
    sums = []
    for half in range(2):
        total = [None] * 4
        for i in range(4):
            at = half * 64 + i * 16
            first, second = columns[at : at + 8], columns[at + 8 : at + 16]
            plain = first * yz[0] + second * yz[1]
            along_y = first * dyz[0] + second * dyz[1]
            along_z = first * ydz[0] + second * ydz[1]
            terms = [x_val[i] * plain, x_der[i] * plain, x_val[i] * along_y, x_val[i] * along_z]
            total = [t if s is None else s + t for s, t in zip(total, terms)]
        sums.append([jnp.sum(t, axis=0, keepdims=True) for t in total])
    state, adjoint = sums
    n = [geom[3 + r : 4 + r] for r in range(3)]
    normal_sq = n[0] * n[0] + n[1] * n[1] + n[2] * n[2]
    inner = state[1] * adjoint[1] + state[2] * adjoint[2] + state[3] * adjoint[3]
    along_s = state[1] * n[0] + state[2] * n[1] + state[3] * n[2]
    along_a = adjoint[1] * n[0] + adjoint[2] * n[1] + adjoint[3] * n[2]
    return normal_sq * inner - 2.0 * along_s * along_a + PENALTY * normal_sq * state[0] * adjoint[0]


def densities(rows_ref, geom_ref, out_ref, count):
    def step(tile, carry):
        at = pl.multiple_of(tile * LANES, LANES)
        columns = rows_ref[pl.ds(at, LANES), :].T
        out_ref[:, pl.ds(at, LANES)] = tile_density(columns, geom_ref[:, pl.ds(at, LANES)])
        return carry

    lax.fori_loop(0, count // LANES, step, 0)


def near_kernel(cell_ref, fields_ref, geom_ref, out_ref, rows_ref):
    count = geom_ref.shape[1]
    gather_rows(lambda p: cell_ref[p], fields_ref, rows_ref, count)
    densities(rows_ref, geom_ref, out_ref, count)


def near_densities(near_cell, fields, near_geom):
    count = near_geom.shape[1]
    return pl.pallas_call(
        near_kernel,
        out_shape=jax.ShapeDtypeStruct((1, count), F32),
        in_specs=[SMEM, VMEM, WHOLE],
        out_specs=VMEM,
        scratch_shapes=[pltpu.VMEM((count, LANES), F32)],
        compiler_params=params(24),
        cost_estimate=pl.CostEstimate(flops=40_000_000, bytes_accessed=4_000_000, transcendentals=0),
        name="near_densities",
    )(near_cell, fields, near_geom)


def far_kernel(request_ref, fields_ref, near_ref, out_ref, query_ref, cell_v, cell_s, rows_ref, dens_ref, sem):
    owners, _, capacity = request_ref.shape
    count = owners * capacity
    for o in range(owners):
        query_ref[:, o * capacity : (o + 1) * capacity] = request_ref[o]
    cell_v[...] = query_ref[6:7, :].astype(jnp.int32)
    copy = pltpu.make_async_copy(cell_v, cell_s, sem)
    copy.start()
    copy.wait()
    gather_rows(lambda p: cell_s[0, p], fields_ref, rows_ref, count)
    densities(rows_ref, query_ref, dens_ref, count)
    for o in range(owners):
        out_ref[o] = dens_ref[:, o * capacity : (o + 1) * capacity]


def far_answers(requests, fields, near_dens):
    owners, _, capacity = requests.shape
    count = owners * capacity
    return pl.pallas_call(
        far_kernel,
        out_shape=jax.ShapeDtypeStruct((owners, 1, capacity), F32),
        in_specs=[VMEM, VMEM, ANY],
        out_specs=VMEM,
        scratch_shapes=[
            pltpu.VMEM((8, count), F32),
            pltpu.VMEM((1, count), jnp.int32),
            pltpu.SMEM((1, count), jnp.int32),
            pltpu.VMEM((count, LANES), F32),
            pltpu.VMEM((1, count), F32),
            pltpu.SemaphoreType.DMA,
        ],
        compiler_params=params(24),
        name="far_answers",
    )(requests, fields, near_dens)


def spline_columns(param):
    scaled = param * float(CTRL - 3)
    start = jnp.clip(jnp.floor(scaled), 0.0, float(CTRL - 4))
    x = scaled - start
    u = 1.0 - x
    cubed, squared = x * x * x, x * x
    weights = [
        u * u * u * (1.0 / 6.0),
        (3.0 * cubed - 6.0 * squared + 4.0) * (1.0 / 6.0),
        (-3.0 * cubed + 3.0 * squared + 3.0 * x + 1.0) * (1.0 / 6.0),
        cubed * (1.0 / 6.0),
    ]
    off = iota((CTRL, param.shape[1]), 0) - start.astype(jnp.int32)
    out = jnp.zeros(off.shape, F32)
    for m in range(4):
        out = jnp.where(off == m, weights[m], out)
    return out


def halves(x):
    high = x.astype(BF16)
    return high, (x - high.astype(F32)).astype(BF16)


def slot_grids(density, s, t, patch, slots):
    left_high, left_low = halves(spline_columns(s))
    right_high, right_low = halves(spline_columns(t) * density)
    masks = [jnp.where(patch == slot, 1.0, 0.0).astype(BF16) for slot in slots]
    high = jnp.concatenate([left_high * m for m in masks], 0)
    low = jnp.concatenate([left_low * m for m in masks], 0)
    return nt(high, right_high) + (nt(high, right_low) + nt(low, right_high))


def near_grid_kernel(dens_ref, geom_ref, near_ref, far_ref, grid_ref, slot_ref):
    near, far = near_ref[...].astype(F32), far_ref[...].astype(F32)
    slots = []
    last = jnp.full((1, 1), -1.0, F32)
    for _ in range(GROUP):
        a = jnp.min(jnp.where(near > last, near, NO_PATCH), axis=1, keepdims=True)
        b = jnp.min(jnp.where(far > last, far, NO_PATCH), axis=1, keepdims=True)
        last = jnp.minimum(a, b)
        slots.append(last)
    slot_ref[...] = jnp.concatenate([jnp.broadcast_to(s, (1, LANES)) for s in slots + slots], 0)
    grid_ref[...] = slot_grids(dens_ref[...], geom_ref[6:7, :], geom_ref[7:8, :], near, slots)


def near_grids(dens, near_geom, near_patch, far_patch):
    return pl.pallas_call(
        near_grid_kernel,
        out_shape=(
            jax.ShapeDtypeStruct((GROUP * CTRL, CTRL), F32),
            jax.ShapeDtypeStruct((8, LANES), F32),
        ),
        in_specs=[VMEM] + [WHOLE] * 3,
        out_specs=(VMEM, VMEM),
        compiler_params=params(24),
        cost_estimate=pl.CostEstimate(flops=80_000_000, bytes_accessed=1_000_000, transcendentals=0),
        name="near_grids",
    )(dens, near_geom, near_patch, far_patch)


def payload_kernel(
    reply_ref, place_ref, geom_ref, far_ref, slot_ref, near_ref,
    basis_ref, pair_ref, edge_ref, scale_ref,
    dens_ref, out_ref, flat_ref,
):
    owners, _, capacity = reply_ref.shape
    count = geom_ref.shape[1]
    for o in range(owners):
        flat_ref[:, o * capacity : (o + 1) * capacity] = reply_ref[o]
    high, mid, low = split3(flat_ref[...])
    parts = jnp.concatenate([high, mid, low, jnp.zeros((5, owners * capacity), F32)], 0).astype(BF16)
    put = jnp.where(iota((owners * capacity, count), 0) == place_ref[...], 1.0, 0.0).astype(BF16)
    got = nn(parts, put)
    dens = (got[2:3] + got[1:2]) + got[0:1]
    dens_ref[...] = dens
    slots = [slot_ref[s : s + 1, 0:1] for s in range(GROUP)]
    grids = near_ref[...] + slot_grids(
        dens, geom_ref[6:7, :], geom_ref[7:8, :], far_ref[...].astype(F32), slots
    )
    lane = iota((1, LANES), 1)
    names = jnp.zeros((1, LANES), F32)
    for s in range(GROUP):
        names = jnp.where(lane == s, slot_ref[s : s + 1, :], names)
    edge = edge_ref[...]
    scale = scale_ref[...]
    blank = jnp.zeros((8, CTRL), F32)
    both = jnp.concatenate(
        [jnp.concatenate([edge, blank], 1), jnp.concatenate([blank, edge], 1)], 0
    )
    out_ref[GRID_ROWS + 6 * GROUP : GRID_ROWS + 7 * GROUP, :] = slot_ref[0:GROUP, :]
    out_ref[GRID_ROWS + 7 * GROUP : GRID_ROWS + 8 * GROUP, :] = jnp.broadcast_to(names, (GROUP, LANES))
    for pair in range(GROUP // 2):
        a, b = 2 * pair, 2 * pair + 1
        both_grids = jnp.concatenate(
            [grids[a * CTRL : (a + 1) * CTRL], grids[b * CTRL : (b + 1) * CTRL]], 1
        )
        spectral = nn(nn(basis_ref[...], both_grids, precision=EXACT), pair_ref[...], precision=EXACT)
        out_ref[pair * CTRL : (pair + 1) * CTRL, :] = spectral
        along_rows = nn(edge, spectral, precision=EXACT)
        along_cols = nt(both, spectral, precision=EXACT)
        for side, slot in enumerate((a, b)):
            block = jnp.concatenate(
                [
                    along_rows[:, side * CTRL : (side + 1) * CTRL] * scale,
                    along_cols[8 * side : 8 * side + 8] * scale,
                ],
                1,
            )
            for r in range(6):
                at = GRID_ROWS + GROUP * r + slot
                out_ref[at : at + 1, :] = block[r : r + 1]


def make_payload(reply, place, far_geom, far_patch, slots, near_grid, const):
    owners, _, capacity = reply.shape
    count = far_geom.shape[1]
    return pl.pallas_call(
        payload_kernel,
        out_shape=(
            jax.ShapeDtypeStruct((1, count), F32),
            jax.ShapeDtypeStruct((PAYLOAD_ROWS, LANES), F32),
        ),
        in_specs=[VMEM] * 2 + [WHOLE] * 2 + [VMEM] * 2 + [WHOLE] * 4,
        out_specs=(VMEM, VMEM),
        scratch_shapes=[pltpu.VMEM((1, owners * capacity), F32)],
        compiler_params=params(24),
        name="make_payload",
    )(
        reply, place, far_geom, far_patch, slots, near_grid,
        const["basis"], const["basis_pair"], const["edge_rows"], const["scale_rows"],
    )


def two(x):
    return jnp.concatenate(halves(x), 1)


def fold(x):
    half = x.shape[1] // 2
    return x[:, :half] + x[:, half:]


def absorb(first_own, y_at, per_owner, items, sums, groups, name_v, name_s, edges, name_sem):
    patches = groups.shape[2]
    total = sum(parts for _, parts, _, _ in items)
    at = 0
    for ref, parts, _, _ in items:
        for p in range(parts):
            last = (p + 1) * PAYLOAD_ROWS - 1
            name_v[at : at + 1, :] = ref[last : last + 1, :].astype(jnp.int32)
            at += 1
    names = pltpu.make_async_copy(name_v, name_s, name_sem)
    names.start()

    for group in sorted({2 * dy + dx for _, _, dy, dx in items}):
        at = 0
        for ref, parts, dy, dx in items:
            if 2 * dy + dx == group:
                for p in range(parts):
                    for r in range(7):
                        row = p * PAYLOAD_ROWS + GRID_ROWS + GROUP * r
                        edges[r, at : at + GROUP, :] = ref[row : row + GROUP, :]
                    at += GROUP
        lane = iota((at, LANES), 1)
        place = jnp.where(lane == edges[6, :at, :].astype(jnp.int32), 1.0, 0.0).T[:patches].astype(BF16)
        for k in range(3):
            rows = jnp.concatenate([edges[2 * k, :at, :], edges[2 * k + 1, :at, :]], 1)
            groups[(group // 2 ^ y_at) * 2 + group % 2, k] = fold(nn(place, two(rows)))

    names.wait()
    low_half = iota((CTRL, LANES), 1) < CTRL
    at = 0
    for ref, parts, dy, _ in items:

        def add_payload(p, carry, ref=ref, at=at, dy=dy):
            for s in range(GROUP):
                patch = name_s[at + p, s] - first_own

                @pl.when((patch >= 0) & (patch < per_owner))
                def _():
                    row = pl.multiple_of(p * PAYLOAD_ROWS + (s // 2) * CTRL, 8)
                    block = ref[pl.ds(row, CTRL), :]
                    block = jnp.where(patch % 2 == s % 2, block, pltpu.roll(block, CTRL, 1))
                    block = jnp.where(low_half == (patch % 2 == 0), block, 0.0)
                    own = pl.multiple_of(patch // 2 * CTRL, CTRL)
                    sums[dy ^ y_at, pl.ds(own, CTRL), :] = sums[dy ^ y_at, pl.ds(own, CTRL), :] + block

            return carry

        lax.fori_loop(0, parts, add_payload, 0)
        at += parts


def early_kernel(per_owner, items, where_ref, *rest):
    refs = rest[: len(items)]
    sums, groups, name_v, name_s, edges, name_sem = rest[len(items) :]
    sums[...] = jnp.zeros(sums.shape, F32)
    groups[...] = jnp.zeros(groups.shape, F32)
    items = [(ref, *item) for ref, item in zip(refs, items)]
    absorb(where_ref[0] * per_owner, where_ref[1], per_owner, items, sums, groups, name_v, name_s, edges, name_sem)


def absorb_scratch(items):
    total = sum(item[0] for item in items)
    return [
        pltpu.VMEM((total, LANES), jnp.int32),
        pltpu.SMEM((total, LANES), jnp.int32),
        pltpu.VMEM((7, total * GROUP, LANES), F32),
        pltpu.SemaphoreType.DMA,
    ]


def sum_shapes(per_owner, patches):
    return (
        jax.ShapeDtypeStruct((2, per_owner // 2 * CTRL, LANES), F32),
        jax.ShapeDtypeStruct((4, 3, patches, 4 * CTRL), F32),
    )


def early_sums(payloads, items, where, per_owner, patches):
    return pl.pallas_call(
        functools.partial(early_kernel, per_owner, items),
        out_shape=sum_shapes(per_owner, patches),
        in_specs=[SMEM] + [VMEM] * len(payloads),
        out_specs=(VMEM, VMEM),
        scratch_shapes=absorb_scratch(items),
        compiler_params=params(16),
        cost_estimate=pl.CostEstimate(flops=20_000_000, bytes_accessed=3_000_000, transcendentals=0),
        name="early_sums",
    )(where, *payloads)


def smooth_kernel(
    items, per_owner, has_early, where_ref, adj_ref, coupling_ref, basis_ref, pair_ref, series_ref, edge_ref,
    scale_ref, *rest
):
    refs, rest = rest[: len(items)], rest[len(items) :]
    if has_early:
        early_sum, early_group, *rest = rest
    out_ref, sums, groups, name_v, name_s, edges, name_sem, halo_all, halo_rows = rest
    if has_early:
        sums[...] = early_sum[...]
        groups[...] = early_group[...]
    else:
        sums[...] = jnp.zeros(sums.shape, F32)
        groups[...] = jnp.zeros(groups.shape, F32)
    patches = adj_ref.shape[0]
    first_own = pl.multiple_of(where_ref[0] * per_owner, 8)
    items = [(ref, *item) for ref, item in zip(refs, items)]
    absorb(first_own, where_ref[1], per_owner, items, sums, groups, name_v, name_s, edges, name_sem)
    base = [(groups[0, k] + groups[1, k]) + (groups[2, k] + groups[3, k]) for k in range(3)]

    column = iota((patches, patches), 1)
    wide = 4 * CTRL

    def facing(adjacency):
        hits = [
            jnp.where(adjacency[:, s : s + 1] == column[: adjacency.shape[0]], 1.0, 0.0).astype(BF16)
            for s in range(4)
        ]
        return jnp.concatenate([hits[0], hits[2]], 0), jnp.concatenate([hits[1], hits[3]], 0)

    def halo(facing, edges):
        count = facing[0].shape[0] // 2
        low_lane = iota((count, LANES), 1) < CTRL
        first = fold(nn(facing[0], two(edges[:, LANES:])))
        second = fold(nn(facing[1], two(edges[:, :LANES])))
        return jnp.concatenate(
            [jnp.where(low_lane, x[:count], x[count:]) for x in (first, second)], 1
        )

    def product(x, y):
        x_high, x_low = halves(x)
        y_high, y_low = halves(y)
        return nn(x_high, y_high) + (nn(x_low, y_high) + nn(x_high, y_low))

    every = facing(adj_ref[...])
    halo0 = halo(every, base[0])
    effect0 = product(halo0, coupling_ref[...])
    edges1 = base[0] + base[1] + effect0[:, :wide]
    halo1 = halo(every, edges1)
    effect1 = product(halo1, coupling_ref[:, :wide])
    edges2 = base[0] + base[1] + base[2] + effect0[:, wide:] + effect1
    halo2 = halo(facing(adj_ref[pl.ds(first_own, per_owner), :]), edges2)
    halo_all[0] = halo1
    halo_all[1] = halo0
    scale = scale_ref[...]
    for k in range(3):
        mine = halo2 if k == 0 else halo_all[k - 1, pl.ds(first_own, per_owner), :]
        factor = SMOOTHING * jnp.concatenate([scale[2 * k : 2 * k + 1]] * 2, 1)
        for side in range(2):
            halo_rows[pl.ds(2 * k + side, per_owner, stride=8), :] = (
                mine[:, side * LANES : (side + 1) * LANES] * factor
            )
    zero = jnp.zeros((per_owner, LANES), F32)
    for r in (6, 7):
        halo_rows[pl.ds(r, per_owner, stride=8), :] = zero

    pairs = per_owner // 2
    edge = edge_ref[...]
    blank = jnp.zeros((8, CTRL), F32)
    both = jnp.concatenate(
        [jnp.concatenate([edge, blank], 1), jnp.concatenate([blank, edge], 1)], 0
    )
    low8 = iota((8, LANES), 1) < CTRL
    along_rows, along_cols = [], []
    for pair in range(pairs):
        a = halo_rows[16 * pair : 16 * pair + 8, :]
        b = halo_rows[16 * pair + 8 : 16 * pair + 16, :]
        along_rows.append(jnp.where(low8, a, pltpu.roll(b, CTRL, 1)))
        along_cols.append(jnp.concatenate([a[:, CTRL:], b[:, CTRL:]], 0))
    from_rows = tn_product(edge, jnp.concatenate(along_rows, 1))
    basis_both = pair_ref[...]
    turned = []
    for pair in range(pairs):
        rows = slice(pair * CTRL, (pair + 1) * CTRL)
        spectral = (sums[0, rows, :] + sums[1, rows, :]) * series_ref[...]
        spectral = spectral + from_rows[:, pair * LANES : (pair + 1) * LANES]
        turned.append(spectral + tn_product(along_cols[pair], both))
    turned = product(jnp.concatenate(turned, 0), basis_both)
    flat = jnp.concatenate([turned[pair * CTRL : (pair + 1) * CTRL] for pair in range(pairs)], 1)
    done = product(basis_ref[...], flat)
    for pair in range(pairs):
        out_ref[2 * pair] = done[:, pair * LANES : pair * LANES + CTRL]
        out_ref[2 * pair + 1] = done[:, pair * LANES + CTRL : (pair + 1) * LANES]


def tn_product(x, y):
    x_high, x_low = halves(x)
    y_high, y_low = halves(y)
    return tn(x_high, y_high) + (tn(x_low, y_high) + tn(x_high, y_low))


def smooth(payloads, items, early, where, adjacency, per_owner, const):
    patches = adjacency.shape[0]
    return pl.pallas_call(
        functools.partial(smooth_kernel, items, per_owner, bool(early)),
        out_shape=jax.ShapeDtypeStruct((per_owner, CTRL, CTRL), F32),
        in_specs=[SMEM] + [WHOLE] * 7 + [VMEM] * (len(payloads) + len(early)),
        out_specs=VMEM,
        scratch_shapes=[
            *[pltpu.VMEM(shape.shape, F32) for shape in sum_shapes(per_owner, patches)],
            *absorb_scratch(items),
            pltpu.VMEM((2, patches, 4 * CTRL), F32),
            pltpu.VMEM((per_owner * 8, LANES), F32),
        ],
        compiler_params=params(32),
        name="smooth",
    )(
        where, adjacency, const["coupling"], const["basis"], const["basis_pair"], const["series"],
        const["edge_rows"], const["scale_rows"], *payloads, *early,
    )


def gather_and_smooth(payload, adjacency, vol_count, dsg_count, const):
    patches = adjacency.shape[0]
    per_owner = patches // dsg_count
    y_at = lax.axis_index("vol") % 2 if (vol_count, dsg_count) == (8, 4) else 0
    where = jnp.stack([lax.axis_index("dsg"), y_at]).astype(jnp.int32)
    if vol_count != 8 or dsg_count != 4:
        whole = lax.all_gather(payload, ("vol", "dsg"), axis=0, tiled=True)
        items = ((vol_count * dsg_count, 0, 0),)
        return smooth([whole], items, (), where, adjacency, per_owner, const)

    def over(axis, array, bit):
        count = vol_count if axis == "vol" else dsg_count
        return lax.ppermute(array, axis, [(i, i ^ bit) for i in range(count)])

    copies = jnp.broadcast_to(payload[None], (vol_count // 2,) + payload.shape)
    along_z = lax.all_to_all(
        copies, "vol", split_axis=0, concat_axis=0, tiled=True,
        axis_index_groups=[list(range(y, vol_count, 2)) for y in range(2)],
    )
    here = along_z.reshape(-1, LANES)
    half = here.shape[0] // 2
    beside_y = over("vol", here, 1)
    beside_x = over("dsg", here, 2)
    corner = [over("dsg", beside_y[:half], 2), over("vol", beside_x[half:], 1)]
    first = [here, over("dsg", here, 1), beside_x, over("dsg", beside_x, 1)]
    first += [beside_y, over("dsg", beside_y, 1)]
    items = ((4, 0, 0), (4, 0, 0), (4, 0, 1), (4, 0, 1), (4, 1, 0), (4, 1, 0))
    early = early_sums(first, items, where, per_owner, patches)
    last = corner + [over("dsg", c, 1) for c in corner]
    return smooth(last, ((2, 1, 1),) * 4, early, where, adjacency, per_owner, const)


def per_device(
    fields, far_geom, far_block, far_cell, far_patch, near_geom, near_cell, near_patch, adjacency
):
    vol_count, dsg_count = lax.axis_size("vol"), lax.axis_size("dsg")
    far_count = far_cell.shape[0]
    capacity = 5 * far_count // (2 * vol_count)
    const = {name: jnp.asarray(value) for name, value in constants().items()}

    request, place = pack_requests(
        far_geom, far_block.reshape(1, -1), far_cell.reshape(1, -1), vol_count, capacity
    )
    asked = lax.all_to_all(request, "vol", split_axis=0, concat_axis=0, tiled=True)
    near_dens = near_densities(near_cell, fields, near_geom)
    answer = far_answers(asked, fields, near_dens)
    reply = lax.all_to_all(answer, "vol", split_axis=0, concat_axis=0, tiled=True)
    near_patch, far_patch = near_patch.reshape(1, -1), far_patch.reshape(1, -1)
    near_grid, slots = near_grids(near_dens, near_geom, near_patch, far_patch)
    far_dens, payload = make_payload(reply, place, far_geom, far_patch, slots, near_grid, const)

    design = gather_and_smooth(payload, adjacency, vol_count, dsg_count, const)
    return far_dens.reshape(-1), design


def solution(mesh):
    return jax.shard_map(
        per_device,
        mesh=mesh,
        in_specs=(
            P("vol", None),
            P(None, ("vol", "dsg")),
            P(("vol", "dsg"), None),
            P(("vol", "dsg")),
            P(("vol", "dsg")),
            P(None, ("vol", "dsg")),
            P(("vol", "dsg")),
            P(("vol", "dsg")),
            P(),
        ),
        out_specs=(P(("vol", "dsg")), P("dsg", None, None)),
        check_vma=False,
    )
```

```python
import functools

import jax
import jax.numpy as jnp
import numpy as np
from jax import lax
from jax.experimental import pallas as pl
from jax.experimental.pallas import tpu as pltpu
from jax.sharding import PartitionSpec as P

CTRL = 64
GROUP = 4
LANES = 128
PENALTY = 4.0
SMOOTHING = 16.0
NO_PATCH = 1.0e6
GRID_ROWS = GROUP // 2 * CTRL
PAYLOAD_ROWS = GRID_ROWS + 2 * GROUP
F32 = jnp.float32
BF16 = jnp.bfloat16
EXACT = lax.Precision.HIGHEST
VMEM = pl.BlockSpec(memory_space=pltpu.VMEM)
SMEM = pl.BlockSpec(memory_space=pltpu.SMEM)
ANY = pl.BlockSpec(memory_space=pl.ANY)
WHOLE = pl.BlockSpec()
HBM = pl.BlockSpec(memory_space=pltpu.HBM)


def params(megabytes):
    return pltpu.CompilerParams(vmem_limit_bytes=megabytes << 20)


def constants():
    order = np.arange(1, CTRL + 1)
    basis = np.sqrt(2.0 / (CTRL + 1)) * np.sin(np.pi * np.outer(order, order) / (CTRL + 1))
    eigen = 1.0 + SMOOTHING * (2.0 - 2.0 * np.cos(np.pi * order / (CTRL + 1)))
    damp = 1.0 / eigen
    keep = 1.0 - damp
    powers = [keep**k * damp for k in range(3)]
    ends = [basis[:, 0], basis[:, CTRL - 1]]
    edge_rows = np.zeros((8, CTRL))
    scale_rows = np.zeros((8, CTRL))
    for k in range(3):
        for side in range(2):
            edge_rows[2 * k + side] = powers[k] * ends[side]
            scale_rows[2 * k + side] = powers[k]
    series = sum(np.outer(keep**k * damp, keep**k * damp) for k in range(4))

    def coupling(k):
        f = powers[k]
        lane = [0, 2, 1, 3]
        out = np.zeros((4 * CTRL, 4 * CTRL))
        for a, side_in in enumerate(lane):
            for b, side_out in enumerate(lane):
                q_in, q_out = ends[side_in % 2], ends[side_out % 2]
                if side_in // 2 == side_out // 2:
                    block = np.diag(f * np.sum(q_in * q_out * f))
                else:
                    block = np.outer(q_out * f, q_in * f)
                out[a * CTRL : (a + 1) * CTRL, b * CTRL : (b + 1) * CTRL] = SMOOTHING * block
        return out

    return dict(
        basis=np.float32(basis),
        basis_pair=np.float32(np.kron(np.eye(2), basis)),
        edge_rows=np.float32(edge_rows),
        scale_rows=np.float32(np.concatenate([scale_rows, scale_rows], 1)),
        series=np.float32(np.concatenate([series, series], 1)),
        coupling=np.float32(np.concatenate([coupling(0), coupling(1)], 1)),
    )


def split3(x):
    high = x.astype(BF16).astype(F32)
    rest = x - high
    mid = rest.astype(BF16).astype(F32)
    return high, mid, rest - mid


def nt(a, b, **kw):
    return lax.dot_general(a, b, (((1,), (1,)), ((), ())), preferred_element_type=F32, **kw)


def nn(a, b, **kw):
    return lax.dot_general(a, b, (((1,), (0,)), ((), ())), preferred_element_type=F32, **kw)


def tn(a, b, **kw):
    return lax.dot_general(a, b, (((0,), (0,)), ((), ())), preferred_element_type=F32, **kw)


def iota(shape, axis):
    return lax.broadcasted_iota(jnp.int32, shape, axis)


def halves(x):
    high = x.astype(BF16)
    return high, (x - high.astype(F32)).astype(BF16)


def two(x):
    return jnp.concatenate(halves(x), 1)


def fold(x):
    half = x.shape[1] // 2
    return x[:, :half] + x[:, half:]


def product(x, y):
    x_high, x_low = halves(x)
    y_high, y_low = halves(y)
    return nn(x_high, y_high) + (nn(x_low, y_high) + nn(x_high, y_low))


def nt_product(x, y):
    x_high, x_low = halves(x)
    y_high, y_low = halves(y)
    return nt(x_high, y_high) + (nt(x_low, y_high) + nt(x_high, y_low))


def fetch(pairs, sem):
    copies = [pltpu.make_async_copy(a, b, sem.at[i]) for i, (a, b) in enumerate(pairs)]
    for copy in copies:
        copy.start()
    for copy in copies:
        copy.wait()


def pack_kernel(capacity, geom_in, block_in, cell_in, request_ref, place_ref, geom_ref, block_ref, cell_ref, sem):
    fetch([(geom_in, geom_ref), (block_in, block_ref), (cell_in, cell_ref)], sem)
    owners = request_ref.shape[0]
    count = geom_ref.shape[1]
    block = block_ref[...]
    owner_id = iota((owners, count), 0)
    chosen = jnp.where(owner_id == block, 1.0, 0.0).astype(F32)
    earlier = jnp.where(iota((count, count), 0) < iota((count, count), 1), 1.0, 0.0).astype(BF16)
    rank = nn(chosen.astype(BF16), earlier)
    place = jnp.sum(chosen * (rank + (capacity * owner_id).astype(F32)), axis=0, keepdims=True)
    place = place.astype(jnp.int32)
    place_ref[...] = place
    row = iota((8, count), 0)
    values = jnp.where(row < 6, geom_ref[...], jnp.where(row == 6, cell_ref[...].astype(F32), 0.0))
    high, mid, low = split3(values)
    parts = jnp.concatenate([high, mid, low], 0).astype(BF16)
    put = jnp.where(iota((owners * capacity, count), 0) == place, 1.0, 0.0).astype(BF16)
    packed = nt(parts, put)
    packed = (packed[16:24] + packed[8:16]) + packed[0:8]
    for owner in range(owners):
        request_ref[owner] = packed[:, owner * capacity : (owner + 1) * capacity]


def pack_requests(far_geom, far_block, far_cell, owners, capacity):
    count = far_geom.shape[1]
    return pl.pallas_call(
        functools.partial(pack_kernel, capacity),
        out_shape=(
            jax.ShapeDtypeStruct((owners, 8, capacity), F32),
            jax.ShapeDtypeStruct((1, count), jnp.int32),
        ),
        in_specs=[HBM] * 3,
        out_specs=(VMEM, VMEM),
        scratch_shapes=[
            pltpu.VMEM((8, count), F32),
            pltpu.VMEM((1, count), jnp.int32),
            pltpu.VMEM((1, count), jnp.int32),
            pltpu.SemaphoreType.DMA((3,)),
        ],
        compiler_params=params(60),
        name="pack_requests",
    )(far_geom, far_block, far_cell)


def gather_rows(cells, fields_ref, rows_ref, count):
    unroll = 32

    def step(i, carry):
        for u in range(unroll):
            p = i * unroll + u
            rows_ref[pl.ds(p, 1), :] = fields_ref[pl.ds(cells(p), 1), :]
        return carry

    lax.fori_loop(0, count // unroll, step, 0)


def bernstein(t):
    u = 1.0 - t
    uu, tt = u * u, t * t
    values = [uu * u, 3.0 * t * uu, 3.0 * tt * u, tt * t]
    tu = 6.0 * t * u
    slopes = [-3.0 * uu, 3.0 * uu - tu, tu - 3.0 * tt, 3.0 * tt]
    return values, slopes


def tile_density(columns, geom):
    row = iota((8, LANES), 0)
    wide = [jnp.broadcast_to(geom[r : r + 1], (8, LANES)) for r in range(3)]
    x_val, x_der = bernstein(wide[0])
    y_val, y_der = bernstein(wide[1])
    z_val, z_der = bernstein(wide[2])
    k = row % 4

    def by_k(v):
        return jnp.where(k == 0, v[0], jnp.where(k == 1, v[1], jnp.where(k == 2, v[2], v[3])))

    def by_j(v, m):
        return jnp.where(row < 4, v[2 * m], v[2 * m + 1])

    z_v, z_d = by_k(z_val), by_k(z_der)
    yz = [by_j(y_val, m) * z_v for m in range(2)]
    dyz = [by_j(y_der, m) * z_v for m in range(2)]
    ydz = [by_j(y_val, m) * z_d for m in range(2)]
    sums = []
    for half in range(2):
        total = [None] * 4
        for i in range(4):
            at = half * 64 + i * 16
            first, second = columns[at : at + 8], columns[at + 8 : at + 16]
            plain = first * yz[0] + second * yz[1]
            along_y = first * dyz[0] + second * dyz[1]
            along_z = first * ydz[0] + second * ydz[1]
            terms = [x_val[i] * plain, x_der[i] * plain, x_val[i] * along_y, x_val[i] * along_z]
            total = [t if s is None else s + t for s, t in zip(total, terms)]
        sums.append([jnp.sum(t, axis=0, keepdims=True) for t in total])
    state, adjoint = sums
    n = [geom[3 + r : 4 + r] for r in range(3)]
    normal_sq = n[0] * n[0] + n[1] * n[1] + n[2] * n[2]
    inner = state[1] * adjoint[1] + state[2] * adjoint[2] + state[3] * adjoint[3]
    along_s = state[1] * n[0] + state[2] * n[1] + state[3] * n[2]
    along_a = adjoint[1] * n[0] + adjoint[2] * n[1] + adjoint[3] * n[2]
    return normal_sq * inner - 2.0 * along_s * along_a + PENALTY * normal_sq * state[0] * adjoint[0]


def densities(rows_ref, geom_ref, out_ref, count):
    def step(tile, carry):
        at = pl.multiple_of(tile * LANES, LANES)
        columns = rows_ref[pl.ds(at, LANES), :].T
        out_ref[:, pl.ds(at, LANES)] = tile_density(columns, geom_ref[:, pl.ds(at, LANES)])
        return carry

    tiles = count // LANES
    lax.fori_loop(0, tiles, step, 0, unroll=4 if tiles % 4 == 0 else 2)


def near_kernel(cell_in, fields_in, geom_in, out_ref, cell_ref, fields_ref, geom_ref, rows_ref, sem):
    count = geom_in.shape[1]
    fetch([(fields_in, fields_ref), (cell_in, cell_ref), (geom_in, geom_ref)], sem)
    gather_rows(lambda p: cell_ref[p], fields_ref, rows_ref, count)
    densities(rows_ref, geom_ref, out_ref, count)


def near_densities(near_cell, fields, near_geom):
    count = near_geom.shape[1]
    return pl.pallas_call(
        near_kernel,
        out_shape=jax.ShapeDtypeStruct((1, count), F32),
        in_specs=[HBM] * 3,
        out_specs=VMEM,
        scratch_shapes=[
            pltpu.SMEM((count,), jnp.int32),
            pltpu.VMEM(fields.shape, F32),
            pltpu.VMEM((8, count), F32),
            pltpu.VMEM((count, LANES), F32),
            pltpu.SemaphoreType.DMA((3,)),
        ],
        compiler_params=params(60),
        cost_estimate=pl.CostEstimate(flops=40_000_000, bytes_accessed=4_000_000, transcendentals=0),
        name="near_densities",
    )(near_cell, fields, near_geom)


def far_kernel(
    request_in, fields_in, near_ref, out_ref, request_ref, fields_ref, query_ref, cell_v, cell_s, rows_ref, dens_ref,
    sems, sem,
):
    owners, _, capacity = request_in.shape
    fields_copy = pltpu.make_async_copy(fields_in, fields_ref, sems.at[1])
    fields_copy.start()
    fetch([(request_in, request_ref)], sems)
    count = owners * capacity
    for o in range(owners):
        query_ref[:, o * capacity : (o + 1) * capacity] = request_ref[o]
    cell_v[...] = query_ref[6:7, :].astype(jnp.int32)
    copy = pltpu.make_async_copy(cell_v, cell_s, sem)
    copy.start()
    copy.wait()
    fields_copy.wait()
    gather_rows(lambda p: cell_s[0, p], fields_ref, rows_ref, count)
    densities(rows_ref, query_ref, dens_ref, count)
    for o in range(owners):
        out_ref[o] = dens_ref[:, o * capacity : (o + 1) * capacity]


def far_answers(requests, fields, near_dens):
    owners, _, capacity = requests.shape
    count = owners * capacity
    return pl.pallas_call(
        far_kernel,
        out_shape=jax.ShapeDtypeStruct((owners, 1, capacity), F32),
        in_specs=[ANY, ANY, ANY],
        out_specs=VMEM,
        scratch_shapes=[
            pltpu.VMEM(requests.shape, F32),
            pltpu.VMEM(fields.shape, F32),
            pltpu.VMEM((8, count), F32),
            pltpu.VMEM((1, count), jnp.int32),
            pltpu.SMEM((1, count), jnp.int32),
            pltpu.VMEM((count, LANES), F32),
            pltpu.VMEM((1, count), F32),
            pltpu.SemaphoreType.DMA((2,)),
            pltpu.SemaphoreType.DMA,
        ],
        compiler_params=params(24),
        name="far_answers",
    )(requests, fields, near_dens)


def spline_columns(param):
    scaled = param * float(CTRL - 3)
    start = jnp.clip(jnp.floor(scaled), 0.0, float(CTRL - 4))
    x = scaled - start
    u = 1.0 - x
    cubed, squared = x * x * x, x * x
    weights = [
        u * u * u * (1.0 / 6.0),
        (3.0 * cubed - 6.0 * squared + 4.0) * (1.0 / 6.0),
        (-3.0 * cubed + 3.0 * squared + 3.0 * x + 1.0) * (1.0 / 6.0),
        cubed * (1.0 / 6.0),
    ]
    off = iota((CTRL, param.shape[1]), 0) - start.astype(jnp.int32)
    out = jnp.zeros(off.shape, F32)
    for m in range(4):
        out = jnp.where(off == m, weights[m], out)
    return out


def slot_grids(density, s, t, patch, slots):
    left_high, left_low = halves(spline_columns(s))
    right_high, right_low = halves(spline_columns(t) * density)
    masks = [jnp.where(patch == slot, 1.0, 0.0).astype(BF16) for slot in slots]
    high = jnp.concatenate([left_high * m for m in masks], 0)
    low = jnp.concatenate([left_low * m for m in masks], 0)
    return nt(high, right_high) + (nt(high, right_low) + nt(low, right_high))


def near_grid_kernel(dens_ref, geom_ref, near_ref, far_ref, grid_ref, slot_ref):
    near, far = near_ref[...].astype(F32), far_ref[...].astype(F32)
    slots = []
    last = jnp.full((1, 1), -1.0, F32)
    for _ in range(GROUP):
        a = jnp.min(jnp.where(near > last, near, NO_PATCH), axis=1, keepdims=True)
        b = jnp.min(jnp.where(far > last, far, NO_PATCH), axis=1, keepdims=True)
        last = jnp.minimum(a, b)
        slots.append(last)
    slot_ref[...] = jnp.concatenate([jnp.broadcast_to(s, (1, LANES)) for s in slots + slots], 0)
    grid_ref[...] = slot_grids(dens_ref[...], geom_ref[6:7, :], geom_ref[7:8, :], near, slots)


def near_grids(dens, near_geom, near_patch, far_patch):
    return pl.pallas_call(
        near_grid_kernel,
        out_shape=(
            jax.ShapeDtypeStruct((GROUP * CTRL, CTRL), F32),
            jax.ShapeDtypeStruct((8, LANES), F32),
        ),
        in_specs=[VMEM] + [WHOLE] * 3,
        out_specs=(VMEM, VMEM),
        compiler_params=params(24),
        cost_estimate=pl.CostEstimate(flops=80_000_000, bytes_accessed=1_000_000, transcendentals=0),
        name="near_grids",
    )(dens, near_geom, near_patch, far_patch)


def payload_kernel(
    reply_ref, place_ref, geom_ref, far_ref, slot_ref, near_ref,
    basis_ref, pair_ref,
    dens_ref, out_ref, flat_ref,
):
    owners, _, capacity = reply_ref.shape
    count = geom_ref.shape[1]
    for o in range(owners):
        flat_ref[:, o * capacity : (o + 1) * capacity] = reply_ref[o]
    high, mid, low = split3(flat_ref[...])
    parts = jnp.concatenate([high, mid, low, jnp.zeros((5, owners * capacity), F32)], 0).astype(BF16)
    put = jnp.where(iota((owners * capacity, count), 0) == place_ref[...], 1.0, 0.0).astype(BF16)
    got = nn(parts, put)
    dens = (got[2:3] + got[1:2]) + got[0:1]
    dens_ref[...] = dens
    slots = [slot_ref[s : s + 1, 0:1] for s in range(GROUP)]
    grids = near_ref[...] + slot_grids(
        dens, geom_ref[6:7, :], geom_ref[7:8, :], far_ref[...].astype(F32), slots
    )
    lane = iota((1, LANES), 1)
    names = jnp.zeros((1, LANES), F32)
    for s in range(GROUP):
        names = jnp.where(lane == s, slot_ref[s : s + 1, :], names)
    out_ref[GRID_ROWS : GRID_ROWS + GROUP, :] = slot_ref[0:GROUP, :]
    out_ref[GRID_ROWS + GROUP : PAYLOAD_ROWS, :] = jnp.broadcast_to(names, (GROUP, LANES))
    blocks = [
        jnp.concatenate([grids[a * CTRL : (a + 1) * CTRL], grids[(a + 1) * CTRL : (a + 2) * CTRL]], 1)
        for a in range(0, GROUP, 2)
    ]
    turned = product(jnp.concatenate(blocks, 0), pair_ref[...])
    turned = jnp.concatenate([turned[:CTRL], turned[CTRL:]], 1)
    spectral = product(basis_ref[...], turned)
    for pair in range(GROUP // 2):
        out_ref[pair * CTRL : (pair + 1) * CTRL, :] = spectral[:, pair * LANES : (pair + 1) * LANES]


def make_payload(reply, place, far_geom, far_patch, slots, near_grid, const):
    owners, _, capacity = reply.shape
    count = far_geom.shape[1]
    return pl.pallas_call(
        payload_kernel,
        out_shape=(
            jax.ShapeDtypeStruct((1, count), F32),
            jax.ShapeDtypeStruct((PAYLOAD_ROWS, LANES), F32),
        ),
        in_specs=[VMEM] * 2 + [WHOLE] * 2 + [VMEM] * 2 + [WHOLE] * 2,
        out_specs=(VMEM, VMEM),
        scratch_shapes=[pltpu.VMEM((1, owners * capacity), F32)],
        compiler_params=params(24),
        name="make_payload",
    )(
        reply, place, far_geom, far_patch, slots, near_grid,
        const["basis"], const["basis_pair"],
    )


def pair_rows(edge):
    blank = jnp.zeros((8, CTRL), F32)
    return jnp.concatenate([jnp.concatenate([edge, blank], 1), jnp.concatenate([blank, edge], 1)], 0)


def absorb(first_own, y_at, per_owner, items, sums, groups, edge, scale, name_v, name_s, edges, where_to, name_sem):
    patches = groups.shape[2]
    low8 = iota((8, LANES), 1) < CTRL
    at = 0
    for ref, parts, _, _ in items:
        for p in range(parts):
            last = (p + 1) * PAYLOAD_ROWS - 1
            name_v[at : at + 1, :] = ref[last : last + 1, :].astype(jnp.int32)
            at += 1
    names = pltpu.make_async_copy(name_v, name_s, name_sem)
    names.start()

    sums[...] = jnp.zeros(sums.shape, F32)
    edge_high, edge_low = halves(edge)
    edge_both = jnp.concatenate([edge_high, edge_low], 0)
    both_high, both_low = halves(pair_rows(edge))
    both_both = jnp.concatenate([both_high, both_low], 0)
    for group in sorted({(dy, dx) for _, _, dy, dx in items}):
        at = 0
        chunks = [
            (ref, p) for ref, parts, dy, dx in items if (dy, dx) == group for p in range(0, parts, 2)
        ]
        for ref, start in chunks:
            blocks = []
            for p in (start, start + 1):
                row = p * PAYLOAD_ROWS
                blocks += [halves(ref[row + q * CTRL : row + (q + 1) * CTRL, :]) for q in range(GROUP // 2)]
                row += GRID_ROWS
                where_to[at + GROUP * (p - start) : at + GROUP * (p - start + 1), :] = ref[row : row + GROUP, :]
            high, low = [jnp.concatenate(x, 1) for x in zip(*blocks)]
            along_rows = nn(edge_both, high)
            along_rows = (along_rows[:8] + along_rows[8:]) + nn(edge_high, low)
            high, low = [jnp.concatenate(x, 0) for x in zip(*blocks)]
            along_cols = nt(both_both, high)
            along_cols = (along_cols[:16] + along_cols[16:]) + nt(both_high, low)
            for s in range(2 * GROUP):
                q = s // 2
                first = along_rows[:, q * LANES : (q + 1) * LANES]
                second = along_cols[8 * (s % 2) : 8 * (s % 2) + 8, q // 2 * LANES : (q // 2 + 1) * LANES]
                if s % 2:
                    first = pltpu.roll(first, CTRL, 1)
                if q % 2 == 0:
                    second = pltpu.roll(second, CTRL, 1)
                edges[8 * at : 8 * at + 8, :] = jnp.where(low8, first, second) * scale
                at += 1
        lane = iota((at, LANES), 1)
        place = jnp.where(lane == where_to[:at, :].astype(jnp.int32), 1.0, 0.0).T[:patches].astype(BF16)
        for k in range(3):
            rows = [edges[pl.ds(2 * k + side, at, stride=8), :] for side in range(2)]
            groups[(group[0] ^ y_at) * 2 + group[1], k] = fold(nn(place, two(jnp.concatenate(rows, 1))))

    names.wait()

    def add_items(wanted):
        at = 0
        for ref, parts, dy, _ in items:

            def add_payload(p, carry, ref=ref, at=at):
                for s in range(GROUP):
                    patch = name_s[at + p, s] - first_own

                    @pl.when((patch >= 0) & (patch < per_owner))
                    def _():
                        row = pl.multiple_of(p * PAYLOAD_ROWS + (s // 2) * CTRL, 8)
                        own = pl.multiple_of(patch * CTRL, CTRL)
                        sums[s % 2, pl.ds(own, CTRL), :] = sums[s % 2, pl.ds(own, CTRL), :] + ref[pl.ds(row, CTRL), :]

                return carry

            if dy == wanted:
                lax.fori_loop(0, parts, add_payload, 0)
            at += parts

    @pl.when(y_at == 0)
    def _():
        add_items(0)
        add_items(1)

    @pl.when(y_at != 0)
    def _():
        add_items(1)
        add_items(0)


def smooth_kernel(
    items, per_owner, where_ref, adj_ref, coupling_ref, basis_ref, pair_ref, series_ref, edge_ref, scale_ref, *rest
):
    refs, rest = rest[: len(items)], rest[len(items) :]
    out_ref, sums, groups, halo_all, halo_rows, *scratch = rest
    patches = adj_ref.shape[0]
    first_own = pl.multiple_of(where_ref[0] * per_owner, 8)
    items = [(ref, *item) for ref, item in zip(refs, items)]
    edge = edge_ref[...]
    scale = scale_ref[...]
    if len(items) == 1:
        groups[...] = jnp.zeros(groups.shape, F32)
    absorb(first_own, where_ref[1], per_owner, items, sums, groups, edge, scale, *scratch)
    base = [(groups[0, k] + groups[1, k]) + (groups[2, k] + groups[3, k]) for k in range(3)]

    column = iota((patches, patches), 1)
    wide = 4 * CTRL

    def facing(adjacency):
        hits = [
            jnp.where(adjacency[:, s : s + 1] == column[: adjacency.shape[0]], 1.0, 0.0).astype(BF16)
            for s in range(4)
        ]
        return jnp.concatenate([hits[0], hits[2]], 0), jnp.concatenate([hits[1], hits[3]], 0)

    def halo(facing, edges):
        count = facing[0].shape[0] // 2
        low_lane = iota((count, LANES), 1) < CTRL
        first = fold(nn(facing[0], two(edges[:, LANES:])))
        second = fold(nn(facing[1], two(edges[:, :LANES])))
        return jnp.concatenate(
            [jnp.where(low_lane, x[:count], x[count:]) for x in (first, second)], 1
        )

    every = facing(adj_ref[...])
    halo0 = halo(every, base[0])
    effect0 = product(halo0, coupling_ref[...])
    edges1 = base[0] + base[1] + effect0[:, :wide]
    halo1 = halo(every, edges1)
    effect1 = product(halo1, coupling_ref[:, :wide])
    edges2 = base[0] + base[1] + base[2] + effect0[:, wide:] + effect1
    halo2 = halo(facing(adj_ref[pl.ds(first_own, per_owner), :]), edges2)
    halo_all[0] = halo1
    halo_all[1] = halo0
    for k in range(3):
        mine = halo2 if k == 0 else halo_all[k - 1, pl.ds(first_own, per_owner), :]
        factor = SMOOTHING * scale[2 * k : 2 * k + 1]
        for side in range(2):
            halo_rows[pl.ds(2 * k + side, per_owner, stride=8), :] = (
                mine[:, side * LANES : (side + 1) * LANES] * factor
            )
    zero = jnp.zeros((per_owner, LANES), F32)
    for r in (6, 7):
        halo_rows[pl.ds(r, per_owner, stride=8), :] = zero

    pairs = per_owner // 2
    both = pair_rows(edge)
    low8 = iota((8, LANES), 1) < CTRL
    along_rows, along_cols = [], []
    for pair in range(pairs):
        a = halo_rows[16 * pair : 16 * pair + 8, :]
        b = halo_rows[16 * pair + 8 : 16 * pair + 16, :]
        along_rows.append(jnp.where(low8, a, pltpu.roll(b, CTRL, 1)))
        along_cols.append(jnp.concatenate([a[:, CTRL:], b[:, CTRL:]], 0))
    from_rows = tn_product(edge, jnp.concatenate(along_rows, 1))
    low_half = iota((CTRL, LANES), 1) < CTRL
    basis_both = pair_ref[...]
    turned = []
    for pair in range(pairs):
        a, b = [slice(patch * CTRL, (patch + 1) * CTRL) for patch in (2 * pair, 2 * pair + 1)]
        left = sums[0, a, :] + pltpu.roll(sums[1, a, :], CTRL, 1)
        right = pltpu.roll(sums[0, b, :], CTRL, 1) + sums[1, b, :]
        spectral = jnp.where(low_half, left, right) * series_ref[...]
        spectral = spectral + from_rows[:, pair * LANES : (pair + 1) * LANES]
        turned.append(spectral + tn_product(along_cols[pair], both))
    turned = product(jnp.concatenate(turned, 0), basis_both)
    flat = jnp.concatenate([turned[pair * CTRL : (pair + 1) * CTRL] for pair in range(pairs)], 1)
    done = product(basis_ref[...], flat)
    for pair in range(pairs):
        out_ref[2 * pair] = done[:, pair * LANES : pair * LANES + CTRL]
        out_ref[2 * pair + 1] = done[:, pair * LANES + CTRL : (pair + 1) * LANES]


def tn_product(x, y):
    x_high, x_low = halves(x)
    y_high, y_low = halves(y)
    return tn(x_high, y_high) + (tn(x_low, y_high) + tn(x_high, y_low))


def smooth(payloads, items, where, adjacency, per_owner, const):
    patches = adjacency.shape[0]
    total = sum(item[0] for item in items)
    return pl.pallas_call(
        functools.partial(smooth_kernel, items, per_owner),
        out_shape=jax.ShapeDtypeStruct((per_owner, CTRL, CTRL), F32),
        in_specs=[SMEM] + [WHOLE] * 7 + [VMEM] * len(payloads),
        out_specs=VMEM,
        scratch_shapes=[
            pltpu.VMEM((2, per_owner * CTRL, LANES), F32),
            pltpu.VMEM((4, 3, patches, 4 * CTRL), F32),
            pltpu.VMEM((2, patches, 4 * CTRL), F32),
            pltpu.VMEM((per_owner * 8, LANES), F32),
            pltpu.VMEM((total, LANES), jnp.int32),
            pltpu.SMEM((total, LANES), jnp.int32),
            pltpu.VMEM((total * GROUP * 8, LANES), F32),
            pltpu.VMEM((total * GROUP, LANES), F32),
            pltpu.SemaphoreType.DMA,
        ],
        compiler_params=params(32),
        name="smooth",
    )(
        where, adjacency, const["coupling"], const["basis"], const["basis_pair"], const["series"],
        const["edge_rows"], const["scale_rows"], *payloads,
    )


def gather_and_smooth(payload, adjacency, vol_count, dsg_count, const):
    patches = adjacency.shape[0]
    per_owner = patches // dsg_count
    y_at = lax.axis_index("vol") % 2 if (vol_count, dsg_count) == (8, 4) else 0
    where = jnp.stack([lax.axis_index("dsg"), y_at]).astype(jnp.int32)
    if vol_count != 8 or dsg_count != 4:
        whole = lax.all_gather(payload, ("vol", "dsg"), axis=0, tiled=True)
        items = ((vol_count * dsg_count, 0, 0),)
        return smooth([whole], items, where, adjacency, per_owner, const)

    def over(axis, array, bit):
        count = vol_count if axis == "vol" else dsg_count
        return lax.ppermute(array, axis, [(i, i ^ bit) for i in range(count)])

    copies = jnp.broadcast_to(payload[None], (vol_count // 2,) + payload.shape)
    along_z = lax.all_to_all(
        copies, "vol", split_axis=0, concat_axis=0, tiled=True,
        axis_index_groups=[list(range(y, vol_count, 2)) for y in range(2)],
    )
    here = along_z.reshape(-1, LANES)
    half = here.shape[0] // 2
    beside_y = over("vol", here, 1)
    beside_x = over("dsg", here, 2)
    corner = [over("dsg", beside_y[:half], 2), over("vol", beside_x[half:], 1)]
    arrays = [here, beside_x, beside_y]
    arrays = [x for array in arrays for x in (array, over("dsg", array, 1))]
    arrays += corner + [over("dsg", c, 1) for c in corner]
    items = ((4, 0, 0), (4, 0, 0), (4, 0, 1), (4, 0, 1), (4, 1, 0), (4, 1, 0)) + ((2, 1, 1),) * 4
    return smooth(arrays, items, where, adjacency, per_owner, const)


def per_device(
    fields, far_geom, far_block, far_cell, far_patch, near_geom, near_cell, near_patch, adjacency
):
    vol_count, dsg_count = lax.axis_size("vol"), lax.axis_size("dsg")
    far_count = far_cell.shape[0]
    capacity = 5 * far_count // (2 * vol_count)
    const = {name: jnp.asarray(value) for name, value in constants().items()}

    request, place = pack_requests(
        far_geom, far_block.reshape(1, -1), far_cell.reshape(1, -1), vol_count, capacity
    )
    asked = lax.all_to_all(request, "vol", split_axis=0, concat_axis=0, tiled=True)
    near_dens = near_densities(near_cell, fields, near_geom)
    answer = far_answers(asked, fields, near_dens)
    reply = lax.all_to_all(answer, "vol", split_axis=0, concat_axis=0, tiled=True)
    near_patch, far_patch = near_patch.reshape(1, -1), far_patch.reshape(1, -1)
    near_grid, slots = near_grids(near_dens, near_geom, near_patch, far_patch)
    far_dens, payload = make_payload(reply, place, far_geom, far_patch, slots, near_grid, const)

    design = gather_and_smooth(payload, adjacency, vol_count, dsg_count, const)
    return far_dens.reshape(-1), design


def solution(mesh):
    return jax.shard_map(
        per_device,
        mesh=mesh,
        in_specs=(
            P("vol", None),
            P(None, ("vol", "dsg")),
            P(("vol", "dsg"), None),
            P(("vol", "dsg")),
            P(("vol", "dsg")),
            P(None, ("vol", "dsg")),
            P(("vol", "dsg")),
            P(("vol", "dsg")),
            P(),
        ),
        out_specs=(P(("vol", "dsg")), P("dsg", None, None)),
        check_vma=False,
    )
```

```python
import functools

import jax
import jax.numpy as jnp
import numpy as np
from jax import lax
from jax.experimental import pallas as pl
from jax.experimental.pallas import tpu as pltpu
from jax.sharding import PartitionSpec as P

CTRL = 64
GROUP = 4
LANES = 128
PENALTY = 4.0
SMOOTHING = 16.0
NO_PATCH = 1.0e6
GRID_ROWS = GROUP // 2 * CTRL
PAYLOAD_ROWS = GRID_ROWS + 2 * GROUP
F32 = jnp.float32
BF16 = jnp.bfloat16
EXACT = lax.Precision.HIGHEST
VMEM = pl.BlockSpec(memory_space=pltpu.VMEM)
SMEM = pl.BlockSpec(memory_space=pltpu.SMEM)
ANY = pl.BlockSpec(memory_space=pl.ANY)
WHOLE = pl.BlockSpec()
HBM = pl.BlockSpec(memory_space=pltpu.HBM)


def params(megabytes):
    return pltpu.CompilerParams(vmem_limit_bytes=megabytes << 20)


def constants():
    order = np.arange(1, CTRL + 1)
    basis = np.sqrt(2.0 / (CTRL + 1)) * np.sin(np.pi * np.outer(order, order) / (CTRL + 1))
    eigen = 1.0 + SMOOTHING * (2.0 - 2.0 * np.cos(np.pi * order / (CTRL + 1)))
    damp = 1.0 / eigen
    keep = 1.0 - damp
    powers = [keep**k * damp for k in range(3)]
    ends = [basis[:, 0], basis[:, CTRL - 1]]
    edge_rows = np.zeros((8, CTRL))
    scale_rows = np.zeros((8, CTRL))
    for k in range(3):
        for side in range(2):
            edge_rows[2 * k + side] = powers[k] * ends[side]
            scale_rows[2 * k + side] = powers[k]
    series = sum(np.outer(keep**k * damp, keep**k * damp) for k in range(4))

    def coupling(k):
        f = powers[k]
        lane = [0, 2, 1, 3]
        out = np.zeros((4 * CTRL, 4 * CTRL))
        for a, side_in in enumerate(lane):
            for b, side_out in enumerate(lane):
                q_in, q_out = ends[side_in % 2], ends[side_out % 2]
                if side_in // 2 == side_out // 2:
                    block = np.diag(f * np.sum(q_in * q_out * f))
                else:
                    block = np.outer(q_out * f, q_in * f)
                out[a * CTRL : (a + 1) * CTRL, b * CTRL : (b + 1) * CTRL] = SMOOTHING * block
        return out

    return dict(
        basis=np.float32(basis),
        basis_pair=np.float32(np.kron(np.eye(2), basis)),
        edge_rows=np.float32(edge_rows),
        scale_rows=np.float32(np.concatenate([scale_rows, scale_rows], 1)),
        series=np.float32(np.concatenate([series, series], 1)),
        coupling=np.float32(np.concatenate([coupling(0), coupling(1)], 1)),
    )


def split3(x):
    high = x.astype(BF16).astype(F32)
    rest = x - high
    mid = rest.astype(BF16).astype(F32)
    return high, mid, rest - mid


def nt(a, b, **kw):
    return lax.dot_general(a, b, (((1,), (1,)), ((), ())), preferred_element_type=F32, **kw)


def nn(a, b, **kw):
    return lax.dot_general(a, b, (((1,), (0,)), ((), ())), preferred_element_type=F32, **kw)


def tn(a, b, **kw):
    return lax.dot_general(a, b, (((0,), (0,)), ((), ())), preferred_element_type=F32, **kw)


def iota(shape, axis):
    return lax.broadcasted_iota(jnp.int32, shape, axis)


def halves(x):
    high = x.astype(BF16)
    return high, (x - high.astype(F32)).astype(BF16)


def two(x):
    return jnp.concatenate(halves(x), 1)


def fold(x):
    half = x.shape[1] // 2
    return x[:, :half] + x[:, half:]


def product(x, y):
    x_high, x_low = halves(x)
    y_high, y_low = halves(y)
    return nn(x_high, y_high) + (nn(x_low, y_high) + nn(x_high, y_low))


def nt_product(x, y):
    x_high, x_low = halves(x)
    y_high, y_low = halves(y)
    return nt(x_high, y_high) + (nt(x_low, y_high) + nt(x_high, y_low))


def fetch(pairs, sem):
    copies = [pltpu.make_async_copy(a, b, sem.at[i]) for i, (a, b) in enumerate(pairs)]
    for copy in copies:
        copy.start()
    for copy in copies:
        copy.wait()


def pack_kernel(capacity, geom_in, block_in, cell_in, request_ref, place_ref, geom_ref, block_ref, cell_ref, sem):
    fetch([(geom_in, geom_ref), (block_in, block_ref), (cell_in, cell_ref)], sem)
    owners = request_ref.shape[0]
    count = geom_ref.shape[1]
    block = block_ref[...]
    owner_id = iota((owners, count), 0)
    chosen = jnp.where(owner_id == block, 1.0, 0.0).astype(F32)
    earlier = jnp.where(iota((count, count), 0) < iota((count, count), 1), 1.0, 0.0).astype(BF16)
    rank = nn(chosen.astype(BF16), earlier)
    place = jnp.sum(chosen * (rank + (capacity * owner_id).astype(F32)), axis=0, keepdims=True)
    place = place.astype(jnp.int32)
    place_ref[...] = place
    row = iota((8, count), 0)
    values = jnp.where(row < 6, geom_ref[...], jnp.where(row == 6, cell_ref[...].astype(F32), 0.0))
    high, mid, low = split3(values)
    parts = jnp.concatenate([high, mid, low], 0).astype(BF16)
    put = jnp.where(iota((owners * capacity, count), 0) == place, 1.0, 0.0).astype(BF16)
    packed = nt(parts, put)
    packed = (packed[16:24] + packed[8:16]) + packed[0:8]
    for owner in range(owners):
        request_ref[owner] = packed[:, owner * capacity : (owner + 1) * capacity]


def pack_requests(far_geom, far_block, far_cell, owners, capacity):
    count = far_geom.shape[1]
    return pl.pallas_call(
        functools.partial(pack_kernel, capacity),
        out_shape=(
            jax.ShapeDtypeStruct((owners, 8, capacity), F32),
            jax.ShapeDtypeStruct((1, count), jnp.int32),
        ),
        in_specs=[HBM] * 3,
        out_specs=(VMEM, VMEM),
        scratch_shapes=[
            pltpu.VMEM((8, count), F32),
            pltpu.VMEM((1, count), jnp.int32),
            pltpu.VMEM((1, count), jnp.int32),
            pltpu.SemaphoreType.DMA((3,)),
        ],
        compiler_params=params(60),
        name="pack_requests",
    )(far_geom, far_block, far_cell)


def gather_rows(cells, fields_ref, rows_ref, count):
    unroll = 32

    def step(i, carry):
        for u in range(unroll):
            p = i * unroll + u
            rows_ref[pl.ds(p, 1), :] = fields_ref[pl.ds(cells(p), 1), :]
        return carry

    lax.fori_loop(0, count // unroll, step, 0)


def bernstein(t):
    u = 1.0 - t
    uu, tt = u * u, t * t
    values = [uu * u, 3.0 * t * uu, 3.0 * tt * u, tt * t]
    tu = 6.0 * t * u
    slopes = [-3.0 * uu, 3.0 * uu - tu, tu - 3.0 * tt, 3.0 * tt]
    return values, slopes


def tile_density(columns, geom):
    row = iota((8, LANES), 0)
    wide = [jnp.broadcast_to(geom[r : r + 1], (8, LANES)) for r in range(3)]
    x_val, x_der = bernstein(wide[0])
    y_val, y_der = bernstein(wide[1])
    z_val, z_der = bernstein(wide[2])
    k = row % 4

    def by_k(v):
        return jnp.where(k == 0, v[0], jnp.where(k == 1, v[1], jnp.where(k == 2, v[2], v[3])))

    def by_j(v, m):
        return jnp.where(row < 4, v[2 * m], v[2 * m + 1])

    z_v, z_d = by_k(z_val), by_k(z_der)
    yz = [by_j(y_val, m) * z_v for m in range(2)]
    dyz = [by_j(y_der, m) * z_v for m in range(2)]
    ydz = [by_j(y_val, m) * z_d for m in range(2)]
    sums = []
    for half in range(2):
        total = [None] * 4
        for i in range(4):
            at = half * 64 + i * 16
            first, second = columns[at : at + 8], columns[at + 8 : at + 16]
            plain = first * yz[0] + second * yz[1]
            along_y = first * dyz[0] + second * dyz[1]
            along_z = first * ydz[0] + second * ydz[1]
            terms = [x_val[i] * plain, x_der[i] * plain, x_val[i] * along_y, x_val[i] * along_z]
            total = [t if s is None else s + t for s, t in zip(total, terms)]
        sums.append([jnp.sum(t, axis=0, keepdims=True) for t in total])
    state, adjoint = sums
    n = [geom[3 + r : 4 + r] for r in range(3)]
    normal_sq = n[0] * n[0] + n[1] * n[1] + n[2] * n[2]
    inner = state[1] * adjoint[1] + state[2] * adjoint[2] + state[3] * adjoint[3]
    along_s = state[1] * n[0] + state[2] * n[1] + state[3] * n[2]
    along_a = adjoint[1] * n[0] + adjoint[2] * n[1] + adjoint[3] * n[2]
    return normal_sq * inner - 2.0 * along_s * along_a + PENALTY * normal_sq * state[0] * adjoint[0]


def densities(rows_ref, geom_ref, out_ref, count):
    def step(tile, carry):
        at = pl.multiple_of(tile * LANES, LANES)
        columns = rows_ref[pl.ds(at, LANES), :].T
        out_ref[:, pl.ds(at, LANES)] = tile_density(columns, geom_ref[:, pl.ds(at, LANES)])
        return carry

    tiles = count // LANES
    lax.fori_loop(0, tiles, step, 0, unroll=4 if tiles % 4 == 0 else 2)


def near_kernel(first, cell_in, fields_in, geom_in, out_ref, cell_ref, fields_ref, geom_ref, rows_ref, sem):
    count = out_ref.shape[1]
    part = pl.ds(first, count)
    fetch([(cell_in.at[part], cell_ref), (geom_in.at[:, part], geom_ref), (fields_in, fields_ref)], sem)
    gather_rows(lambda p: cell_ref[p], fields_ref, rows_ref, count)
    densities(rows_ref, geom_ref, out_ref, count)


def near_scratch(fields, count):
    return [
        pltpu.SMEM((count,), jnp.int32),
        pltpu.VMEM(fields.shape, F32),
        pltpu.VMEM((8, count), F32),
        pltpu.VMEM((count, LANES), F32),
        pltpu.SemaphoreType.DMA((3,)),
    ]


def near_densities(near_cell, fields, near_geom, count):
    return pl.pallas_call(
        functools.partial(near_kernel, 0),
        out_shape=jax.ShapeDtypeStruct((1, count), F32),
        in_specs=[HBM] * 3,
        out_specs=VMEM,
        scratch_shapes=near_scratch(fields, count),
        compiler_params=params(60),
        cost_estimate=pl.CostEstimate(flops=20_000_000, bytes_accessed=4_000_000, transcendentals=0),
        name="near_densities",
    )(near_cell, fields, near_geom)


def far_kernel(
    request_in, fields_ref, out_ref, request_ref, query_ref, cell_v, cell_s, rows_ref, dens_ref, sems, sem
):
    owners, _, capacity = request_in.shape
    fetch([(request_in, request_ref)], sems)
    count = owners * capacity
    for o in range(owners):
        query_ref[:, o * capacity : (o + 1) * capacity] = request_ref[o]
    cell_v[...] = query_ref[6:7, :].astype(jnp.int32)
    copy = pltpu.make_async_copy(cell_v, cell_s, sem)
    copy.start()
    copy.wait()
    gather_rows(lambda p: cell_s[0, p], fields_ref, rows_ref, count)
    densities(rows_ref, query_ref, dens_ref, count)
    for o in range(owners):
        out_ref[o] = dens_ref[:, o * capacity : (o + 1) * capacity]


def far_answers(requests, fields):
    owners, _, capacity = requests.shape
    count = owners * capacity
    return pl.pallas_call(
        far_kernel,
        out_shape=jax.ShapeDtypeStruct((owners, 1, capacity), F32),
        in_specs=[ANY, VMEM],
        out_specs=VMEM,
        scratch_shapes=[
            pltpu.VMEM(requests.shape, F32),
            pltpu.VMEM((8, count), F32),
            pltpu.VMEM((1, count), jnp.int32),
            pltpu.SMEM((1, count), jnp.int32),
            pltpu.VMEM((count, LANES), F32),
            pltpu.VMEM((1, count), F32),
            pltpu.SemaphoreType.DMA((1,)),
            pltpu.SemaphoreType.DMA,
        ],
        compiler_params=params(24),
        name="far_answers",
    )(requests, fields)


def spline_columns(param):
    scaled = param * float(CTRL - 3)
    start = jnp.clip(jnp.floor(scaled), 0.0, float(CTRL - 4))
    x = scaled - start
    u = 1.0 - x
    cubed, squared = x * x * x, x * x
    weights = [
        u * u * u * (1.0 / 6.0),
        (3.0 * cubed - 6.0 * squared + 4.0) * (1.0 / 6.0),
        (-3.0 * cubed + 3.0 * squared + 3.0 * x + 1.0) * (1.0 / 6.0),
        cubed * (1.0 / 6.0),
    ]
    off = iota((CTRL, param.shape[1]), 0) - start.astype(jnp.int32)
    out = jnp.zeros(off.shape, F32)
    for m in range(4):
        out = jnp.where(off == m, weights[m], out)
    return out


def slot_grids(density, s, t, patch, slots):
    left_high, left_low = halves(spline_columns(s))
    right_high, right_low = halves(spline_columns(t) * density)
    masks = [jnp.where(patch == slot, 1.0, 0.0).astype(BF16) for slot in slots]
    high = jnp.concatenate([left_high * m for m in masks], 0)
    low = jnp.concatenate([left_low * m for m in masks], 0)
    return nt(high, right_high) + (nt(high, right_low) + nt(low, right_high))


def near_grid_kernel(
    dens_in, cell_in, fields_in, geom_in, near_in, far_in, grid_ref, slot_ref,
    dens_ref, spline_ref, near_ref, far_ref, rest_ref, cell_ref, fields_ref, geom_ref, rows_ref, more, sem,
):
    count, done = near_in.shape[1], dens_in.shape[1]
    others = [
        (dens_in, dens_ref.at[:, pl.ds(0, done)]),
        (geom_in, spline_ref),
        (near_in, near_ref),
        (far_in, far_ref),
    ]
    others = [pltpu.make_async_copy(a, b, more.at[i]) for i, (a, b) in enumerate(others)]
    for copy in others:
        copy.start()
    near_kernel(done, cell_in, fields_in, geom_in, rest_ref, cell_ref, fields_ref, geom_ref, rows_ref, sem)
    for copy in others:
        copy.wait()
    dens_ref[:, done:count] = rest_ref[...]
    near, far = near_ref[...].astype(F32), far_ref[...].astype(F32)
    slots = []
    last = jnp.full((1, 1), -1.0, F32)
    for _ in range(GROUP):
        a = jnp.min(jnp.where(near > last, near, NO_PATCH), axis=1, keepdims=True)
        b = jnp.min(jnp.where(far > last, far, NO_PATCH), axis=1, keepdims=True)
        last = jnp.minimum(a, b)
        slots.append(last)
    slot_ref[...] = jnp.concatenate([jnp.broadcast_to(s, (1, LANES)) for s in slots + slots], 0)
    grid_ref[...] = slot_grids(dens_ref[...], spline_ref[6:7, :], spline_ref[7:8, :], near, slots)


def near_grids(dens, near_cell, fields, near_geom, near_patch, far_patch):
    count, done = near_geom.shape[1], dens.shape[1]
    return pl.pallas_call(
        near_grid_kernel,
        out_shape=(
            jax.ShapeDtypeStruct((GROUP * CTRL, CTRL), F32),
            jax.ShapeDtypeStruct((8, LANES), F32),
        ),
        in_specs=[ANY] * 6,
        out_specs=(VMEM, VMEM),
        scratch_shapes=[
            pltpu.VMEM((1, count), F32),
            pltpu.VMEM((8, count), F32),
            pltpu.VMEM((1, count), jnp.int32),
            pltpu.VMEM(far_patch.shape, jnp.int32),
            pltpu.VMEM((1, count - done), F32),
            *near_scratch(fields, count - done)[:-1],
            pltpu.SemaphoreType.DMA((4,)),
            pltpu.SemaphoreType.DMA((3,)),
        ],
        compiler_params=params(24),
        cost_estimate=pl.CostEstimate(flops=100_000_000, bytes_accessed=4_000_000, transcendentals=0),
        name="near_grids",
    )(dens, near_cell, fields, near_geom, near_patch, far_patch)


def payload_kernel(
    reply_ref, place_ref, geom_ref, far_ref, slot_ref, near_ref,
    basis_ref, pair_ref,
    dens_ref, out_ref, flat_ref,
):
    owners, _, capacity = reply_ref.shape
    count = geom_ref.shape[1]
    for o in range(owners):
        flat_ref[:, o * capacity : (o + 1) * capacity] = reply_ref[o]
    high, mid, low = split3(flat_ref[...])
    parts = jnp.concatenate([high, mid, low, jnp.zeros((5, owners * capacity), F32)], 0).astype(BF16)
    put = jnp.where(iota((owners * capacity, count), 0) == place_ref[...], 1.0, 0.0).astype(BF16)
    got = nn(parts, put)
    dens = (got[2:3] + got[1:2]) + got[0:1]
    dens_ref[...] = dens
    slots = [slot_ref[s : s + 1, 0:1] for s in range(GROUP)]
    grids = near_ref[...] + slot_grids(
        dens, geom_ref[6:7, :], geom_ref[7:8, :], far_ref[...].astype(F32), slots
    )
    lane = iota((1, LANES), 1)
    names = jnp.zeros((1, LANES), F32)
    for s in range(GROUP):
        names = jnp.where(lane == s, slot_ref[s : s + 1, :], names)
    out_ref[GRID_ROWS : GRID_ROWS + GROUP, :] = slot_ref[0:GROUP, :]
    out_ref[GRID_ROWS + GROUP : PAYLOAD_ROWS, :] = jnp.broadcast_to(names, (GROUP, LANES))
    blocks = [
        jnp.concatenate([grids[a * CTRL : (a + 1) * CTRL], grids[(a + 1) * CTRL : (a + 2) * CTRL]], 1)
        for a in range(0, GROUP, 2)
    ]
    turned = product(jnp.concatenate(blocks, 0), pair_ref[...])
    turned = jnp.concatenate([turned[:CTRL], turned[CTRL:]], 1)
    spectral = product(basis_ref[...], turned)
    for pair in range(GROUP // 2):
        out_ref[pair * CTRL : (pair + 1) * CTRL, :] = spectral[:, pair * LANES : (pair + 1) * LANES]


def make_payload(reply, place, far_geom, far_patch, slots, near_grid, const):
    owners, _, capacity = reply.shape
    count = far_geom.shape[1]
    return pl.pallas_call(
        payload_kernel,
        out_shape=(
            jax.ShapeDtypeStruct((1, count), F32),
            jax.ShapeDtypeStruct((PAYLOAD_ROWS, LANES), F32),
        ),
        in_specs=[VMEM] * 2 + [WHOLE] * 2 + [VMEM] * 2 + [WHOLE] * 2,
        out_specs=(VMEM, VMEM),
        scratch_shapes=[pltpu.VMEM((1, owners * capacity), F32)],
        compiler_params=params(24),
        name="make_payload",
    )(
        reply, place, far_geom, far_patch, slots, near_grid,
        const["basis"], const["basis_pair"],
    )


def pair_rows(edge):
    blank = jnp.zeros((8, CTRL), F32)
    return jnp.concatenate([jnp.concatenate([edge, blank], 1), jnp.concatenate([blank, edge], 1)], 0)


def absorb(first_own, y_at, per_owner, items, sums, groups, edge, scale, name_v, name_s, edges, where_to, name_sem):
    patches = groups.shape[1]
    low8 = iota((8, LANES), 1) < CTRL
    at = 0
    for ref, parts, _, _ in items:
        for p in range(parts):
            last = (p + 1) * PAYLOAD_ROWS - 1
            patch = ref[last : last + 1, :].astype(jnp.int32) - first_own
            name_v[at : at + 1, :] = jnp.where((patch >= 0) & (patch < per_owner), patch, -1)
            at += 1
    names = pltpu.make_async_copy(name_v, name_s, name_sem)
    names.start()

    sums[...] = jnp.zeros(sums.shape, F32)
    edge_high, edge_low = halves(edge)
    edge_both = jnp.concatenate([edge_high, edge_low], 0)
    both_high, both_low = halves(pair_rows(edge))
    both_both = jnp.concatenate([both_high, both_low], 0)
    for dy in sorted({dy for _, _, dy, _ in items}):
        at = 0
        chunks = [(ref, p) for ref, parts, own, _ in items if own == dy for p in range(0, parts, 2)]
        for ref, start in chunks:
            blocks = []
            for p in (start, start + 1):
                row = p * PAYLOAD_ROWS
                blocks += [halves(ref[row + q * CTRL : row + (q + 1) * CTRL, :]) for q in range(GROUP // 2)]
                row += GRID_ROWS
                where_to[at + GROUP * (p - start) : at + GROUP * (p - start + 1), :] = ref[row : row + GROUP, :]
            high, low = [jnp.concatenate(x, 1) for x in zip(*blocks)]
            along_rows = nn(edge_both, high)
            along_rows = (along_rows[:8] + along_rows[8:]) + nn(edge_high, low)
            high, low = [jnp.concatenate(x, 0) for x in zip(*blocks)]
            along_cols = nt(both_both, high)
            along_cols = (along_cols[:16] + along_cols[16:]) + nt(both_high, low)
            for s in range(2 * GROUP):
                q = s // 2
                first = along_rows[:, q * LANES : (q + 1) * LANES]
                second = along_cols[8 * (s % 2) : 8 * (s % 2) + 8, q // 2 * LANES : (q // 2 + 1) * LANES]
                if s % 2:
                    first = pltpu.roll(first, CTRL, 1)
                if q % 2 == 0:
                    second = pltpu.roll(second, CTRL, 1)
                edges[8 * at : 8 * at + 8, :] = jnp.where(low8, first, second) * scale
                at += 1
        lane = iota((at, LANES), 1)
        place = jnp.where(lane == where_to[:at, :].astype(jnp.int32), 1.0, 0.0).T[:patches].astype(BF16)
        rows = jnp.concatenate([edges[pl.ds(r, at, stride=8), :] for r in range(6)], 1)
        groups[dy ^ y_at] = fold(nn(place, two(rows)))

    names.wait()

    def add_items(wanted):
        at = 0
        for ref, parts, dy, _ in items:

            def add_payload(p, carry, ref=ref, at=at):
                for s in range(GROUP):
                    patch = name_s[at + p, s]

                    @pl.when(patch >= 0)
                    def _():
                        row = pl.multiple_of(p * PAYLOAD_ROWS + (s // 2) * CTRL, 8)
                        own = pl.multiple_of(patch * CTRL, CTRL)
                        sums[s % 2, pl.ds(own, CTRL), :] = sums[s % 2, pl.ds(own, CTRL), :] + ref[pl.ds(row, CTRL), :]

                return carry

            if dy == wanted:
                lax.fori_loop(0, parts, add_payload, 0)
            at += parts

    @pl.when(y_at == 0)
    def _():
        add_items(0)
        add_items(1)

    @pl.when(y_at != 0)
    def _():
        add_items(1)
        add_items(0)


def smooth_kernel(
    items, per_owner, where_ref, adj_ref, coupling_ref, basis_ref, pair_ref, series_ref, edge_ref, scale_ref, *rest
):
    refs, rest = rest[: len(items)], rest[len(items) :]
    out_ref, sums, groups, halo_all, halo_rows, *scratch = rest
    patches = adj_ref.shape[0]
    first_own = pl.multiple_of(where_ref[0] * per_owner, 8)
    items = [(ref, *item) for ref, item in zip(refs, items)]
    edge = edge_ref[...]
    scale = scale_ref[...]
    if len(items) == 1:
        groups[...] = jnp.zeros(groups.shape, F32)
    absorb(first_own, where_ref[1], per_owner, items, sums, groups, edge, scale, *scratch)
    base = groups[0] + groups[1]
    base = [base[:, 4 * CTRL * k : 4 * CTRL * (k + 1)] for k in range(3)]

    column = iota((patches, patches), 1)
    wide = 4 * CTRL

    def facing(adjacency):
        hits = [
            jnp.where(adjacency[:, s : s + 1] == column[: adjacency.shape[0]], 1.0, 0.0).astype(BF16)
            for s in range(4)
        ]
        return jnp.concatenate([hits[0], hits[2]], 0), jnp.concatenate([hits[1], hits[3]], 0)

    def halo(facing, edges):
        count = facing[0].shape[0] // 2
        low_lane = iota((count, LANES), 1) < CTRL
        first = fold(nn(facing[0], two(edges[:, LANES:])))
        second = fold(nn(facing[1], two(edges[:, :LANES])))
        return jnp.concatenate(
            [jnp.where(low_lane, x[:count], x[count:]) for x in (first, second)], 1
        )

    every = facing(adj_ref[...])
    halo0 = halo(every, base[0])
    effect0 = product(halo0, coupling_ref[...])
    edges1 = base[0] + base[1] + effect0[:, :wide]
    halo1 = halo(every, edges1)
    effect1 = product(halo1, coupling_ref[:, :wide])
    edges2 = base[0] + base[1] + base[2] + effect0[:, wide:] + effect1
    halo2 = halo(facing(adj_ref[pl.ds(first_own, per_owner), :]), edges2)
    halo_all[0] = halo1
    halo_all[1] = halo0
    for k in range(3):
        mine = halo2 if k == 0 else halo_all[k - 1, pl.ds(first_own, per_owner), :]
        factor = SMOOTHING * scale[2 * k : 2 * k + 1]
        for side in range(2):
            halo_rows[pl.ds(2 * k + side, per_owner, stride=8), :] = (
                mine[:, side * LANES : (side + 1) * LANES] * factor
            )
    zero = jnp.zeros((per_owner, LANES), F32)
    for r in (6, 7):
        halo_rows[pl.ds(r, per_owner, stride=8), :] = zero

    pairs = per_owner // 2
    both = pair_rows(edge)
    low8 = iota((8, LANES), 1) < CTRL
    along_rows, along_cols = [], []
    for pair in range(pairs):
        a = halo_rows[16 * pair : 16 * pair + 8, :]
        b = halo_rows[16 * pair + 8 : 16 * pair + 16, :]
        along_rows.append(jnp.where(low8, a, pltpu.roll(b, CTRL, 1)))
        low, high = (pltpu.roll(x, CTRL, 1) for x in (a, b)) if pair % 2 == 0 else (a, b)
        along_cols.append(jnp.concatenate([low, high], 0))
    from_rows = tn_product(edge, jnp.concatenate(along_rows, 1))
    low_half = iota((CTRL, LANES), 1) < CTRL
    basis_both = pair_ref[...]
    low16 = iota((16, LANES), 1) < CTRL
    along_cols = [jnp.where(low16, x, y) for x, y in zip(along_cols[::2], along_cols[1::2])]
    from_cols = tn_product(jnp.concatenate(along_cols, 1), both)
    turned = []
    for pair in range(pairs):
        a, b = [slice(patch * CTRL, (patch + 1) * CTRL) for patch in (2 * pair, 2 * pair + 1)]
        left = sums[0, a, :] + pltpu.roll(sums[1, a, :], CTRL, 1)
        right = pltpu.roll(sums[0, b, :], CTRL, 1) + sums[1, b, :]
        spectral = jnp.where(low_half, left, right) * series_ref[...]
        spectral = spectral + from_rows[:, pair * LANES : (pair + 1) * LANES]
        turned.append(spectral + from_cols[pair * CTRL : (pair + 1) * CTRL, :])
    turned = product(jnp.concatenate(turned, 0), basis_both)
    flat = jnp.concatenate([turned[pair * CTRL : (pair + 1) * CTRL] for pair in range(pairs)], 1)
    done = product(basis_ref[...], flat)
    for pair in range(pairs):
        out_ref[2 * pair] = done[:, pair * LANES : pair * LANES + CTRL]
        out_ref[2 * pair + 1] = done[:, pair * LANES + CTRL : (pair + 1) * LANES]


def tn_product(x, y):
    x_high, x_low = halves(x)
    y_high, y_low = halves(y)
    return tn(x_high, y_high) + (tn(x_low, y_high) + tn(x_high, y_low))


def smooth(payloads, items, where, adjacency, per_owner, const):
    patches = adjacency.shape[0]
    total = sum(item[0] for item in items)
    return pl.pallas_call(
        functools.partial(smooth_kernel, items, per_owner),
        out_shape=jax.ShapeDtypeStruct((per_owner, CTRL, CTRL), F32),
        in_specs=[SMEM] + [WHOLE] * 7 + [VMEM] * len(payloads),
        out_specs=VMEM,
        scratch_shapes=[
            pltpu.VMEM((2, per_owner * CTRL, LANES), F32),
            pltpu.VMEM((2, patches, 12 * CTRL), F32),
            pltpu.VMEM((2, patches, 4 * CTRL), F32),
            pltpu.VMEM((per_owner * 8, LANES), F32),
            pltpu.VMEM((total, LANES), jnp.int32),
            pltpu.SMEM((total, LANES), jnp.int32),
            pltpu.VMEM((total * GROUP * 8, LANES), F32),
            pltpu.VMEM((total * GROUP, LANES), F32),
            pltpu.SemaphoreType.DMA,
        ],
        compiler_params=params(32),
        name="smooth",
    )(
        where, adjacency, const["coupling"], const["basis"], const["basis_pair"], const["series"],
        const["edge_rows"], const["scale_rows"], *payloads,
    )


def gather_and_smooth(payload, adjacency, vol_count, dsg_count, const):
    patches = adjacency.shape[0]
    per_owner = patches // dsg_count
    y_at = lax.axis_index("vol") % 2 if (vol_count, dsg_count) == (8, 4) else 0
    where = jnp.stack([lax.axis_index("dsg"), y_at]).astype(jnp.int32)
    if vol_count != 8 or dsg_count != 4:
        whole = lax.all_gather(payload, ("vol", "dsg"), axis=0, tiled=True)
        items = ((vol_count * dsg_count, 0, 0),)
        return smooth([whole], items, where, adjacency, per_owner, const)

    def over(axis, array, bit):
        count = vol_count if axis == "vol" else dsg_count
        return lax.ppermute(array, axis, [(i, i ^ bit) for i in range(count)])

    copies = jnp.broadcast_to(payload[None], (vol_count // 2,) + payload.shape)
    along_z = lax.all_to_all(
        copies, "vol", split_axis=0, concat_axis=0, tiled=True,
        axis_index_groups=[list(range(y, vol_count, 2)) for y in range(2)],
    )
    here = along_z.reshape(-1, LANES)
    half = here.shape[0] // 2
    beside_y = over("vol", here, 1)
    beside_x = over("dsg", here, 2)
    corner = [over("dsg", beside_y[:half], 2), over("vol", beside_x[half:], 1)]
    arrays = [here, beside_x, beside_y]
    arrays = [x for array in arrays for x in (array, over("dsg", array, 1))]
    arrays += corner + [over("dsg", c, 1) for c in corner]
    items = ((4, 0, 0), (4, 0, 0), (4, 0, 1), (4, 0, 1), (4, 1, 0), (4, 1, 0)) + ((2, 1, 1),) * 4
    return smooth(arrays, items, where, adjacency, per_owner, const)


def per_device(
    fields, far_geom, far_block, far_cell, far_patch, near_geom, near_cell, near_patch, adjacency
):
    vol_count, dsg_count = lax.axis_size("vol"), lax.axis_size("dsg")
    far_count = far_cell.shape[0]
    capacity = 5 * far_count // (2 * vol_count)
    const = {name: jnp.asarray(value) for name, value in constants().items()}

    request, place = pack_requests(
        far_geom, far_block.reshape(1, -1), far_cell.reshape(1, -1), vol_count, capacity
    )
    asked = lax.all_to_all(request, "vol", split_axis=0, concat_axis=0, tiled=True)
    near_dens = near_densities(near_cell, fields, near_geom, near_cell.shape[0] // 2)
    asked, near_dens = lax.optimization_barrier((asked, near_dens))
    answer = far_answers(asked, fields)
    reply = lax.all_to_all(answer, "vol", split_axis=0, concat_axis=0, tiled=True)
    near_patch, far_patch = near_patch.reshape(1, -1), far_patch.reshape(1, -1)
    near_grid, slots = near_grids(near_dens, near_cell, fields, near_geom, near_patch, far_patch)
    far_dens, payload = make_payload(reply, place, far_geom, far_patch, slots, near_grid, const)

    design = gather_and_smooth(payload, adjacency, vol_count, dsg_count, const)
    return far_dens.reshape(-1), design


def solution(mesh):
    return jax.shard_map(
        per_device,
        mesh=mesh,
        in_specs=(
            P("vol", None),
            P(None, ("vol", "dsg")),
            P(("vol", "dsg"), None),
            P(("vol", "dsg")),
            P(("vol", "dsg")),
            P(None, ("vol", "dsg")),
            P(("vol", "dsg")),
            P(("vol", "dsg")),
            P(),
        ),
        out_specs=(P(("vol", "dsg")), P("dsg", None, None)),
        check_vma=False,
    )
```

```python
import functools

import jax
import jax.numpy as jnp
import numpy as np
from jax import lax
from jax.experimental import pallas as pl
from jax.experimental.pallas import tpu as pltpu
from jax.sharding import PartitionSpec as P

CTRL = 64
GROUP = 4
LANES = 128
PENALTY = 4.0
SMOOTHING = 16.0
NO_PATCH = 1.0e6
GRID_ROWS = GROUP // 2 * CTRL
PAYLOAD_ROWS = GRID_ROWS + 2 * GROUP
F32 = jnp.float32
BF16 = jnp.bfloat16
EXACT = lax.Precision.HIGHEST
VMEM = pl.BlockSpec(memory_space=pltpu.VMEM)
SMEM = pl.BlockSpec(memory_space=pltpu.SMEM)
ANY = pl.BlockSpec(memory_space=pl.ANY)
WHOLE = pl.BlockSpec()
HBM = pl.BlockSpec(memory_space=pltpu.HBM)


def params(megabytes):
    return pltpu.CompilerParams(vmem_limit_bytes=megabytes << 20)


def constants():
    order = np.arange(1, CTRL + 1)
    basis = np.sqrt(2.0 / (CTRL + 1)) * np.sin(np.pi * np.outer(order, order) / (CTRL + 1))
    eigen = 1.0 + SMOOTHING * (2.0 - 2.0 * np.cos(np.pi * order / (CTRL + 1)))
    damp = 1.0 / eigen
    keep = 1.0 - damp
    powers = [keep**k * damp for k in range(3)]
    ends = [basis[:, 0], basis[:, CTRL - 1]]
    edge_rows = np.zeros((8, CTRL))
    scale_rows = np.zeros((8, CTRL))
    for k in range(3):
        for side in range(2):
            edge_rows[2 * k + side] = powers[k] * ends[side]
            scale_rows[2 * k + side] = powers[k]
    series = sum(np.outer(keep**k * damp, keep**k * damp) for k in range(4))

    def coupling(k):
        f = powers[k]
        lane = [0, 2, 1, 3]
        out = np.zeros((4 * CTRL, 4 * CTRL))
        for a, side_in in enumerate(lane):
            for b, side_out in enumerate(lane):
                q_in, q_out = ends[side_in % 2], ends[side_out % 2]
                if side_in // 2 == side_out // 2:
                    block = np.diag(f * np.sum(q_in * q_out * f))
                else:
                    block = np.outer(q_out * f, q_in * f)
                out[a * CTRL : (a + 1) * CTRL, b * CTRL : (b + 1) * CTRL] = SMOOTHING * block
        return out

    return dict(
        basis=np.float32(basis),
        basis_pair=np.float32(np.kron(np.eye(2), basis)),
        edge_rows=np.float32(edge_rows),
        scale_rows=np.float32(np.concatenate([scale_rows, scale_rows], 1)),
        series=np.float32(np.concatenate([series, series], 1)),
        coupling=np.float32(np.concatenate([coupling(0), coupling(1)], 1)),
    )


def split3(x):
    high = x.astype(BF16).astype(F32)
    rest = x - high
    mid = rest.astype(BF16).astype(F32)
    return high, mid, rest - mid


def nt(a, b, **kw):
    return lax.dot_general(a, b, (((1,), (1,)), ((), ())), preferred_element_type=F32, **kw)


def nn(a, b, **kw):
    return lax.dot_general(a, b, (((1,), (0,)), ((), ())), preferred_element_type=F32, **kw)


def tn(a, b, **kw):
    return lax.dot_general(a, b, (((0,), (0,)), ((), ())), preferred_element_type=F32, **kw)


def iota(shape, axis):
    return lax.broadcasted_iota(jnp.int32, shape, axis)


def halves(x):
    high = x.astype(BF16)
    return high, (x - high.astype(F32)).astype(BF16)


def two(x):
    return jnp.concatenate(halves(x), 1)


def fold(x):
    half = x.shape[1] // 2
    return x[:, :half] + x[:, half:]


def product(x, y):
    x_high, x_low = halves(x)
    y_high, y_low = halves(y)
    return nn(x_high, y_high) + (nn(x_low, y_high) + nn(x_high, y_low))


def nt_product(x, y):
    x_high, x_low = halves(x)
    y_high, y_low = halves(y)
    return nt(x_high, y_high) + (nt(x_low, y_high) + nt(x_high, y_low))


def fetch(pairs, sem):
    copies = [pltpu.make_async_copy(a, b, sem.at[i]) for i, (a, b) in enumerate(pairs)]
    for copy in copies:
        copy.start()
    for copy in copies:
        copy.wait()


def pack_kernel(capacity, geom_in, block_in, cell_in, request_ref, place_ref, geom_ref, block_ref, cell_ref, sem):
    fetch([(geom_in, geom_ref), (block_in, block_ref), (cell_in, cell_ref)], sem)
    owners = request_ref.shape[0]
    count = geom_ref.shape[1]
    block = block_ref[...]
    owner_id = iota((owners, count), 0)
    chosen = jnp.where(owner_id == block, 1.0, 0.0).astype(F32)
    earlier = jnp.where(iota((count, count), 0) < iota((count, count), 1), 1.0, 0.0).astype(BF16)
    rank = nn(chosen.astype(BF16), earlier)
    place = jnp.sum(chosen * (rank + (capacity * owner_id).astype(F32)), axis=0, keepdims=True)
    place = place.astype(jnp.int32)
    place_ref[...] = place
    row = iota((8, count), 0)
    values = jnp.where(row < 6, geom_ref[...], jnp.where(row == 6, cell_ref[...].astype(F32), 0.0))
    high, mid, low = split3(values)
    parts = jnp.concatenate([high, mid, low], 0).astype(BF16)
    put = jnp.where(iota((owners * capacity, count), 0) == place, 1.0, 0.0).astype(BF16)
    packed = nt(parts, put)
    packed = (packed[16:24] + packed[8:16]) + packed[0:8]
    for owner in range(owners):
        request_ref[owner] = packed[:, owner * capacity : (owner + 1) * capacity]


def pack_requests(far_geom, far_block, far_cell, owners, capacity):
    count = far_geom.shape[1]
    return pl.pallas_call(
        functools.partial(pack_kernel, capacity),
        out_shape=(
            jax.ShapeDtypeStruct((owners, 8, capacity), F32),
            jax.ShapeDtypeStruct((1, count), jnp.int32),
        ),
        in_specs=[HBM] * 3,
        out_specs=(VMEM, VMEM),
        scratch_shapes=[
            pltpu.VMEM((8, count), F32),
            pltpu.VMEM((1, count), jnp.int32),
            pltpu.VMEM((1, count), jnp.int32),
            pltpu.SemaphoreType.DMA((3,)),
        ],
        compiler_params=params(60),
        name="pack_requests",
    )(far_geom, far_block, far_cell)


def gather_rows(cells, fields_ref, rows_ref, count):
    unroll = 32

    def step(i, carry):
        for u in range(unroll):
            p = i * unroll + u
            rows_ref[pl.ds(p, 1), :] = fields_ref[pl.ds(cells(p), 1), :]
        return carry

    lax.fori_loop(0, count // unroll, step, 0)


def bernstein(t):
    u = 1.0 - t
    uu, tt = u * u, t * t
    values = [uu * u, 3.0 * t * uu, 3.0 * tt * u, tt * t]
    tu = 6.0 * t * u
    slopes = [-3.0 * uu, 3.0 * uu - tu, tu - 3.0 * tt, 3.0 * tt]
    return values, slopes


def tile_density(columns, geom):
    row = iota((8, LANES), 0)
    wide = [jnp.broadcast_to(geom[r : r + 1], (8, LANES)) for r in range(3)]
    x_val, x_der = bernstein(wide[0])
    y_val, y_der = bernstein(wide[1])
    z_val, z_der = bernstein(wide[2])
    k = row % 4

    def by_k(v):
        return jnp.where(k == 0, v[0], jnp.where(k == 1, v[1], jnp.where(k == 2, v[2], v[3])))

    def by_j(v, m):
        return jnp.where(row < 4, v[2 * m], v[2 * m + 1])

    z_v, z_d = by_k(z_val), by_k(z_der)
    yz = [by_j(y_val, m) * z_v for m in range(2)]
    dyz = [by_j(y_der, m) * z_v for m in range(2)]
    ydz = [by_j(y_val, m) * z_d for m in range(2)]
    sums = []
    for half in range(2):
        total = [None] * 4
        for i in range(4):
            at = half * 64 + i * 16
            first, second = columns[at : at + 8], columns[at + 8 : at + 16]
            plain = first * yz[0] + second * yz[1]
            along_y = first * dyz[0] + second * dyz[1]
            along_z = first * ydz[0] + second * ydz[1]
            terms = [x_val[i] * plain, x_der[i] * plain, x_val[i] * along_y, x_val[i] * along_z]
            total = [t if s is None else s + t for s, t in zip(total, terms)]
        sums.append([jnp.sum(t, axis=0, keepdims=True) for t in total])
    state, adjoint = sums
    n = [geom[3 + r : 4 + r] for r in range(3)]
    normal_sq = n[0] * n[0] + n[1] * n[1] + n[2] * n[2]
    inner = state[1] * adjoint[1] + state[2] * adjoint[2] + state[3] * adjoint[3]
    along_s = state[1] * n[0] + state[2] * n[1] + state[3] * n[2]
    along_a = adjoint[1] * n[0] + adjoint[2] * n[1] + adjoint[3] * n[2]
    return normal_sq * inner - 2.0 * along_s * along_a + PENALTY * normal_sq * state[0] * adjoint[0]


def densities(rows_ref, geom_ref, out_ref, count):
    def step(tile, carry):
        at = pl.multiple_of(tile * LANES, LANES)
        columns = rows_ref[pl.ds(at, LANES), :].T
        out_ref[:, pl.ds(at, LANES)] = tile_density(columns, geom_ref[:, pl.ds(at, LANES)])
        return carry

    tiles = count // LANES
    lax.fori_loop(0, tiles, step, 0, unroll=4 if tiles % 4 == 0 else 2)


def near_kernel(first, cell_in, fields_in, geom_in, out_ref, cell_ref, fields_ref, geom_ref, rows_ref, sem):
    count = out_ref.shape[1]
    part = pl.ds(first, count)
    fetch([(cell_in.at[part], cell_ref), (geom_in.at[:, part], geom_ref), (fields_in, fields_ref)], sem)
    gather_rows(lambda p: cell_ref[p], fields_ref, rows_ref, count)
    densities(rows_ref, geom_ref, out_ref, count)


def near_scratch(fields, count):
    return [
        pltpu.SMEM((count,), jnp.int32),
        pltpu.VMEM(fields.shape, F32),
        pltpu.VMEM((8, count), F32),
        pltpu.VMEM((count, LANES), F32),
        pltpu.SemaphoreType.DMA((3,)),
    ]


def near_densities(near_cell, fields, near_geom, count):
    return pl.pallas_call(
        functools.partial(near_kernel, 0),
        out_shape=jax.ShapeDtypeStruct((1, count), F32),
        in_specs=[HBM] * 3,
        out_specs=VMEM,
        scratch_shapes=near_scratch(fields, count),
        compiler_params=params(60),
        cost_estimate=pl.CostEstimate(flops=20_000_000, bytes_accessed=4_000_000, transcendentals=0),
        name="near_densities",
    )(near_cell, fields, near_geom)


def far_kernel(
    request_in, fields_ref, out_ref, request_ref, query_ref, cell_v, cell_s, rows_ref, dens_ref, sems, sem
):
    owners, _, capacity = request_in.shape
    fetch([(request_in, request_ref)], sems)
    count = owners * capacity
    for o in range(owners):
        query_ref[:, o * capacity : (o + 1) * capacity] = request_ref[o]
    cell_v[...] = query_ref[6:7, :].astype(jnp.int32)
    copy = pltpu.make_async_copy(cell_v, cell_s, sem)
    copy.start()
    copy.wait()
    gather_rows(lambda p: cell_s[0, p], fields_ref, rows_ref, count)
    densities(rows_ref, query_ref, dens_ref, count)
    for o in range(owners):
        out_ref[o] = dens_ref[:, o * capacity : (o + 1) * capacity]


def far_answers(requests, fields):
    owners, _, capacity = requests.shape
    count = owners * capacity
    return pl.pallas_call(
        far_kernel,
        out_shape=jax.ShapeDtypeStruct((owners, 1, capacity), F32),
        in_specs=[ANY, VMEM],
        out_specs=VMEM,
        scratch_shapes=[
            pltpu.VMEM(requests.shape, F32),
            pltpu.VMEM((8, count), F32),
            pltpu.VMEM((1, count), jnp.int32),
            pltpu.SMEM((1, count), jnp.int32),
            pltpu.VMEM((count, LANES), F32),
            pltpu.VMEM((1, count), F32),
            pltpu.SemaphoreType.DMA((1,)),
            pltpu.SemaphoreType.DMA,
        ],
        compiler_params=params(24),
        name="far_answers",
    )(requests, fields)


def spline_columns(param):
    scaled = param * float(CTRL - 3)
    start = jnp.clip(jnp.floor(scaled), 0.0, float(CTRL - 4))
    x = scaled - start
    u = 1.0 - x
    cubed, squared = x * x * x, x * x
    weights = [
        u * u * u * (1.0 / 6.0),
        (3.0 * cubed - 6.0 * squared + 4.0) * (1.0 / 6.0),
        (-3.0 * cubed + 3.0 * squared + 3.0 * x + 1.0) * (1.0 / 6.0),
        cubed * (1.0 / 6.0),
    ]
    off = iota((CTRL, param.shape[1]), 0) - start.astype(jnp.int32)
    out = jnp.zeros(off.shape, F32)
    for m in range(4):
        out = jnp.where(off == m, weights[m], out)
    return out


def slot_grids(density, s, t, patch, slots):
    left_high, left_low = halves(spline_columns(s))
    right_high, right_low = halves(spline_columns(t) * density)
    masks = [jnp.where(patch == slot, 1.0, 0.0).astype(BF16) for slot in slots]
    high = jnp.concatenate([left_high * m for m in masks], 0)
    low = jnp.concatenate([left_low * m for m in masks], 0)
    return nt(high, right_high) + (nt(high, right_low) + nt(low, right_high))


def near_grid_kernel(
    dens_in, cell_in, fields_in, geom_in, near_in, far_in, grid_ref, slot_ref,
    dens_ref, spline_ref, near_ref, far_ref, rest_ref, cell_ref, fields_ref, geom_ref, rows_ref, more, sem,
):
    count, done = near_in.shape[1], dens_in.shape[1]
    others = [
        (dens_in, dens_ref.at[:, pl.ds(0, done)]),
        (geom_in, spline_ref),
        (near_in, near_ref),
        (far_in, far_ref),
    ]
    others = [pltpu.make_async_copy(a, b, more.at[i]) for i, (a, b) in enumerate(others)]
    for copy in others:
        copy.start()
    near_kernel(done, cell_in, fields_in, geom_in, rest_ref, cell_ref, fields_ref, geom_ref, rows_ref, sem)
    for copy in others:
        copy.wait()
    dens_ref[:, done:count] = rest_ref[...]
    near, far = near_ref[...].astype(F32), far_ref[...].astype(F32)
    slots = []
    last = jnp.full((1, 1), -1.0, F32)
    for _ in range(GROUP):
        a = jnp.min(jnp.where(near > last, near, NO_PATCH), axis=1, keepdims=True)
        b = jnp.min(jnp.where(far > last, far, NO_PATCH), axis=1, keepdims=True)
        last = jnp.minimum(a, b)
        slots.append(last)
    slot_ref[...] = jnp.concatenate([jnp.broadcast_to(s, (1, LANES)) for s in slots + slots], 0)
    grid_ref[...] = slot_grids(dens_ref[...], spline_ref[6:7, :], spline_ref[7:8, :], near, slots)


def near_grids(dens, near_cell, fields, near_geom, near_patch, far_patch):
    count, done = near_geom.shape[1], dens.shape[1]
    return pl.pallas_call(
        near_grid_kernel,
        out_shape=(
            jax.ShapeDtypeStruct((GROUP * CTRL, CTRL), F32),
            jax.ShapeDtypeStruct((8, LANES), F32),
        ),
        in_specs=[ANY] * 6,
        out_specs=(VMEM, VMEM),
        scratch_shapes=[
            pltpu.VMEM((1, count), F32),
            pltpu.VMEM((8, count), F32),
            pltpu.VMEM((1, count), jnp.int32),
            pltpu.VMEM(far_patch.shape, jnp.int32),
            pltpu.VMEM((1, count - done), F32),
            *near_scratch(fields, count - done)[:-1],
            pltpu.SemaphoreType.DMA((4,)),
            pltpu.SemaphoreType.DMA((3,)),
        ],
        compiler_params=params(24),
        cost_estimate=pl.CostEstimate(flops=100_000_000, bytes_accessed=4_000_000, transcendentals=0),
        name="near_grids",
    )(dens, near_cell, fields, near_geom, near_patch, far_patch)


def payload_kernel(
    reply_ref, place_ref, geom_ref, far_ref, slot_ref, near_ref,
    basis_ref, pair_ref,
    dens_ref, out_ref, flat_ref,
):
    owners, _, capacity = reply_ref.shape
    count = geom_ref.shape[1]
    for o in range(owners):
        flat_ref[:, o * capacity : (o + 1) * capacity] = reply_ref[o]
    high, mid, low = split3(flat_ref[...])
    parts = jnp.concatenate([high, mid, low, jnp.zeros((5, owners * capacity), F32)], 0).astype(BF16)
    put = jnp.where(iota((owners * capacity, count), 0) == place_ref[...], 1.0, 0.0).astype(BF16)
    got = nn(parts, put)
    dens = (got[2:3] + got[1:2]) + got[0:1]
    dens_ref[...] = dens
    slots = [slot_ref[s : s + 1, 0:1] for s in range(GROUP)]
    grids = near_ref[...] + slot_grids(
        dens, geom_ref[6:7, :], geom_ref[7:8, :], far_ref[...].astype(F32), slots
    )
    lane = iota((1, LANES), 1)
    names = jnp.zeros((1, LANES), F32)
    for s in range(GROUP):
        names = jnp.where(lane == s, slot_ref[s : s + 1, :], names)
    out_ref[GRID_ROWS : GRID_ROWS + GROUP, :] = slot_ref[0:GROUP, :]
    out_ref[GRID_ROWS + GROUP : PAYLOAD_ROWS, :] = jnp.broadcast_to(names, (GROUP, LANES))
    blocks = [
        jnp.concatenate([grids[a * CTRL : (a + 1) * CTRL], grids[(a + 1) * CTRL : (a + 2) * CTRL]], 1)
        for a in range(0, GROUP, 2)
    ]
    turned = product(jnp.concatenate(blocks, 0), pair_ref[...])
    turned = jnp.concatenate([turned[:CTRL], turned[CTRL:]], 1)
    spectral = product(basis_ref[...], turned)
    for pair in range(GROUP // 2):
        out_ref[pair * CTRL : (pair + 1) * CTRL, :] = spectral[:, pair * LANES : (pair + 1) * LANES]


def make_payload(reply, place, far_geom, far_patch, slots, near_grid, const):
    owners, _, capacity = reply.shape
    count = far_geom.shape[1]
    return pl.pallas_call(
        payload_kernel,
        out_shape=(
            jax.ShapeDtypeStruct((1, count), F32),
            jax.ShapeDtypeStruct((PAYLOAD_ROWS, LANES), F32),
        ),
        in_specs=[VMEM] * 2 + [WHOLE] * 2 + [VMEM] * 2 + [WHOLE] * 2,
        out_specs=(VMEM, VMEM),
        scratch_shapes=[pltpu.VMEM((1, owners * capacity), F32)],
        compiler_params=params(24),
        name="make_payload",
    )(
        reply, place, far_geom, far_patch, slots, near_grid,
        const["basis"], const["basis_pair"],
    )


def pair_rows(edge):
    blank = jnp.zeros((8, CTRL), F32)
    return jnp.concatenate([jnp.concatenate([edge, blank], 1), jnp.concatenate([blank, edge], 1)], 0)


def absorb(first_own, y_at, per_owner, items, sums, groups, edge, scale, name_v, name_s, edges, where_to, name_sem):
    patches = groups.shape[1]
    low8 = iota((8, LANES), 1) < CTRL
    at = 0
    for ref, parts, _, _ in items:
        for p in range(parts):
            last = (p + 1) * PAYLOAD_ROWS - 1
            patch = ref[last : last + 1, :].astype(jnp.int32) - first_own
            name_v[at : at + 1, :] = jnp.where((patch >= 0) & (patch < per_owner), patch, -1)
            at += 1
    names = pltpu.make_async_copy(name_v, name_s, name_sem)
    names.start()

    sums[...] = jnp.zeros(sums.shape, F32)
    edge_high, edge_low = halves(edge)
    edge_both = jnp.concatenate([edge_high, edge_low], 0)
    both_high, both_low = halves(pair_rows(edge))
    both_both = jnp.concatenate([both_high, both_low], 0)
    for dy in sorted({dy for _, _, dy, _ in items}):
        at = 0
        chunks = [(ref, p) for ref, parts, own, _ in items if own == dy for p in range(0, parts, 2)]
        for ref, start in chunks:
            blocks = []
            for p in (start, start + 1):
                row = p * PAYLOAD_ROWS
                blocks += [halves(ref[row + q * CTRL : row + (q + 1) * CTRL, :]) for q in range(GROUP // 2)]
                row += GRID_ROWS
                where_to[at + GROUP * (p - start) : at + GROUP * (p - start + 1), :] = ref[row : row + GROUP, :]
            high, low = [jnp.concatenate(x, 1) for x in zip(*blocks)]
            along_rows = nn(edge_both, high)
            along_rows = (along_rows[:8] + along_rows[8:]) + nn(edge_high, low)
            high, low = [jnp.concatenate(x, 0) for x in zip(*blocks)]
            along_cols = nt(both_both, high)
            along_cols = (along_cols[:16] + along_cols[16:]) + nt(both_high, low)
            for s in range(2 * GROUP):
                q = s // 2
                first = along_rows[:, q * LANES : (q + 1) * LANES]
                second = along_cols[8 * (s % 2) : 8 * (s % 2) + 8, q // 2 * LANES : (q // 2 + 1) * LANES]
                if s % 2:
                    first = pltpu.roll(first, CTRL, 1)
                if q % 2 == 0:
                    second = pltpu.roll(second, CTRL, 1)
                edges[8 * at : 8 * at + 8, :] = jnp.where(low8, first, second) * scale
                at += 1
        lane = iota((at, LANES), 1)
        place = jnp.where(lane == where_to[:at, :].astype(jnp.int32), 1.0, 0.0).T[:patches].astype(BF16)
        rows = jnp.concatenate([edges[pl.ds(r, at, stride=8), :] for r in range(6)], 1)
        groups[dy ^ y_at] = fold(nn(place, two(rows)))

    names.wait()

    def add_items(wanted):
        at = 0
        for ref, parts, dy, _ in items:

            def add_payload(p, carry, ref=ref, at=at):
                for s in range(GROUP):
                    patch = name_s[at + p, s]

                    @pl.when(patch >= 0)
                    def _():
                        row = pl.multiple_of(p * PAYLOAD_ROWS + (s // 2) * CTRL, 8)
                        own = pl.multiple_of(patch * CTRL, CTRL)
                        sums[s % 2, pl.ds(own, CTRL), :] = sums[s % 2, pl.ds(own, CTRL), :] + ref[pl.ds(row, CTRL), :]

                return carry

            if dy == wanted:
                lax.fori_loop(0, parts, add_payload, 0)
            at += parts

    @pl.when(y_at == 0)
    def _():
        add_items(0)
        add_items(1)

    @pl.when(y_at != 0)
    def _():
        add_items(1)
        add_items(0)


def smooth_kernel(
    items, per_owner, where_ref, adj_ref, coupling_ref, basis_ref, pair_ref, series_ref, edge_ref, scale_ref, *rest
):
    refs, rest = rest[: len(items)], rest[len(items) :]
    out_ref, sums, groups, halo_all, halo_rows, *scratch = rest
    patches = adj_ref.shape[0]
    first_own = pl.multiple_of(where_ref[0] * per_owner, 8)
    items = [(ref, *item) for ref, item in zip(refs, items)]
    edge = edge_ref[...]
    scale = scale_ref[...]
    if len(items) == 1:
        groups[...] = jnp.zeros(groups.shape, F32)
    absorb(first_own, where_ref[1], per_owner, items, sums, groups, edge, scale, *scratch)
    base = groups[0] + groups[1]
    base = [base[:, 4 * CTRL * k : 4 * CTRL * (k + 1)] for k in range(3)]

    column = iota((patches, patches), 1)
    wide = 4 * CTRL

    def facing(adjacency):
        hits = [
            jnp.where(adjacency[:, s : s + 1] == column[: adjacency.shape[0]], 1.0, 0.0).astype(BF16)
            for s in range(4)
        ]
        return jnp.concatenate([hits[0], hits[2]], 0), jnp.concatenate([hits[1], hits[3]], 0)

    def halo(facing, edges):
        count = facing[0].shape[0] // 2
        low_lane = iota((count, LANES), 1) < CTRL
        first = fold(nn(facing[0], two(edges[:, LANES:])))
        second = fold(nn(facing[1], two(edges[:, :LANES])))
        return jnp.concatenate(
            [jnp.where(low_lane, x[:count], x[count:]) for x in (first, second)], 1
        )

    every = facing(adj_ref[...])
    halo0 = halo(every, base[0])
    effect0 = product(halo0, coupling_ref[...])
    edges1 = base[0] + base[1] + effect0[:, :wide]
    halo1 = halo(every, edges1)
    effect1 = product(halo1, coupling_ref[:, :wide])
    edges2 = base[0] + base[1] + base[2] + effect0[:, wide:] + effect1
    halo2 = halo(facing(adj_ref[pl.ds(first_own, per_owner), :]), edges2)
    halo_all[0] = halo1
    halo_all[1] = halo0
    for k in range(3):
        mine = halo2 if k == 0 else halo_all[k - 1, pl.ds(first_own, per_owner), :]
        factor = SMOOTHING * scale[2 * k : 2 * k + 1]
        for side in range(2):
            halo_rows[pl.ds(2 * k + side, per_owner, stride=8), :] = (
                mine[:, side * LANES : (side + 1) * LANES] * factor
            )
    zero = jnp.zeros((per_owner, LANES), F32)
    for r in (6, 7):
        halo_rows[pl.ds(r, per_owner, stride=8), :] = zero

    pairs = per_owner // 2
    both = pair_rows(edge)
    low8 = iota((8, LANES), 1) < CTRL
    along_rows, along_cols = [], []
    for pair in range(pairs):
        a = halo_rows[16 * pair : 16 * pair + 8, :]
        b = halo_rows[16 * pair + 8 : 16 * pair + 16, :]
        along_rows.append(jnp.where(low8, a, pltpu.roll(b, CTRL, 1)))
        low, high = (pltpu.roll(x, CTRL, 1) for x in (a, b)) if pair % 2 == 0 else (a, b)
        along_cols.append(jnp.concatenate([low, high], 0))
    from_rows = tn_product(edge, jnp.concatenate(along_rows, 1))
    low_half = iota((CTRL, LANES), 1) < CTRL
    basis_both = pair_ref[...]
    low16 = iota((16, LANES), 1) < CTRL
    along_cols = [jnp.where(low16, x, y) for x, y in zip(along_cols[::2], along_cols[1::2])]
    from_cols = tn_product(jnp.concatenate(along_cols, 1), both)
    turned = []
    for pair in range(pairs):
        a, b = [slice(patch * CTRL, (patch + 1) * CTRL) for patch in (2 * pair, 2 * pair + 1)]
        left = sums[0, a, :] + pltpu.roll(sums[1, a, :], CTRL, 1)
        right = pltpu.roll(sums[0, b, :], CTRL, 1) + sums[1, b, :]
        spectral = jnp.where(low_half, left, right) * series_ref[...]
        spectral = spectral + from_rows[:, pair * LANES : (pair + 1) * LANES]
        turned.append(spectral + from_cols[pair * CTRL : (pair + 1) * CTRL, :])
    turned = product(jnp.concatenate(turned, 0), basis_both)
    flat = jnp.concatenate([turned[pair * CTRL : (pair + 1) * CTRL] for pair in range(pairs)], 1)
    done = product(basis_ref[...], flat)
    for pair in range(pairs):
        out_ref[2 * pair] = done[:, pair * LANES : pair * LANES + CTRL]
        out_ref[2 * pair + 1] = done[:, pair * LANES + CTRL : (pair + 1) * LANES]


def tn_product(x, y):
    x_high, x_low = halves(x)
    y_high, y_low = halves(y)
    return tn(x_high, y_high) + (tn(x_low, y_high) + tn(x_high, y_low))


def smooth(payloads, items, where, adjacency, per_owner, const):
    patches = adjacency.shape[0]
    total = sum(item[0] for item in items)
    return pl.pallas_call(
        functools.partial(smooth_kernel, items, per_owner),
        out_shape=jax.ShapeDtypeStruct((per_owner, CTRL, CTRL), F32),
        in_specs=[SMEM] + [WHOLE] * 7 + [VMEM] * len(payloads),
        out_specs=VMEM,
        scratch_shapes=[
            pltpu.VMEM((2, per_owner * CTRL, LANES), F32),
            pltpu.VMEM((2, patches, 12 * CTRL), F32),
            pltpu.VMEM((2, patches, 4 * CTRL), F32),
            pltpu.VMEM((per_owner * 8, LANES), F32),
            pltpu.VMEM((total, LANES), jnp.int32),
            pltpu.SMEM((total, LANES), jnp.int32),
            pltpu.VMEM((total * GROUP * 8, LANES), F32),
            pltpu.VMEM((total * GROUP, LANES), F32),
            pltpu.SemaphoreType.DMA,
        ],
        compiler_params=params(32),
        name="smooth",
    )(
        where, adjacency, const["coupling"], const["basis"], const["basis_pair"], const["series"],
        const["edge_rows"], const["scale_rows"], *payloads,
    )


def join_kernel(where_ref, *refs):
    *parts, out_ref, sem = refs
    copies = []
    for k, part in enumerate(parts):
        at = pl.multiple_of((where_ref[2] // 2 ^ k) * PAYLOAD_ROWS, 8)
        copies.append(pltpu.make_async_copy(part, out_ref.at[pl.ds(at, PAYLOAD_ROWS)], sem.at[k]))
        copies[-1].start()
    for copy in copies:
        copy.wait()


def join(parts, where):
    return pl.pallas_call(
        join_kernel,
        out_shape=jax.ShapeDtypeStruct((len(parts) * PAYLOAD_ROWS, LANES), F32),
        in_specs=[SMEM] + [VMEM] * len(parts),
        out_specs=VMEM,
        scratch_shapes=[pltpu.SemaphoreType.DMA((len(parts),))],
        compiler_params=params(16),
        name="join",
    )(where, *parts)


def gather_and_smooth(payload, adjacency, vol_count, dsg_count, const):
    patches = adjacency.shape[0]
    per_owner = patches // dsg_count
    y_at = lax.axis_index("vol") % 2 if (vol_count, dsg_count) == (8, 4) else 0
    where = jnp.stack([lax.axis_index("dsg"), y_at, lax.axis_index("vol")]).astype(jnp.int32)
    if vol_count != 8 or dsg_count != 4:
        whole = lax.all_gather(payload, ("vol", "dsg"), axis=0, tiled=True)
        items = ((vol_count * dsg_count, 0, 0),)
        return smooth([whole], items, where, adjacency, per_owner, const)

    def over(axis, array, bit):
        count = vol_count if axis == "vol" else dsg_count
        return lax.ppermute(array, axis, [(i, i ^ bit) for i in range(count)])

    here = join([payload] + [over("vol", payload, 2 * k) for k in (1, 2, 3)], where)
    half = here.shape[0] // 2
    beside_y = over("vol", here, 1)
    beside_x = over("dsg", here, 2)
    corner = [over("dsg", beside_y[:half], 2), over("vol", beside_x[half:], 1)]
    arrays = [here, beside_x, beside_y]
    arrays = [x for array in arrays for x in (array, over("dsg", array, 1))]
    arrays += corner + [over("dsg", c, 1) for c in corner]
    items = ((4, 0, 0), (4, 0, 0), (4, 0, 1), (4, 0, 1), (4, 1, 0), (4, 1, 0)) + ((2, 1, 1),) * 4
    return smooth(arrays, items, where, adjacency, per_owner, const)


def per_device(
    fields, far_geom, far_block, far_cell, far_patch, near_geom, near_cell, near_patch, adjacency
):
    vol_count, dsg_count = lax.axis_size("vol"), lax.axis_size("dsg")
    far_count = far_cell.shape[0]
    capacity = 5 * far_count // (2 * vol_count)
    const = {name: jnp.asarray(value) for name, value in constants().items()}

    request, place = pack_requests(
        far_geom, far_block.reshape(1, -1), far_cell.reshape(1, -1), vol_count, capacity
    )
    asked = lax.all_to_all(request, "vol", split_axis=0, concat_axis=0, tiled=True)
    near_dens = near_densities(near_cell, fields, near_geom, near_cell.shape[0] // 2)
    asked, near_dens = lax.optimization_barrier((asked, near_dens))
    answer = far_answers(asked, fields)
    reply = lax.all_to_all(answer, "vol", split_axis=0, concat_axis=0, tiled=True)
    near_patch, far_patch = near_patch.reshape(1, -1), far_patch.reshape(1, -1)
    near_grid, slots = near_grids(near_dens, near_cell, fields, near_geom, near_patch, far_patch)
    far_dens, payload = make_payload(reply, place, far_geom, far_patch, slots, near_grid, const)

    design = gather_and_smooth(payload, adjacency, vol_count, dsg_count, const)
    return far_dens.reshape(-1), design


def solution(mesh):
    return jax.shard_map(
        per_device,
        mesh=mesh,
        in_specs=(
            P("vol", None),
            P(None, ("vol", "dsg")),
            P(("vol", "dsg"), None),
            P(("vol", "dsg")),
            P(("vol", "dsg")),
            P(None, ("vol", "dsg")),
            P(("vol", "dsg")),
            P(("vol", "dsg")),
            P(),
        ),
        out_specs=(P(("vol", "dsg")), P("dsg", None, None)),
        check_vma=False,
    )
```

```python
import functools

import jax
import jax.numpy as jnp
import numpy as np
from jax import lax
from jax.experimental import pallas as pl
from jax.experimental.pallas import tpu as pltpu
from jax.sharding import PartitionSpec as P

CTRL = 64
GROUP = 4
LANES = 128
PENALTY = 4.0
SMOOTHING = 16.0
NO_PATCH = 1.0e6
GRID_ROWS = GROUP // 2 * CTRL
PAYLOAD_ROWS = GRID_ROWS + 2 * GROUP
LINES = 4
CHUNKS = 3
NEAR_ROWS = PAYLOAD_ROWS + 4 * LINES
F32 = jnp.float32
BF16 = jnp.bfloat16
EXACT = lax.Precision.HIGHEST
VMEM = pl.BlockSpec(memory_space=pltpu.VMEM)
SMEM = pl.BlockSpec(memory_space=pltpu.SMEM)
ANY = pl.BlockSpec(memory_space=pl.ANY)
WHOLE = pl.BlockSpec()
HBM = pl.BlockSpec(memory_space=pltpu.HBM)


def params(megabytes):
    return pltpu.CompilerParams(vmem_limit_bytes=megabytes << 20)


def constants():
    order = np.arange(1, CTRL + 1)
    basis = np.sqrt(2.0 / (CTRL + 1)) * np.sin(np.pi * np.outer(order, order) / (CTRL + 1))
    eigen = 1.0 + SMOOTHING * (2.0 - 2.0 * np.cos(np.pi * order / (CTRL + 1)))
    damp = 1.0 / eigen
    keep = 1.0 - damp
    powers = [keep**k * damp for k in range(3)]
    ends = [basis[:, 0], basis[:, CTRL - 1]]
    edge_rows = np.zeros((8, CTRL))
    scale_rows = np.zeros((8, CTRL))
    for k in range(3):
        for side in range(2):
            edge_rows[2 * k + side] = powers[k] * ends[side]
            scale_rows[2 * k + side] = powers[k]
    series = sum(np.outer(keep**k * damp, keep**k * damp) for k in range(4))

    def coupling(k):
        f = powers[k]
        lane = [0, 2, 1, 3]
        out = np.zeros((4 * CTRL, 4 * CTRL))
        for a, side_in in enumerate(lane):
            for b, side_out in enumerate(lane):
                q_in, q_out = ends[side_in % 2], ends[side_out % 2]
                if side_in // 2 == side_out // 2:
                    block = np.diag(f * np.sum(q_in * q_out * f))
                else:
                    block = np.outer(q_out * f, q_in * f)
                out[a * CTRL : (a + 1) * CTRL, b * CTRL : (b + 1) * CTRL] = SMOOTHING * block
        return out

    return dict(
        basis=np.float32(basis),
        basis_pair=np.float32(np.kron(np.eye(2), basis)),
        edge_rows=np.float32(edge_rows),
        scale_rows=np.float32(np.concatenate([scale_rows, scale_rows], 1)),
        series=np.float32(np.concatenate([series, series], 1)),
        coupling=np.float32(np.concatenate([coupling(0), coupling(1)], 1)),
    )


def split3(x):
    high = x.astype(BF16).astype(F32)
    rest = x - high
    mid = rest.astype(BF16).astype(F32)
    return high, mid, rest - mid


def nt(a, b, **kw):
    return lax.dot_general(a, b, (((1,), (1,)), ((), ())), preferred_element_type=F32, **kw)


def nn(a, b, **kw):
    return lax.dot_general(a, b, (((1,), (0,)), ((), ())), preferred_element_type=F32, **kw)


def tn(a, b, **kw):
    return lax.dot_general(a, b, (((0,), (0,)), ((), ())), preferred_element_type=F32, **kw)


def iota(shape, axis):
    return lax.broadcasted_iota(jnp.int32, shape, axis)


def halves(x):
    high = x.astype(BF16)
    return high, (x - high.astype(F32)).astype(BF16)


def two(x):
    return jnp.concatenate(halves(x), 1)


def fold(x):
    half = x.shape[1] // 2
    return x[:, :half] + x[:, half:]


def product(x, y):
    x_high, x_low = halves(x)
    y_high, y_low = halves(y)
    return nn(x_high, y_high) + (nn(x_low, y_high) + nn(x_high, y_low))


def nt_product(x, y):
    x_high, x_low = halves(x)
    y_high, y_low = halves(y)
    return nt(x_high, y_high) + (nt(x_low, y_high) + nt(x_high, y_low))


def fetch(pairs, sem):
    copies = [pltpu.make_async_copy(a, b, sem.at[i]) for i, (a, b) in enumerate(pairs)]
    for copy in copies:
        copy.start()
    for copy in copies:
        copy.wait()


def pack_kernel(capacity, geom_in, block_in, cell_in, request_ref, place_ref, geom_ref, block_ref, cell_ref, sem):
    fetch([(geom_in, geom_ref), (block_in, block_ref), (cell_in, cell_ref)], sem)
    owners = request_ref.shape[0]
    count = geom_ref.shape[1]
    block = block_ref[...]
    owner_id = iota((owners, count), 0)
    chosen = jnp.where(owner_id == block, 1.0, 0.0).astype(F32)
    earlier = jnp.where(iota((count, count), 0) < iota((count, count), 1), 1.0, 0.0).astype(BF16)
    rank = nn(chosen.astype(BF16), earlier)
    place = jnp.sum(chosen * (rank + (capacity * owner_id).astype(F32)), axis=0, keepdims=True)
    place = place.astype(jnp.int32)
    place_ref[...] = place
    row = iota((8, count), 0)
    number = (iota((8, count), 1) + 1).astype(F32)
    values = jnp.where(row < 6, geom_ref[...], jnp.where(row == 6, cell_ref[...].astype(F32), number))
    high, mid, low = split3(values)
    parts = jnp.concatenate([high, mid, low], 0).astype(BF16)
    put = jnp.where(iota((owners * capacity, count), 0) == place, 1.0, 0.0).astype(BF16)
    packed = nt(parts, put)
    packed = (packed[16:24] + packed[8:16]) + packed[0:8]
    for owner in range(owners):
        request_ref[owner] = packed[:, owner * capacity : (owner + 1) * capacity]


def pack_requests(far_geom, far_block, far_cell, owners, capacity):
    count = far_geom.shape[1]
    return pl.pallas_call(
        functools.partial(pack_kernel, capacity),
        out_shape=(
            jax.ShapeDtypeStruct((owners, 8, capacity), F32),
            jax.ShapeDtypeStruct((1, count), jnp.int32),
        ),
        in_specs=[HBM] * 3,
        out_specs=(VMEM, VMEM),
        scratch_shapes=[
            pltpu.VMEM((8, count), F32),
            pltpu.VMEM((1, count), jnp.int32),
            pltpu.VMEM((1, count), jnp.int32),
            pltpu.SemaphoreType.DMA((3,)),
        ],
        compiler_params=params(60),
        name="pack_requests",
    )(far_geom, far_block, far_cell)


def gather_rows(cells, fields_ref, rows_ref, count):
    unroll = 32

    def step(i, carry):
        for u in range(unroll):
            p = i * unroll + u
            rows_ref[pl.ds(p, 1), :] = fields_ref[pl.ds(cells(p), 1), :]
        return carry

    lax.fori_loop(0, count // unroll, step, 0)


def bernstein(t):
    u = 1.0 - t
    uu, tt = u * u, t * t
    values = [uu * u, 3.0 * t * uu, 3.0 * tt * u, tt * t]
    tu = 6.0 * t * u
    slopes = [-3.0 * uu, 3.0 * uu - tu, tu - 3.0 * tt, 3.0 * tt]
    return values, slopes


def tile_density(columns, geom):
    row = iota((8, LANES), 0)
    wide = [jnp.broadcast_to(geom[r : r + 1], (8, LANES)) for r in range(3)]
    x_val, x_der = bernstein(wide[0])
    y_val, y_der = bernstein(wide[1])
    z_val, z_der = bernstein(wide[2])
    k = row % 4

    def by_k(v):
        return jnp.where(k == 0, v[0], jnp.where(k == 1, v[1], jnp.where(k == 2, v[2], v[3])))

    def by_j(v, m):
        return jnp.where(row < 4, v[2 * m], v[2 * m + 1])

    z_v, z_d = by_k(z_val), by_k(z_der)
    yz = [by_j(y_val, m) * z_v for m in range(2)]
    dyz = [by_j(y_der, m) * z_v for m in range(2)]
    ydz = [by_j(y_val, m) * z_d for m in range(2)]
    sums = []
    for half in range(2):
        total = [None] * 4
        for i in range(4):
            at = half * 64 + i * 16
            first, second = columns[at : at + 8], columns[at + 8 : at + 16]
            plain = first * yz[0] + second * yz[1]
            along_y = first * dyz[0] + second * dyz[1]
            along_z = first * ydz[0] + second * ydz[1]
            terms = [x_val[i] * plain, x_der[i] * plain, x_val[i] * along_y, x_val[i] * along_z]
            total = [t if s is None else s + t for s, t in zip(total, terms)]
        sums.append([jnp.sum(t, axis=0, keepdims=True) for t in total])
    state, adjoint = sums
    n = [geom[3 + r : 4 + r] for r in range(3)]
    normal_sq = n[0] * n[0] + n[1] * n[1] + n[2] * n[2]
    inner = state[1] * adjoint[1] + state[2] * adjoint[2] + state[3] * adjoint[3]
    along_s = state[1] * n[0] + state[2] * n[1] + state[3] * n[2]
    along_a = adjoint[1] * n[0] + adjoint[2] * n[1] + adjoint[3] * n[2]
    return normal_sq * inner - 2.0 * along_s * along_a + PENALTY * normal_sq * state[0] * adjoint[0]


def densities(rows_ref, geom_ref, out_ref, count):
    def step(tile, carry):
        at = pl.multiple_of(tile * LANES, LANES)
        columns = rows_ref[pl.ds(at, LANES), :].T
        out_ref[:, pl.ds(at, LANES)] = tile_density(columns, geom_ref[:, pl.ds(at, LANES)])
        return carry

    tiles = count // LANES
    lax.fori_loop(0, tiles, step, 0, unroll=4 if tiles % 4 == 0 else 2)


def near_kernel(first, cell_in, fields_in, geom_in, out_ref, cell_ref, fields_ref, geom_ref, rows_ref, sem):
    count = out_ref.shape[1]
    part = pl.ds(first, count)
    fetch([(cell_in.at[part], cell_ref), (geom_in.at[:, part], geom_ref), (fields_in, fields_ref)], sem)
    gather_rows(lambda p: cell_ref[p], fields_ref, rows_ref, count)
    densities(rows_ref, geom_ref, out_ref, count)


def far_densities(request_in, fields_ref, request_ref, query_ref, cell_v, cell_s, rows_ref, dens_ref, sems, sem):
    owners, _, capacity = request_in.shape
    count = owners * capacity
    fetch([(request_in, request_ref)], sems)
    for o in range(owners):
        query_ref[:, o * capacity : (o + 1) * capacity] = request_ref[o]
    cell_v[...] = query_ref[6:7, :].astype(jnp.int32)
    copy = pltpu.make_async_copy(cell_v, cell_s, sem)
    copy.start()
    copy.wait()
    gather_rows(lambda p: cell_s[0, p], fields_ref, rows_ref, count)
    densities(rows_ref, query_ref, dens_ref, count)


def far_kernel(request_in, fields_ref, out_ref, *scratch):
    owners, _, capacity = request_in.shape
    far_densities(request_in, fields_ref, *scratch)
    dens_ref = scratch[5]
    for o in range(owners):
        out_ref[o] = dens_ref[:, o * capacity : (o + 1) * capacity]


def in_rows(x):
    return jnp.concatenate([x[:, i : i + LANES] for i in range(0, x.shape[1], LANES)], 0)


def in_line(x):
    return jnp.concatenate([x[i : i + 1, :] for i in range(x.shape[0])], 1)


def far_spread_kernel(request_in, fields_ref, out_ref, *scratch):
    owners, _, capacity = request_in.shape
    far_densities(request_in, fields_ref, *scratch)
    query_ref, dens_ref = scratch[1], scratch[5]
    number = iota((LINES * LANES, capacity), 0) + 1
    found = []
    for o in range(owners):
        part = slice(o * capacity, (o + 1) * capacity)
        place = jnp.where(number == query_ref[7:8, part].astype(jnp.int32), 1.0, 0.0).astype(BF16)
        high, mid, low = split3(dens_ref[:, part])
        parts = jnp.concatenate([high, mid, low, jnp.zeros((5, capacity), F32)], 0).astype(BF16)
        got = nt(parts, place)
        found.append(in_rows((got[2:3] + got[1:2]) + got[0:1]))
    lines = [jnp.concatenate(found[y::2], 0) for y in range(2)]
    for o in range(owners):
        out_ref[o] = lines[o % 2]


def far_scratch(requests):
    owners, _, capacity = requests.shape
    count = owners * capacity
    return [
        pltpu.VMEM(requests.shape, F32),
        pltpu.VMEM((8, count), F32),
        pltpu.VMEM((1, count), jnp.int32),
        pltpu.SMEM((1, count), jnp.int32),
        pltpu.VMEM((count, LANES), F32),
        pltpu.VMEM((1, count), F32),
        pltpu.SemaphoreType.DMA((1,)),
        pltpu.SemaphoreType.DMA,
    ]


def far_answers(requests, fields):
    owners, _, capacity = requests.shape
    return pl.pallas_call(
        far_kernel,
        out_shape=jax.ShapeDtypeStruct((owners, 1, capacity), F32),
        in_specs=[ANY, VMEM],
        out_specs=VMEM,
        scratch_shapes=far_scratch(requests),
        compiler_params=params(24),
        name="far_answers",
    )(requests, fields)


def far_spread(requests, fields):
    owners = requests.shape[0]
    return pl.pallas_call(
        far_spread_kernel,
        out_shape=jax.ShapeDtypeStruct((owners, owners // 2 * LINES, LANES), F32),
        in_specs=[ANY, VMEM],
        out_specs=VMEM,
        scratch_shapes=far_scratch(requests),
        compiler_params=params(24),
        cost_estimate=pl.CostEstimate(flops=40_000_000, bytes_accessed=4_000_000, transcendentals=0),
        name="far_spread",
    )(requests, fields)


def spline_weights(param):
    scaled = param * float(CTRL - 3)
    start = jnp.clip(jnp.floor(scaled), 0.0, float(CTRL - 4))
    x = scaled - start
    u = 1.0 - x
    cubed, squared = x * x * x, x * x
    weights = [
        u * u * u * (1.0 / 6.0),
        (3.0 * cubed - 6.0 * squared + 4.0) * (1.0 / 6.0),
        (-3.0 * cubed + 3.0 * squared + 3.0 * x + 1.0) * (1.0 / 6.0),
        cubed * (1.0 / 6.0),
    ]
    return start.astype(jnp.int32), weights


def spline_columns(start, weights):
    off = iota((CTRL, start.shape[1]), 0) - start
    out = jnp.zeros(off.shape, F32)
    for m in range(4):
        out = jnp.where(off == m, weights[m], out)
    return out


def slot_grids(density, s, t, patch, slots):
    start, weights = spline_weights(t)
    right = spline_columns(start, [w * density for w in weights])
    return grids_of(spline_columns(*spline_weights(s)), right, patch, slots)


def grids_of(left, right, patch, slots):
    left_high, left_low = halves(left)
    right_high, right_low = halves(right)
    masks = [jnp.where(patch == slot, 1.0, 0.0).astype(BF16) for slot in slots]
    high = jnp.concatenate([left_high * m for m in masks], 0)
    low = jnp.concatenate([left_low * m for m in masks], 0)
    return fold(nt(high, jnp.concatenate([right_high, right_low], 0))) + nt(low, right_high)


def side_by_side(grids):
    return [
        jnp.concatenate([grids[a * CTRL : (a + 1) * CTRL], grids[(a + 1) * CTRL : (a + 2) * CTRL]], 1)
        for a in range(0, GROUP, 2)
    ]


def near_payload_kernel(
    cell_in, fields_in, geom_in, near_in, far_in, far_geom_in, out_ref, slot_ref,
    near_ref, far_ref, far_geom_ref, dens_ref, cell_ref, fields_ref, geom_ref, rows_ref, more, sem,
):
    others = [(near_in, near_ref), (far_in, far_ref), (far_geom_in, far_geom_ref)]
    others = [pltpu.make_async_copy(a, b, more.at[i]) for i, (a, b) in enumerate(others)]
    for copy in others:
        copy.start()
    near_kernel(0, cell_in, fields_in, geom_in, dens_ref, cell_ref, fields_ref, geom_ref, rows_ref, sem)
    for copy in others:
        copy.wait()
    near, far = near_ref[...].astype(F32), far_ref[...].astype(F32)
    slots = []
    last = jnp.full((1, 1), -1.0, F32)
    for _ in range(GROUP):
        a = jnp.min(jnp.where(near > last, near, NO_PATCH), axis=1, keepdims=True)
        b = jnp.min(jnp.where(far > last, far, NO_PATCH), axis=1, keepdims=True)
        last = jnp.minimum(a, b)
        slots.append(last)
    grids = slot_grids(dens_ref[...], geom_ref[6:7, :], geom_ref[7:8, :], near, slots)
    lane = iota((1, LANES), 1)
    names = jnp.zeros((1, LANES), F32)
    for s in range(GROUP):
        names = jnp.where(lane == s, slots[s], names)
    slots = [jnp.broadcast_to(s, (1, LANES)) for s in slots]
    slot_ref[...] = jnp.concatenate(slots + slots, 0)
    out_ref[0:PAYLOAD_ROWS, :] = jnp.concatenate(side_by_side(grids) + slots + [names] * GROUP, 0)
    if out_ref.shape[0] > PAYLOAD_ROWS:
        held = [in_rows(x) for x in (far_geom_ref[6:7, :], far_geom_ref[7:8, :], far)]
        out_ref[PAYLOAD_ROWS:, :] = jnp.concatenate(held + [jnp.zeros((LINES, LANES), F32)], 0)


def near_payload(near_cell, fields, near_geom, near_patch, far_patch, far_geom, rows):
    count = near_geom.shape[1]
    return pl.pallas_call(
        near_payload_kernel,
        out_shape=(
            jax.ShapeDtypeStruct((rows, LANES), F32),
            jax.ShapeDtypeStruct((8, LANES), F32),
        ),
        in_specs=[HBM] * 6,
        out_specs=(VMEM, VMEM),
        scratch_shapes=[
            pltpu.VMEM(near_patch.shape, jnp.int32),
            pltpu.VMEM(far_patch.shape, jnp.int32),
            pltpu.VMEM(far_geom.shape, F32),
            pltpu.VMEM((1, count), F32),
            pltpu.SMEM((count,), jnp.int32),
            pltpu.VMEM(fields.shape, F32),
            pltpu.VMEM((8, count), F32),
            pltpu.VMEM((count, LANES), F32),
            pltpu.SemaphoreType.DMA((3,)),
            pltpu.SemaphoreType.DMA((3,)),
        ],
        compiler_params=params(60),
        cost_estimate=pl.CostEstimate(flops=100_000_000, bytes_accessed=4_000_000, transcendentals=0),
        name="near_payload",
    )(near_cell, fields, near_geom, near_patch, far_patch, far_geom)


def to_spectral(blocks, basis, basis_pair):
    turned = product(blocks, basis_pair)
    parts = range(0, blocks.shape[0], CTRL)
    turned = product(basis, jnp.concatenate([turned[at : at + CTRL] for at in parts], 1))
    return jnp.concatenate([turned[:, 2 * at : 2 * at + LANES] for at in parts], 0)


def payload_kernel(
    reply_ref, place_ref, geom_ref, far_ref, slot_ref, near_ref, basis_ref, pair_ref, dens_ref, out_ref, flat_ref
):
    owners, _, capacity = reply_ref.shape
    count = geom_ref.shape[1]
    for o in range(owners):
        flat_ref[:, o * capacity : (o + 1) * capacity] = reply_ref[o]
    high, mid, low = split3(flat_ref[...])
    parts = jnp.concatenate([high, mid, low, jnp.zeros((5, owners * capacity), F32)], 0).astype(BF16)
    put = jnp.where(iota((owners * capacity, count), 0) == place_ref[...], 1.0, 0.0).astype(BF16)
    got = nn(parts, put)
    dens = (got[2:3] + got[1:2]) + got[0:1]
    dens_ref[...] = dens
    slots = [slot_ref[s : s + 1, 0:1] for s in range(GROUP)]
    grids = slot_grids(dens, geom_ref[6:7, :], geom_ref[7:8, :], far_ref[...].astype(F32), slots)
    out_ref[GRID_ROWS:PAYLOAD_ROWS, :] = near_ref[GRID_ROWS:PAYLOAD_ROWS, :]
    blocks = near_ref[0:GRID_ROWS, :] + jnp.concatenate(side_by_side(grids), 0)
    out_ref[0:GRID_ROWS, :] = to_spectral(blocks, basis_ref[...], pair_ref[...])


def make_payload(reply, place, far_geom, far_patch, slots, near, const):
    owners, _, capacity = reply.shape
    count = far_geom.shape[1]
    return pl.pallas_call(
        payload_kernel,
        out_shape=(
            jax.ShapeDtypeStruct((1, count), F32),
            jax.ShapeDtypeStruct((PAYLOAD_ROWS, LANES), F32),
        ),
        in_specs=[VMEM] * 6 + [WHOLE] * 2,
        out_specs=(VMEM, VMEM),
        scratch_shapes=[pltpu.VMEM((1, owners * capacity), F32)],
        compiler_params=params(24),
        name="make_payload",
    )(reply, place, far_geom, far_patch, slots, near, const["basis"], const["basis_pair"])


def pair_rows(edge):
    blank = jnp.zeros((8, CTRL), F32)
    return jnp.concatenate([jnp.concatenate([edge, blank], 1), jnp.concatenate([blank, edge], 1)], 0)


def absorb(first_own, y_at, per_owner, items, sums, groups, edge, scale, name_v, name_s, edges, where_to, name_sem):
    patches = groups.shape[1]
    low8 = iota((8, LANES), 1) < CTRL
    spare = per_owner + iota((1, LANES), 1) // 2 % 2
    at = 0
    for ref, parts, _, _ in items:
        for p in range(parts):
            last = (p + 1) * PAYLOAD_ROWS - 1
            patch = ref[last : last + 1, :].astype(jnp.int32) - first_own
            name_v[at : at + 1, :] = jnp.where((patch >= 0) & (patch < per_owner), patch, spare)
            at += 1
    names = pltpu.make_async_copy(name_v, name_s, name_sem)
    names.start()

    sums[...] = jnp.zeros(sums.shape, F32)
    edge_high, edge_low = halves(edge)
    edge_both = jnp.concatenate([edge_high, edge_low], 0)
    both_high, both_low = halves(pair_rows(edge))
    both_both = jnp.concatenate([both_high, both_low], 0)
    for dy in sorted({dy for _, _, dy, _ in items}):
        at = 0
        chunks = [(ref, p) for ref, parts, own, _ in items if own == dy for p in range(0, parts, 2)]
        for ref, start in chunks:
            blocks = []
            for p in (start, start + 1):
                row = p * PAYLOAD_ROWS
                blocks += [halves(ref[row + q * CTRL : row + (q + 1) * CTRL, :]) for q in range(GROUP // 2)]
                row += GRID_ROWS
                where_to[at + GROUP * (p - start) : at + GROUP * (p - start + 1), :] = ref[row : row + GROUP, :]
            high, low = [jnp.concatenate(x, 1) for x in zip(*blocks)]
            along_rows = nn(edge_both, high)
            along_rows = (along_rows[:8] + along_rows[8:]) + nn(edge_high, low)
            high, low = [jnp.concatenate(x, 0) for x in zip(*blocks)]
            along_cols = nt(both_both, high)
            along_cols = (along_cols[:16] + along_cols[16:]) + nt(both_high, low)
            for s in range(2 * GROUP):
                q = s // 2
                first = along_rows[:, q * LANES : (q + 1) * LANES]
                second = along_cols[8 * (s % 2) : 8 * (s % 2) + 8, q // 2 * LANES : (q // 2 + 1) * LANES]
                if s % 2:
                    first = pltpu.roll(first, CTRL, 1)
                if q % 2 == 0:
                    second = pltpu.roll(second, CTRL, 1)
                edges[8 * at : 8 * at + 8, :] = jnp.where(low8, first, second) * scale
                at += 1
        lane = iota((at, LANES), 1)
        place = jnp.where(lane == where_to[:at, :].astype(jnp.int32), 1.0, 0.0).T[:patches].astype(BF16)
        rows = jnp.concatenate([edges[pl.ds(r, at, stride=8), :] for r in range(6)], 1)
        groups[dy ^ y_at] = fold(nn(place, two(rows)))

    names.wait()

    def add_items(wanted):
        at = 0
        for ref, parts, dy, _ in items:

            def add_payload(p, carry, ref=ref, at=at):
                places = [pl.ds(pl.multiple_of(name_s[at + p, s] * CTRL, CTRL), CTRL) for s in range(GROUP)]
                first = pl.multiple_of(p * PAYLOAD_ROWS, 8)
                blocks = [ref[pl.ds(first + q * CTRL, CTRL), :] for q in range(GROUP // 2)]
                held = [sums[s % 2, places[s], :] + blocks[s // 2] for s in range(GROUP)]
                for s in range(GROUP):
                    sums[s % 2, places[s], :] = held[s]
                return carry

            if dy == wanted:
                lax.fori_loop(0, parts, add_payload, 0, unroll=2)
            at += parts

    @pl.when(y_at == 0)
    def _():
        add_items(0)
        add_items(1)

    @pl.when(y_at != 0)
    def _():
        add_items(1)
        add_items(0)


def smooth_kernel(
    items, per_owner, where_ref, adj_ref, coupling_ref, basis_ref, pair_ref, series_ref, edge_ref, scale_ref, *rest
):
    refs, rest = rest[: len(items)], rest[len(items) :]
    out_ref, sums, groups, halo_all, halo_rows, out_v, out_sem, *scratch = rest
    patches = adj_ref.shape[0]
    first_own = pl.multiple_of(where_ref[0] * per_owner, 8)
    items = [(ref, *item) for ref, item in zip(refs, items)]
    edge = edge_ref[...]
    scale = scale_ref[...]
    if len(items) == 1:
        groups[...] = jnp.zeros(groups.shape, F32)
    absorb(first_own, where_ref[1], per_owner, items, sums, groups, edge, scale, *scratch)
    base = groups[0] + groups[1]
    base = [base[:, 4 * CTRL * k : 4 * CTRL * (k + 1)] for k in range(3)]

    column = iota((patches, patches), 1)
    wide = 4 * CTRL

    def facing(adjacency):
        hits = [
            jnp.where(adjacency[:, s : s + 1] == column[: adjacency.shape[0]], 1.0, 0.0).astype(BF16)
            for s in range(4)
        ]
        return jnp.concatenate([hits[0], hits[2]], 0), jnp.concatenate([hits[1], hits[3]], 0)

    def halo(facing, edges):
        count = facing[0].shape[0] // 2
        low_lane = iota((count, LANES), 1) < CTRL
        first = fold(nn(facing[0], two(edges[:, LANES:])))
        second = fold(nn(facing[1], two(edges[:, :LANES])))
        return jnp.concatenate(
            [jnp.where(low_lane, x[:count], x[count:]) for x in (first, second)], 1
        )

    every = facing(adj_ref[...])
    halo0 = halo(every, base[0])
    effect0 = product(halo0, coupling_ref[...])
    edges1 = base[0] + base[1] + effect0[:, :wide]
    halo1 = halo(every, edges1)
    effect1 = product(halo1, coupling_ref[:, :wide])
    edges2 = base[0] + base[1] + base[2] + effect0[:, wide:] + effect1
    halo2 = halo(facing(adj_ref[pl.ds(first_own, per_owner), :]), edges2)
    halo_all[0] = halo1
    halo_all[1] = halo0
    for k in range(3):
        mine = halo2 if k == 0 else halo_all[k - 1, pl.ds(first_own, per_owner), :]
        factor = SMOOTHING * scale[2 * k : 2 * k + 1]
        for side in range(2):
            halo_rows[pl.ds(2 * k + side, per_owner, stride=8), :] = (
                mine[:, side * LANES : (side + 1) * LANES] * factor
            )
    zero = jnp.zeros((per_owner, LANES), F32)
    for r in (6, 7):
        halo_rows[pl.ds(r, per_owner, stride=8), :] = zero

    pairs = per_owner // 2
    both = pair_rows(edge)
    low8 = iota((8, LANES), 1) < CTRL
    along_rows, along_cols = [], []
    for pair in range(pairs):
        a = halo_rows[16 * pair : 16 * pair + 8, :]
        b = halo_rows[16 * pair + 8 : 16 * pair + 16, :]
        along_rows.append(jnp.where(low8, a, pltpu.roll(b, CTRL, 1)))
        low, high = (pltpu.roll(x, CTRL, 1) for x in (a, b)) if pair % 2 == 0 else (a, b)
        along_cols.append(jnp.concatenate([low, high], 0))
    from_rows = tn_product(edge, jnp.concatenate(along_rows, 1))
    low_half = iota((CTRL, LANES), 1) < CTRL
    basis_both = pair_ref[...]
    low16 = iota((16, LANES), 1) < CTRL
    along_cols = [jnp.where(low16, x, y) for x, y in zip(along_cols[::2], along_cols[1::2])]
    from_cols = tn_product(jnp.concatenate(along_cols, 1), both)
    step = pairs // CHUNKS if pairs % CHUNKS == 0 else pairs
    stores = []
    for start in range(0, pairs, step):
        turned = []
        for pair in range(start, start + step):
            a, b = [slice(patch * CTRL, (patch + 1) * CTRL) for patch in (2 * pair, 2 * pair + 1)]
            left = sums[0, a, :] + pltpu.roll(sums[1, a, :], CTRL, 1)
            right = pltpu.roll(sums[0, b, :], CTRL, 1) + sums[1, b, :]
            spectral = jnp.where(low_half, left, right) * series_ref[...]
            spectral = spectral + from_rows[:, pair * LANES : (pair + 1) * LANES]
            turned.append(spectral + from_cols[pair * CTRL : (pair + 1) * CTRL, :])
        turned = product(jnp.concatenate(turned, 0), basis_both)
        flat = jnp.concatenate([turned[at : at + CTRL] for at in range(0, step * CTRL, CTRL)], 1)
        done = product(basis_ref[...], flat)
        for pair in range(start, start + step):
            at = (pair - start) * LANES
            out_v[2 * pair] = done[:, at : at + CTRL]
            out_v[2 * pair + 1] = done[:, at + CTRL : at + LANES]
        part = pl.ds(2 * start, 2 * step)
        stores.append(pltpu.make_async_copy(out_v.at[part], out_ref.at[part], out_sem.at[len(stores)]))
        stores[-1].start()
    for store in stores:
        store.wait()


def tn_product(x, y):
    x_high, x_low = halves(x)
    y_high, y_low = halves(y)
    return tn(x_high, y_high) + (tn(x_low, y_high) + tn(x_high, y_low))


def smooth(payloads, items, where, adjacency, per_owner, const):
    patches = adjacency.shape[0]
    total = sum(item[0] for item in items)
    return pl.pallas_call(
        functools.partial(smooth_kernel, items, per_owner),
        out_shape=jax.ShapeDtypeStruct((per_owner, CTRL, CTRL), F32),
        in_specs=[SMEM] + [WHOLE] * 7 + [VMEM] * len(payloads),
        out_specs=HBM,
        scratch_shapes=[
            pltpu.VMEM((2, (per_owner + 2) * CTRL, LANES), F32),
            pltpu.VMEM((2, patches, 12 * CTRL), F32),
            pltpu.VMEM((2, patches, 4 * CTRL), F32),
            pltpu.VMEM((per_owner * 8, LANES), F32),
            pltpu.VMEM((per_owner, CTRL, CTRL), F32),
            pltpu.SemaphoreType.DMA((CHUNKS,)),
            pltpu.VMEM((total, LANES), jnp.int32),
            pltpu.SMEM((total, LANES), jnp.int32),
            pltpu.VMEM((total * GROUP * 8, LANES), F32),
            pltpu.VMEM((total * GROUP, LANES), F32),
            pltpu.SemaphoreType.DMA,
        ],
        compiler_params=params(32),
        name="smooth",
    )(
        where, adjacency, const["coupling"], const["basis"], const["basis_pair"], const["series"],
        const["edge_rows"], const["scale_rows"], *payloads,
    )


def join_kernel(where_ref, spread_ref, basis_ref, pair_ref, *refs):
    *parts, out_ref, own_ref, total_ref, near_ref = refs
    z_at = where_ref[2] // 2
    total = spread_ref[0]
    for o in range(1, spread_ref.shape[0]):
        total = total + spread_ref[o]
    total_ref[...] = total
    own_ref[...] = total_ref[pl.ds(z_at * LINES, LINES), :]
    for k, part in enumerate(parts):
        near_ref[z_at ^ k] = part[...]
    blocks = []
    for z in range(len(parts)):
        part = near_ref.at[z]
        dens = total_ref[z * LINES : (z + 1) * LINES, :]
        s, t, patch = [part[PAYLOAD_ROWS + i * LINES : PAYLOAD_ROWS + (i + 1) * LINES, :] for i in range(3)]
        start_s, weights_s = spline_weights(s)
        start_t, weights_t = spline_weights(t)
        left = spline_columns(in_line(start_s), [in_line(w) for w in weights_s])
        right = spline_columns(in_line(start_t), [in_line(w * dens) for w in weights_t])
        slots = [part[GRID_ROWS + i : GRID_ROWS + i + 1, 0:1] for i in range(GROUP)]
        far = side_by_side(grids_of(left, right, in_line(patch), slots))
        blocks.append(part[0:GRID_ROWS, :] + jnp.concatenate(far, 0))
    blocks = to_spectral(jnp.concatenate(blocks, 0), basis_ref[...], pair_ref[...])
    for z in range(len(parts)):
        at = z * PAYLOAD_ROWS
        out_ref[at : at + GRID_ROWS, :] = blocks[z * GRID_ROWS : (z + 1) * GRID_ROWS]
        out_ref[at + GRID_ROWS : at + PAYLOAD_ROWS, :] = near_ref[z, GRID_ROWS:PAYLOAD_ROWS, :]


def join(parts, spread, where, const):
    return pl.pallas_call(
        join_kernel,
        out_shape=(
            jax.ShapeDtypeStruct((len(parts) * PAYLOAD_ROWS, LANES), F32),
            jax.ShapeDtypeStruct((LINES, LANES), F32),
        ),
        in_specs=[SMEM, VMEM, WHOLE, WHOLE] + [VMEM] * len(parts),
        out_specs=(VMEM, VMEM),
        scratch_shapes=[
            pltpu.VMEM((len(parts) * LINES, LANES), F32),
            pltpu.VMEM((len(parts), NEAR_ROWS, LANES), F32),
        ],
        compiler_params=params(16),
        name="join",
    )(where, spread, const["basis"], const["basis_pair"], *parts)


def over(axis, array, bit):
    count = lax.axis_size(axis)
    return lax.ppermute(array, axis, [(i, i ^ bit) for i in range(count)])


def gather_in_plane(here):
    half = here.shape[0] // 2
    beside_y = over("vol", here, 1)
    beside_x = over("dsg", here, 2)
    corner = [over("dsg", beside_y[:half], 2), over("vol", beside_x[half:], 1)]
    arrays = [here, beside_x, beside_y]
    arrays = [x for array in arrays for x in (array, over("dsg", array, 1))]
    arrays += corner + [over("dsg", c, 1) for c in corner]
    items = ((4, 0, 0), (4, 0, 0), (4, 0, 1), (4, 0, 1), (4, 1, 0), (4, 1, 0)) + ((2, 1, 1),) * 4
    return arrays, items


def per_device(
    fields, far_geom, far_block, far_cell, far_patch, near_geom, near_cell, near_patch, adjacency
):
    vol_count, dsg_count = lax.axis_size("vol"), lax.axis_size("dsg")
    far_count = far_cell.shape[0]
    capacity = 5 * far_count // (2 * vol_count)
    const = {name: jnp.asarray(value) for name, value in constants().items()}

    per_owner = adjacency.shape[0] // dsg_count
    staged = vol_count == 8 and dsg_count == 4 and far_count == LINES * LANES
    vol_at = lax.axis_index("vol")
    where = jnp.stack([lax.axis_index("dsg"), vol_at % 2 if staged else 0, vol_at]).astype(jnp.int32)
    request, place = pack_requests(
        far_geom, far_block.reshape(1, -1), far_cell.reshape(1, -1), vol_count, capacity
    )
    asked = lax.all_to_all(request, "vol", split_axis=0, concat_axis=0, tiled=True)
    near_patch, far_patch = near_patch.reshape(1, -1), far_patch.reshape(1, -1)
    near, slots = near_payload(
        near_cell, fields, near_geom, near_patch, far_patch, far_geom, NEAR_ROWS if staged else PAYLOAD_ROWS
    )
    asked, near, slots = lax.optimization_barrier((asked, near, slots))
    if staged:
        spread = far_spread(asked, fields)
        spread = lax.all_to_all(spread, "vol", split_axis=0, concat_axis=0, tiled=True)
        parts = [near] + [over("vol", near, 2 * k) for k in (1, 2, 3)]
        here, far_dens = join(parts, spread, where, const)
        arrays, items = gather_in_plane(here)
    else:
        reply = lax.all_to_all(far_answers(asked, fields), "vol", split_axis=0, concat_axis=0, tiled=True)
        far_dens, payload = make_payload(reply, place, far_geom, far_patch, slots, near, const)
        arrays = [lax.all_gather(payload, ("vol", "dsg"), axis=0, tiled=True)]
        items = ((vol_count * dsg_count, 0, 0),)
    design = smooth(arrays, items, where, adjacency, per_owner, const)
    return far_dens.reshape(-1), design


def solution(mesh):
    return jax.shard_map(
        per_device,
        mesh=mesh,
        in_specs=(
            P("vol", None),
            P(None, ("vol", "dsg")),
            P(("vol", "dsg"), None),
            P(("vol", "dsg")),
            P(("vol", "dsg")),
            P(None, ("vol", "dsg")),
            P(("vol", "dsg")),
            P(("vol", "dsg")),
            P(),
        ),
        out_specs=(P(("vol", "dsg")), P("dsg", None, None)),
        check_vma=False,
    )
```

```python
import functools

import jax
import jax.numpy as jnp
import numpy as np
from jax import lax
from jax.experimental import pallas as pl
from jax.experimental.pallas import tpu as pltpu
from jax.sharding import PartitionSpec as P

CTRL = 64
GROUP = 4
LANES = 128
PENALTY = 4.0
SMOOTHING = 16.0
NO_PATCH = 1.0e6
GRID_ROWS = GROUP // 2 * CTRL
PAYLOAD_ROWS = GRID_ROWS + 2 * GROUP
LINES = 4
CHUNKS = 3
F32 = jnp.float32
BF16 = jnp.bfloat16
EXACT = lax.Precision.HIGHEST
VMEM = pl.BlockSpec(memory_space=pltpu.VMEM)
SMEM = pl.BlockSpec(memory_space=pltpu.SMEM)
ANY = pl.BlockSpec(memory_space=pl.ANY)
WHOLE = pl.BlockSpec()
HBM = pl.BlockSpec(memory_space=pltpu.HBM)


def params(megabytes):
    return pltpu.CompilerParams(vmem_limit_bytes=megabytes << 20)


def constants():
    order = np.arange(1, CTRL + 1)
    basis = np.sqrt(2.0 / (CTRL + 1)) * np.sin(np.pi * np.outer(order, order) / (CTRL + 1))
    eigen = 1.0 + SMOOTHING * (2.0 - 2.0 * np.cos(np.pi * order / (CTRL + 1)))
    damp = 1.0 / eigen
    keep = 1.0 - damp
    powers = [keep**k * damp for k in range(3)]
    ends = [basis[:, 0], basis[:, CTRL - 1]]
    edge_rows = np.zeros((8, CTRL))
    scale_rows = np.zeros((8, CTRL))
    for k in range(3):
        for side in range(2):
            edge_rows[2 * k + side] = powers[k] * ends[side]
            scale_rows[2 * k + side] = powers[k]
    series = sum(np.outer(keep**k * damp, keep**k * damp) for k in range(4))

    def coupling(k):
        f = powers[k]
        lane = [0, 2, 1, 3]
        out = np.zeros((4 * CTRL, 4 * CTRL))
        for a, side_in in enumerate(lane):
            for b, side_out in enumerate(lane):
                q_in, q_out = ends[side_in % 2], ends[side_out % 2]
                if side_in // 2 == side_out // 2:
                    block = np.diag(f * np.sum(q_in * q_out * f))
                else:
                    block = np.outer(q_out * f, q_in * f)
                out[a * CTRL : (a + 1) * CTRL, b * CTRL : (b + 1) * CTRL] = SMOOTHING * block
        return out

    return dict(
        basis=np.float32(basis),
        basis_pair=np.float32(np.kron(np.eye(2), basis)),
        edge_rows=np.float32(edge_rows),
        scale_rows=np.float32(np.concatenate([scale_rows, scale_rows], 1)),
        series=np.float32(np.concatenate([series, series], 1)),
        coupling=np.float32(np.concatenate([coupling(0), coupling(1)], 1)),
    )


def split3(x):
    high = x.astype(BF16).astype(F32)
    rest = x - high
    mid = rest.astype(BF16).astype(F32)
    return high, mid, rest - mid


def nt(a, b, **kw):
    return lax.dot_general(a, b, (((1,), (1,)), ((), ())), preferred_element_type=F32, **kw)


def nn(a, b, **kw):
    return lax.dot_general(a, b, (((1,), (0,)), ((), ())), preferred_element_type=F32, **kw)


def tn(a, b, **kw):
    return lax.dot_general(a, b, (((0,), (0,)), ((), ())), preferred_element_type=F32, **kw)


def iota(shape, axis):
    return lax.broadcasted_iota(jnp.int32, shape, axis)


def halves(x):
    high = x.astype(BF16)
    return high, (x - high.astype(F32)).astype(BF16)


def two(x):
    return jnp.concatenate(halves(x), 1)


def fold(x):
    half = x.shape[1] // 2
    return x[:, :half] + x[:, half:]


def product(x, y):
    x_high, x_low = halves(x)
    y_high, y_low = halves(y)
    return nn(x_high, y_high) + (nn(x_low, y_high) + nn(x_high, y_low))


def nt_product(x, y):
    x_high, x_low = halves(x)
    y_high, y_low = halves(y)
    return nt(x_high, y_high) + (nt(x_low, y_high) + nt(x_high, y_low))


def fetch(pairs, sem):
    copies = [pltpu.make_async_copy(a, b, sem.at[i]) for i, (a, b) in enumerate(pairs)]
    for copy in copies:
        copy.start()
    for copy in copies:
        copy.wait()


def pack_kernel(
    capacity, geom_in, block_in, cell_in, near_in, far_in, request_ref, place_ref, slot_ref,
    geom_ref, block_ref, cell_ref, near_ref, far_ref, sem,
):
    fetch([(geom_in, geom_ref), (block_in, block_ref), (cell_in, cell_ref), (near_in, near_ref), (far_in, far_ref)], sem)
    near, far = near_ref[...].astype(F32), far_ref[...].astype(F32)
    slots = []
    last = jnp.full((1, 1), -1.0, F32)
    for _ in range(GROUP):
        a = jnp.min(jnp.where(near > last, near, NO_PATCH), axis=1, keepdims=True)
        b = jnp.min(jnp.where(far > last, far, NO_PATCH), axis=1, keepdims=True)
        last = jnp.minimum(a, b)
        slots.append(jnp.broadcast_to(last, (1, LANES)))
    slot_ref[...] = jnp.concatenate(slots + slots, 0)
    owners = request_ref.shape[0]
    count = geom_ref.shape[1]
    block = block_ref[...]
    owner_id = iota((owners, count), 0)
    chosen = jnp.where(owner_id == block, 1.0, 0.0).astype(F32)
    earlier = jnp.where(iota((count, count), 0) < iota((count, count), 1), 1.0, 0.0).astype(BF16)
    rank = nn(chosen.astype(BF16), earlier)
    place = jnp.sum(chosen * (rank + (capacity * owner_id).astype(F32)), axis=0, keepdims=True)
    place = place.astype(jnp.int32)
    place_ref[...] = place
    row = iota((8, count), 0)
    number = (iota((8, count), 1) + 1).astype(F32)
    values = jnp.where(row < 6, geom_ref[...], jnp.where(row == 6, cell_ref[...].astype(F32), number))
    high, mid, low = split3(values)
    parts = jnp.concatenate([high, mid, low], 0).astype(BF16)
    put = jnp.where(iota((owners * capacity, count), 0) == place, 1.0, 0.0).astype(BF16)
    packed = nt(parts, put)
    packed = (packed[16:24] + packed[8:16]) + packed[0:8]
    for owner in range(owners):
        request_ref[owner, 0:8, :] = packed[:, owner * capacity : (owner + 1) * capacity]
    if request_ref.shape[1] > 8:
        own = [in_rows(x) for x in (geom_ref[6:7, :], geom_ref[7:8, :], far)] + [slot_ref[0:GROUP, :]]
        own = jnp.concatenate(own, 0)
        for owner in range(owners):
            request_ref[owner, 8:, 0:LANES] = own
            request_ref[owner, 8:, LANES:] = jnp.zeros((own.shape[0], capacity - LANES), F32)


def pack_requests(far_geom, far_block, far_cell, near_patch, far_patch, owners, capacity, staged):
    count = far_geom.shape[1]
    return pl.pallas_call(
        functools.partial(pack_kernel, capacity),
        out_shape=(
            jax.ShapeDtypeStruct((owners, 8 + staged * (3 * LINES + GROUP), capacity), F32),
            jax.ShapeDtypeStruct((1, count), jnp.int32),
            jax.ShapeDtypeStruct((8, LANES), F32),
        ),
        in_specs=[HBM] * 5,
        out_specs=(VMEM, VMEM, VMEM),
        scratch_shapes=[
            pltpu.VMEM((8, count), F32),
            pltpu.VMEM((1, count), jnp.int32),
            pltpu.VMEM((1, count), jnp.int32),
            pltpu.VMEM(near_patch.shape, jnp.int32),
            pltpu.VMEM(far_patch.shape, jnp.int32),
            pltpu.SemaphoreType.DMA((5,)),
        ],
        compiler_params=params(60),
        name="pack_requests",
    )(far_geom, far_block, far_cell, near_patch, far_patch)


def gather_rows(cells, fields_ref, rows_ref, count):
    unroll = 32

    def step(i, carry):
        for u in range(unroll):
            p = i * unroll + u
            rows_ref[pl.ds(p, 1), :] = fields_ref[pl.ds(cells(p), 1), :]
        return carry

    lax.fori_loop(0, count // unroll, step, 0)


def bernstein(t):
    u = 1.0 - t
    uu, tt = u * u, t * t
    values = [uu * u, 3.0 * t * uu, 3.0 * tt * u, tt * t]
    tu = 6.0 * t * u
    slopes = [-3.0 * uu, 3.0 * uu - tu, tu - 3.0 * tt, 3.0 * tt]
    return values, slopes


def tile_density(columns, geom):
    row = iota((8, LANES), 0)
    wide = [jnp.broadcast_to(geom[r : r + 1], (8, LANES)) for r in range(3)]
    x_val, x_der = bernstein(wide[0])
    y_val, y_der = bernstein(wide[1])
    z_val, z_der = bernstein(wide[2])
    k = row % 4

    def by_k(v):
        return jnp.where(k == 0, v[0], jnp.where(k == 1, v[1], jnp.where(k == 2, v[2], v[3])))

    def by_j(v, m):
        return jnp.where(row < 4, v[2 * m], v[2 * m + 1])

    z_v, z_d = by_k(z_val), by_k(z_der)
    yz = [by_j(y_val, m) * z_v for m in range(2)]
    dyz = [by_j(y_der, m) * z_v for m in range(2)]
    ydz = [by_j(y_val, m) * z_d for m in range(2)]
    sums = []
    for half in range(2):
        total = [None] * 4
        for i in range(4):
            at = half * 64 + i * 16
            first, second = columns[at : at + 8], columns[at + 8 : at + 16]
            plain = first * yz[0] + second * yz[1]
            along_y = first * dyz[0] + second * dyz[1]
            along_z = first * ydz[0] + second * ydz[1]
            terms = [x_val[i] * plain, x_der[i] * plain, x_val[i] * along_y, x_val[i] * along_z]
            total = [t if s is None else s + t for s, t in zip(total, terms)]
        sums.append([jnp.sum(t, axis=0, keepdims=True) for t in total])
    state, adjoint = sums
    n = [geom[3 + r : 4 + r] for r in range(3)]
    normal_sq = n[0] * n[0] + n[1] * n[1] + n[2] * n[2]
    inner = state[1] * adjoint[1] + state[2] * adjoint[2] + state[3] * adjoint[3]
    along_s = state[1] * n[0] + state[2] * n[1] + state[3] * n[2]
    along_a = adjoint[1] * n[0] + adjoint[2] * n[1] + adjoint[3] * n[2]
    return normal_sq * inner - 2.0 * along_s * along_a + PENALTY * normal_sq * state[0] * adjoint[0]


def densities(rows_ref, geom_ref, out_ref, count):
    def step(tile, carry):
        at = pl.multiple_of(tile * LANES, LANES)
        columns = rows_ref[pl.ds(at, LANES), :].T
        out_ref[:, pl.ds(at, LANES)] = tile_density(columns, geom_ref[:, pl.ds(at, LANES)])
        return carry

    tiles = count // LANES
    lax.fori_loop(0, tiles, step, 0, unroll=4 if tiles % 4 == 0 else 2)


def near_kernel(first, cell_in, fields_in, geom_in, out_ref, cell_ref, fields_ref, geom_ref, rows_ref, sem):
    count = out_ref.shape[1]
    part = pl.ds(first, count)
    fetch([(cell_in.at[part], cell_ref), (geom_in.at[:, part], geom_ref), (fields_in, fields_ref)], sem)
    gather_rows(lambda p: cell_ref[p], fields_ref, rows_ref, count)
    densities(rows_ref, geom_ref, out_ref, count)


def far_densities(request_in, fields_ref, request_ref, query_ref, cell_v, cell_s, rows_ref, dens_ref, sems, sem):
    owners, _, capacity = request_in.shape
    count = owners * capacity
    fetch([(request_in.at[:, pl.ds(0, 8), :], request_ref)], sems)
    for o in range(owners):
        query_ref[:, o * capacity : (o + 1) * capacity] = request_ref[o]
    cell_v[...] = query_ref[6:7, :].astype(jnp.int32)
    copy = pltpu.make_async_copy(cell_v, cell_s, sem)
    copy.start()
    copy.wait()
    gather_rows(lambda p: cell_s[0, p], fields_ref, rows_ref, count)
    densities(rows_ref, query_ref, dens_ref, count)


def far_kernel(request_in, fields_ref, out_ref, *scratch):
    owners, _, capacity = request_in.shape
    far_densities(request_in, fields_ref, *scratch)
    dens_ref = scratch[5]
    for o in range(owners):
        out_ref[o] = dens_ref[:, o * capacity : (o + 1) * capacity]


def in_rows(x):
    return jnp.concatenate([x[:, i : i + LANES] for i in range(0, x.shape[1], LANES)], 0)


def in_line(x):
    return jnp.concatenate([x[i : i + 1, :] for i in range(x.shape[0])], 1)


def far_spread_kernel(request_in, fields_ref, out_ref, *scratch):
    owners, _, capacity = request_in.shape
    far_densities(request_in, fields_ref, *scratch)
    query_ref, dens_ref = scratch[1], scratch[5]
    number = iota((LINES * LANES, capacity), 0) + 1
    found = []
    for o in range(owners):
        part = slice(o * capacity, (o + 1) * capacity)
        place = jnp.where(number == query_ref[7:8, part].astype(jnp.int32), 1.0, 0.0).astype(BF16)
        high, mid, low = split3(dens_ref[:, part])
        parts = jnp.concatenate([high, mid, low, jnp.zeros((5, capacity), F32)], 0).astype(BF16)
        got = nt(parts, place)
        found.append(in_rows((got[2:3] + got[1:2]) + got[0:1]))
    lines = [jnp.concatenate(found[y::2], 0) for y in range(2)]
    for o in range(owners):
        out_ref[o] = lines[o % 2]


def far_scratch(requests):
    owners, _, capacity = requests.shape
    count = owners * capacity
    return [
        pltpu.VMEM((owners, 8, capacity), F32),
        pltpu.VMEM((8, count), F32),
        pltpu.VMEM((1, count), jnp.int32),
        pltpu.SMEM((1, count), jnp.int32),
        pltpu.VMEM((count, LANES), F32),
        pltpu.VMEM((1, count), F32),
        pltpu.SemaphoreType.DMA((1,)),
        pltpu.SemaphoreType.DMA,
    ]


def far_answers(requests, fields):
    owners, _, capacity = requests.shape
    return pl.pallas_call(
        far_kernel,
        out_shape=jax.ShapeDtypeStruct((owners, 1, capacity), F32),
        in_specs=[ANY, VMEM],
        out_specs=VMEM,
        scratch_shapes=far_scratch(requests),
        compiler_params=params(24),
        name="far_answers",
    )(requests, fields)


def far_spread(requests, fields):
    owners = requests.shape[0]
    return pl.pallas_call(
        far_spread_kernel,
        out_shape=jax.ShapeDtypeStruct((owners, owners // 2 * LINES, LANES), F32),
        in_specs=[ANY, VMEM],
        out_specs=VMEM,
        scratch_shapes=far_scratch(requests),
        compiler_params=params(24),
        cost_estimate=pl.CostEstimate(flops=40_000_000, bytes_accessed=4_000_000, transcendentals=0),
        name="far_spread",
    )(requests, fields)


def spline_weights(param):
    scaled = param * float(CTRL - 3)
    start = jnp.clip(jnp.floor(scaled), 0.0, float(CTRL - 4))
    x = scaled - start
    u = 1.0 - x
    cubed, squared = x * x * x, x * x
    weights = [
        u * u * u * (1.0 / 6.0),
        (3.0 * cubed - 6.0 * squared + 4.0) * (1.0 / 6.0),
        (-3.0 * cubed + 3.0 * squared + 3.0 * x + 1.0) * (1.0 / 6.0),
        cubed * (1.0 / 6.0),
    ]
    return start.astype(jnp.int32), weights


def spline_columns(start, weights):
    off = iota((CTRL, start.shape[1]), 0) - start
    out = jnp.zeros(off.shape, F32)
    for m in range(4):
        out = jnp.where(off == m, weights[m], out)
    return out


def slot_grids(density, s, t, patch, slots):
    start, weights = spline_weights(t)
    right = spline_columns(start, [w * density for w in weights])
    return grids_of(spline_columns(*spline_weights(s)), right, patch, slots)


def grids_of(left, right, patch, slots):
    left_high, left_low = halves(left)
    right_high, right_low = halves(right)
    masks = [jnp.where(patch == slot, 1.0, 0.0).astype(BF16) for slot in slots]
    high = jnp.concatenate([left_high * m for m in masks], 0)
    low = jnp.concatenate([left_low * m for m in masks], 0)
    return fold(nt(high, jnp.concatenate([right_high, right_low], 0))) + nt(low, right_high)


def side_by_side(grids):
    return [
        jnp.concatenate([grids[a * CTRL : (a + 1) * CTRL], grids[(a + 1) * CTRL : (a + 2) * CTRL]], 1)
        for a in range(0, GROUP, 2)
    ]


def near_payload_kernel(
    cell_in, fields_in, geom_in, near_in, slot_in, out_ref,
    near_ref, slot_ref, dens_ref, cell_ref, fields_ref, geom_ref, rows_ref, more, sem,
):
    others = [(near_in, near_ref), (slot_in, slot_ref)]
    others = [pltpu.make_async_copy(a, b, more.at[i]) for i, (a, b) in enumerate(others)]
    for copy in others:
        copy.start()
    near_kernel(0, cell_in, fields_in, geom_in, dens_ref, cell_ref, fields_ref, geom_ref, rows_ref, sem)
    for copy in others:
        copy.wait()
    slots = [slot_ref[s : s + 1, 0:1] for s in range(GROUP)]
    near = near_ref[...].astype(F32)
    grids = slot_grids(dens_ref[...], geom_ref[6:7, :], geom_ref[7:8, :], near, slots)
    lane = iota((1, LANES), 1)
    names = jnp.zeros((1, LANES), F32)
    for s in range(GROUP):
        names = jnp.where(lane == s, slots[s], names)
    out_ref[...] = jnp.concatenate(side_by_side(grids) + [slot_ref[0:GROUP, :]] + [names] * GROUP, 0)


def near_payload(near_cell, fields, near_geom, near_patch, slots):
    count = near_geom.shape[1]
    return pl.pallas_call(
        near_payload_kernel,
        out_shape=jax.ShapeDtypeStruct((PAYLOAD_ROWS, LANES), F32),
        in_specs=[HBM] * 5,
        out_specs=VMEM,
        scratch_shapes=[
            pltpu.VMEM(near_patch.shape, jnp.int32),
            pltpu.VMEM(slots.shape, F32),
            pltpu.VMEM((1, count), F32),
            pltpu.SMEM((count,), jnp.int32),
            pltpu.VMEM(fields.shape, F32),
            pltpu.VMEM((8, count), F32),
            pltpu.VMEM((count, LANES), F32),
            pltpu.SemaphoreType.DMA((2,)),
            pltpu.SemaphoreType.DMA((3,)),
        ],
        compiler_params=params(60),
        cost_estimate=pl.CostEstimate(flops=100_000_000, bytes_accessed=4_000_000, transcendentals=0),
        name="near_payload",
    )(near_cell, fields, near_geom, near_patch, slots)


def to_spectral(blocks, basis, basis_pair):
    turned = product(blocks, basis_pair)
    parts = range(0, blocks.shape[0], CTRL)
    turned = product(basis, jnp.concatenate([turned[at : at + CTRL] for at in parts], 1))
    return jnp.concatenate([turned[:, 2 * at : 2 * at + LANES] for at in parts], 0)


def payload_kernel(
    reply_ref, place_ref, geom_ref, far_ref, slot_ref, near_ref, basis_ref, pair_ref, dens_ref, out_ref, flat_ref
):
    owners, _, capacity = reply_ref.shape
    count = geom_ref.shape[1]
    for o in range(owners):
        flat_ref[:, o * capacity : (o + 1) * capacity] = reply_ref[o]
    high, mid, low = split3(flat_ref[...])
    parts = jnp.concatenate([high, mid, low, jnp.zeros((5, owners * capacity), F32)], 0).astype(BF16)
    put = jnp.where(iota((owners * capacity, count), 0) == place_ref[...], 1.0, 0.0).astype(BF16)
    got = nn(parts, put)
    dens = (got[2:3] + got[1:2]) + got[0:1]
    dens_ref[...] = dens
    slots = [slot_ref[s : s + 1, 0:1] for s in range(GROUP)]
    grids = slot_grids(dens, geom_ref[6:7, :], geom_ref[7:8, :], far_ref[...].astype(F32), slots)
    out_ref[GRID_ROWS:PAYLOAD_ROWS, :] = near_ref[GRID_ROWS:PAYLOAD_ROWS, :]
    blocks = near_ref[0:GRID_ROWS, :] + jnp.concatenate(side_by_side(grids), 0)
    out_ref[0:GRID_ROWS, :] = to_spectral(blocks, basis_ref[...], pair_ref[...])


def make_payload(reply, place, far_geom, far_patch, slots, near, const):
    owners, _, capacity = reply.shape
    count = far_geom.shape[1]
    return pl.pallas_call(
        payload_kernel,
        out_shape=(
            jax.ShapeDtypeStruct((1, count), F32),
            jax.ShapeDtypeStruct((PAYLOAD_ROWS, LANES), F32),
        ),
        in_specs=[VMEM] * 6 + [WHOLE] * 2,
        out_specs=(VMEM, VMEM),
        scratch_shapes=[pltpu.VMEM((1, owners * capacity), F32)],
        compiler_params=params(24),
        name="make_payload",
    )(reply, place, far_geom, far_patch, slots, near, const["basis"], const["basis_pair"])


def pair_rows(edge):
    blank = jnp.zeros((8, CTRL), F32)
    return jnp.concatenate([jnp.concatenate([edge, blank], 1), jnp.concatenate([blank, edge], 1)], 0)


def absorb(first_own, y_at, per_owner, items, sums, groups, edge, scale, name_v, name_s, edges, where_to, name_sem):
    patches = groups.shape[1]
    low8 = iota((8, LANES), 1) < CTRL
    spare = per_owner + iota((1, LANES), 1) // 2 % 2
    at = 0
    for ref, parts, _, _ in items:
        for p in range(parts):
            last = (p + 1) * PAYLOAD_ROWS - 1
            patch = ref[last : last + 1, :].astype(jnp.int32) - first_own
            name_v[at : at + 1, :] = jnp.where((patch >= 0) & (patch < per_owner), patch, spare)
            at += 1
    names = pltpu.make_async_copy(name_v, name_s, name_sem)
    names.start()

    sums[...] = jnp.zeros(sums.shape, F32)
    edge_high, edge_low = halves(edge)
    edge_both = jnp.concatenate([edge_high, edge_low], 0)
    both_high, both_low = halves(pair_rows(edge))
    both_both = jnp.concatenate([both_high, both_low], 0)
    for dy in sorted({dy for _, _, dy, _ in items}):
        at = 0
        chunks = [(ref, p) for ref, parts, own, _ in items if own == dy for p in range(0, parts, 2)]
        for ref, start in chunks:
            blocks = []
            for p in (start, start + 1):
                row = p * PAYLOAD_ROWS
                blocks += [halves(ref[row + q * CTRL : row + (q + 1) * CTRL, :]) for q in range(GROUP // 2)]
                row += GRID_ROWS
                where_to[at + GROUP * (p - start) : at + GROUP * (p - start + 1), :] = ref[row : row + GROUP, :]
            high, low = [jnp.concatenate(x, 1) for x in zip(*blocks)]
            along_rows = nn(edge_both, high)
            along_rows = (along_rows[:8] + along_rows[8:]) + nn(edge_high, low)
            high, low = [jnp.concatenate(x, 0) for x in zip(*blocks)]
            along_cols = nt(both_both, high)
            along_cols = (along_cols[:16] + along_cols[16:]) + nt(both_high, low)
            for s in range(2 * GROUP):
                q = s // 2
                first = along_rows[:, q * LANES : (q + 1) * LANES]
                second = along_cols[8 * (s % 2) : 8 * (s % 2) + 8, q // 2 * LANES : (q // 2 + 1) * LANES]
                if s % 2:
                    first = pltpu.roll(first, CTRL, 1)
                if q % 2 == 0:
                    second = pltpu.roll(second, CTRL, 1)
                edges[8 * at : 8 * at + 8, :] = jnp.where(low8, first, second) * scale
                at += 1
        lane = iota((at, LANES), 1)
        place = jnp.where(lane == where_to[:at, :].astype(jnp.int32), 1.0, 0.0).T[:patches].astype(BF16)
        rows = jnp.concatenate([edges[pl.ds(r, at, stride=8), :] for r in range(6)], 1)
        groups[dy ^ y_at] = fold(nn(place, two(rows)))

    names.wait()

    def add_items(wanted):
        at = 0
        for ref, parts, dy, _ in items:

            def add_payload(p, carry, ref=ref, at=at):
                places = [pl.ds(pl.multiple_of(name_s[at + p, s] * CTRL, CTRL), CTRL) for s in range(GROUP)]
                first = pl.multiple_of(p * PAYLOAD_ROWS, 8)
                blocks = [ref[pl.ds(first + q * CTRL, CTRL), :] for q in range(GROUP // 2)]
                held = [sums[s % 2, places[s], :] + blocks[s // 2] for s in range(GROUP)]
                for s in range(GROUP):
                    sums[s % 2, places[s], :] = held[s]
                return carry

            if dy == wanted:
                lax.fori_loop(0, parts, add_payload, 0, unroll=2)
            at += parts

    @pl.when(y_at == 0)
    def _():
        add_items(0)
        add_items(1)

    @pl.when(y_at != 0)
    def _():
        add_items(1)
        add_items(0)


def smooth_kernel(
    items, per_owner, where_ref, adj_ref, coupling_ref, basis_ref, pair_ref, series_ref, edge_ref, scale_ref, *rest
):
    refs, rest = rest[: len(items)], rest[len(items) :]
    out_ref, sums, groups, halo_all, halo_rows, out_v, out_sem, *scratch = rest
    patches = adj_ref.shape[0]
    first_own = pl.multiple_of(where_ref[0] * per_owner, 8)
    items = [(ref, *item) for ref, item in zip(refs, items)]
    edge = edge_ref[...]
    scale = scale_ref[...]
    if len(items) == 1:
        groups[...] = jnp.zeros(groups.shape, F32)
    absorb(first_own, where_ref[1], per_owner, items, sums, groups, edge, scale, *scratch)
    base = groups[0] + groups[1]
    base = [base[:, 4 * CTRL * k : 4 * CTRL * (k + 1)] for k in range(3)]

    column = iota((patches, patches), 1)
    wide = 4 * CTRL

    def facing(adjacency):
        hits = [
            jnp.where(adjacency[:, s : s + 1] == column[: adjacency.shape[0]], 1.0, 0.0).astype(BF16)
            for s in range(4)
        ]
        return jnp.concatenate([hits[0], hits[2]], 0), jnp.concatenate([hits[1], hits[3]], 0)

    def halo(facing, edges):
        count = facing[0].shape[0] // 2
        low_lane = iota((count, LANES), 1) < CTRL
        first = fold(nn(facing[0], two(edges[:, LANES:])))
        second = fold(nn(facing[1], two(edges[:, :LANES])))
        return jnp.concatenate(
            [jnp.where(low_lane, x[:count], x[count:]) for x in (first, second)], 1
        )

    every = facing(adj_ref[...])
    halo0 = halo(every, base[0])
    effect0 = product(halo0, coupling_ref[...])
    edges1 = base[0] + base[1] + effect0[:, :wide]
    halo1 = halo(every, edges1)
    effect1 = product(halo1, coupling_ref[:, :wide])
    edges2 = base[0] + base[1] + base[2] + effect0[:, wide:] + effect1
    halo2 = halo(facing(adj_ref[pl.ds(first_own, per_owner), :]), edges2)
    halo_all[0] = halo1
    halo_all[1] = halo0
    for k in range(3):
        mine = halo2 if k == 0 else halo_all[k - 1, pl.ds(first_own, per_owner), :]
        factor = SMOOTHING * scale[2 * k : 2 * k + 1]
        for side in range(2):
            halo_rows[pl.ds(2 * k + side, per_owner, stride=8), :] = (
                mine[:, side * LANES : (side + 1) * LANES] * factor
            )
    zero = jnp.zeros((per_owner, LANES), F32)
    for r in (6, 7):
        halo_rows[pl.ds(r, per_owner, stride=8), :] = zero

    pairs = per_owner // 2
    both = pair_rows(edge)
    low8 = iota((8, LANES), 1) < CTRL
    along_rows, along_cols = [], []
    for pair in range(pairs):
        a = halo_rows[16 * pair : 16 * pair + 8, :]
        b = halo_rows[16 * pair + 8 : 16 * pair + 16, :]
        along_rows.append(jnp.where(low8, a, pltpu.roll(b, CTRL, 1)))
        low, high = (pltpu.roll(x, CTRL, 1) for x in (a, b)) if pair % 2 == 0 else (a, b)
        along_cols.append(jnp.concatenate([low, high], 0))
    from_rows = tn_product(edge, jnp.concatenate(along_rows, 1))
    low_half = iota((CTRL, LANES), 1) < CTRL
    basis_both = pair_ref[...]
    low16 = iota((16, LANES), 1) < CTRL
    along_cols = [jnp.where(low16, x, y) for x, y in zip(along_cols[::2], along_cols[1::2])]
    from_cols = tn_product(jnp.concatenate(along_cols, 1), both)
    step = pairs // CHUNKS if pairs % CHUNKS == 0 else pairs
    stores = []
    for start in range(0, pairs, step):
        turned = []
        for pair in range(start, start + step):
            a, b = [slice(patch * CTRL, (patch + 1) * CTRL) for patch in (2 * pair, 2 * pair + 1)]
            left = sums[0, a, :] + pltpu.roll(sums[1, a, :], CTRL, 1)
            right = pltpu.roll(sums[0, b, :], CTRL, 1) + sums[1, b, :]
            spectral = jnp.where(low_half, left, right) * series_ref[...]
            spectral = spectral + from_rows[:, pair * LANES : (pair + 1) * LANES]
            turned.append(spectral + from_cols[pair * CTRL : (pair + 1) * CTRL, :])
        turned = product(jnp.concatenate(turned, 0), basis_both)
        flat = jnp.concatenate([turned[at : at + CTRL] for at in range(0, step * CTRL, CTRL)], 1)
        done = product(basis_ref[...], flat)
        for pair in range(start, start + step):
            at = (pair - start) * LANES
            out_v[2 * pair] = done[:, at : at + CTRL]
            out_v[2 * pair + 1] = done[:, at + CTRL : at + LANES]
        part = pl.ds(2 * start, 2 * step)
        stores.append(pltpu.make_async_copy(out_v.at[part], out_ref.at[part], out_sem.at[len(stores)]))
        stores[-1].start()
    for store in stores:
        store.wait()


def tn_product(x, y):
    x_high, x_low = halves(x)
    y_high, y_low = halves(y)
    return tn(x_high, y_high) + (tn(x_low, y_high) + tn(x_high, y_low))


def smooth(payloads, items, where, adjacency, per_owner, const):
    patches = adjacency.shape[0]
    total = sum(item[0] for item in items)
    return pl.pallas_call(
        functools.partial(smooth_kernel, items, per_owner),
        out_shape=jax.ShapeDtypeStruct((per_owner, CTRL, CTRL), F32),
        in_specs=[SMEM] + [WHOLE] * 7 + [VMEM] * len(payloads),
        out_specs=HBM,
        scratch_shapes=[
            pltpu.VMEM((2, (per_owner + 2) * CTRL, LANES), F32),
            pltpu.VMEM((2, patches, 12 * CTRL), F32),
            pltpu.VMEM((2, patches, 4 * CTRL), F32),
            pltpu.VMEM((per_owner * 8, LANES), F32),
            pltpu.VMEM((per_owner, CTRL, CTRL), F32),
            pltpu.SemaphoreType.DMA((CHUNKS,)),
            pltpu.VMEM((total, LANES), jnp.int32),
            pltpu.SMEM((total, LANES), jnp.int32),
            pltpu.VMEM((total * GROUP * 8, LANES), F32),
            pltpu.VMEM((total * GROUP, LANES), F32),
            pltpu.SemaphoreType.DMA,
        ],
        compiler_params=params(32),
        name="smooth",
    )(
        where, adjacency, const["coupling"], const["basis"], const["basis_pair"], const["series"],
        const["edge_rows"], const["scale_rows"], *payloads,
    )


def far_line_kernel(where_ref, spread_ref, asked_ref, out_ref, own_ref, total_ref):
    owners = spread_ref.shape[0]
    line = owners // 2
    total = spread_ref[0]
    for o in range(1, owners):
        total = total + spread_ref[o]
    total_ref[...] = total
    own_ref[...] = total_ref[pl.ds(where_ref[2] // 2 * LINES, LINES), :]
    for z in range(line):
        dens = total[z * LINES : (z + 1) * LINES]
        held = asked_ref[2 * z + where_ref[1], 8:, 0:LANES]
        s, t, patch = [held[i * LINES : (i + 1) * LINES] for i in range(3)]
        start_s, weights_s = spline_weights(s)
        start_t, weights_t = spline_weights(t)
        left = spline_columns(in_line(start_s), [in_line(w) for w in weights_s])
        right = spline_columns(in_line(start_t), [in_line(w * dens) for w in weights_t])
        slots = [held[3 * LINES + i : 3 * LINES + i + 1, 0:1] for i in range(GROUP)]
        far = side_by_side(grids_of(left, right, in_line(patch), slots))
        out_ref[z * GRID_ROWS : (z + 1) * GRID_ROWS, :] = jnp.concatenate(far, 0)


def far_line(spread, asked, where):
    line = spread.shape[0] // 2
    return pl.pallas_call(
        far_line_kernel,
        out_shape=(
            jax.ShapeDtypeStruct((line * GRID_ROWS, LANES), F32),
            jax.ShapeDtypeStruct((LINES, LANES), F32),
        ),
        in_specs=[SMEM, VMEM, VMEM],
        out_specs=(VMEM, VMEM),
        scratch_shapes=[pltpu.VMEM((line * LINES, LANES), F32)],
        compiler_params=params(16),
        cost_estimate=pl.CostEstimate(flops=100_000_000, bytes_accessed=1_000_000, transcendentals=0),
        name="far_line",
    )(where, spread, asked)


def join_kernel(where_ref, far_ref, basis_ref, pair_ref, *refs):
    *parts, out_ref, near_ref = refs
    for k, part in enumerate(parts):
        near_ref[where_ref[2] // 2 ^ k] = part[...]
    blocks = [near_ref[z, 0:GRID_ROWS, :] + far_ref[z * GRID_ROWS : (z + 1) * GRID_ROWS, :] for z in range(len(parts))]
    blocks = to_spectral(jnp.concatenate(blocks, 0), basis_ref[...], pair_ref[...])
    for z in range(len(parts)):
        at = z * PAYLOAD_ROWS
        out_ref[at : at + GRID_ROWS, :] = blocks[z * GRID_ROWS : (z + 1) * GRID_ROWS]
        out_ref[at + GRID_ROWS : at + PAYLOAD_ROWS, :] = near_ref[z, GRID_ROWS:PAYLOAD_ROWS, :]


def join(parts, far, where, const):
    return pl.pallas_call(
        join_kernel,
        out_shape=jax.ShapeDtypeStruct((len(parts) * PAYLOAD_ROWS, LANES), F32),
        in_specs=[SMEM, VMEM, WHOLE, WHOLE] + [VMEM] * len(parts),
        out_specs=VMEM,
        scratch_shapes=[pltpu.VMEM((len(parts), PAYLOAD_ROWS, LANES), F32)],
        compiler_params=params(16),
        name="join",
    )(where, far, const["basis"], const["basis_pair"], *parts)


def over(axis, array, bit):
    count = lax.axis_size(axis)
    return lax.ppermute(array, axis, [(i, i ^ bit) for i in range(count)])


def gather_in_plane(here):
    half = here.shape[0] // 2
    beside_y = over("vol", here, 1)
    beside_x = over("dsg", here, 2)
    corner = [over("dsg", beside_y[:half], 2), over("vol", beside_x[half:], 1)]
    arrays = [here, beside_x, beside_y]
    arrays = [x for array in arrays for x in (array, over("dsg", array, 1))]
    arrays += corner + [over("dsg", c, 1) for c in corner]
    items = ((4, 0, 0), (4, 0, 0), (4, 0, 1), (4, 0, 1), (4, 1, 0), (4, 1, 0)) + ((2, 1, 1),) * 4
    return arrays, items


def per_device(
    fields, far_geom, far_block, far_cell, far_patch, near_geom, near_cell, near_patch, adjacency
):
    vol_count, dsg_count = lax.axis_size("vol"), lax.axis_size("dsg")
    far_count = far_cell.shape[0]
    capacity = 5 * far_count // (2 * vol_count)
    const = {name: jnp.asarray(value) for name, value in constants().items()}

    per_owner = adjacency.shape[0] // dsg_count
    staged = vol_count == 8 and dsg_count == 4 and far_count == LINES * LANES
    vol_at = lax.axis_index("vol")
    where = jnp.stack([lax.axis_index("dsg"), vol_at % 2 if staged else 0, vol_at]).astype(jnp.int32)
    near_patch, far_patch = near_patch.reshape(1, -1), far_patch.reshape(1, -1)
    request, place, slots = pack_requests(
        far_geom, far_block.reshape(1, -1), far_cell.reshape(1, -1), near_patch, far_patch, vol_count, capacity, staged
    )
    asked = lax.all_to_all(request, "vol", split_axis=0, concat_axis=0, tiled=True)
    near = near_payload(near_cell, fields, near_geom, near_patch, slots)
    asked, near = lax.optimization_barrier((asked, near))
    if staged:
        spread = far_spread(asked, fields)
        spread = lax.all_to_all(spread, "vol", split_axis=0, concat_axis=0, tiled=True)
        parts = [near] + [over("vol", near, 2 * k) for k in (1, 2, 3)]
        far, far_dens = far_line(spread, asked, where)
        here = join(parts, far, where, const)
        arrays, items = gather_in_plane(here)
    else:
        reply = lax.all_to_all(far_answers(asked, fields), "vol", split_axis=0, concat_axis=0, tiled=True)
        far_dens, payload = make_payload(reply, place, far_geom, far_patch, slots, near, const)
        arrays = [lax.all_gather(payload, ("vol", "dsg"), axis=0, tiled=True)]
        items = ((vol_count * dsg_count, 0, 0),)
    design = smooth(arrays, items, where, adjacency, per_owner, const)
    return far_dens.reshape(-1), design


def solution(mesh):
    return jax.shard_map(
        per_device,
        mesh=mesh,
        in_specs=(
            P("vol", None),
            P(None, ("vol", "dsg")),
            P(("vol", "dsg"), None),
            P(("vol", "dsg")),
            P(("vol", "dsg")),
            P(None, ("vol", "dsg")),
            P(("vol", "dsg")),
            P(("vol", "dsg")),
            P(),
        ),
        out_specs=(P(("vol", "dsg")), P("dsg", None, None)),
        check_vma=False,
    )
```

```python
import functools

import jax
import jax.numpy as jnp
import numpy as np
from jax import lax
from jax.experimental import pallas as pl
from jax.experimental.pallas import tpu as pltpu
from jax.sharding import PartitionSpec as P

CTRL = 64
GROUP = 4
LANES = 128
PENALTY = 4.0
SMOOTHING = 16.0
NO_PATCH = 1.0e6
GRID_ROWS = GROUP // 2 * CTRL
PAYLOAD_ROWS = GRID_ROWS + 2 * GROUP
LINES = 4
CHUNKS = 3
F32 = jnp.float32
BF16 = jnp.bfloat16
EXACT = lax.Precision.HIGHEST
VMEM = pl.BlockSpec(memory_space=pltpu.VMEM)
SMEM = pl.BlockSpec(memory_space=pltpu.SMEM)
ANY = pl.BlockSpec(memory_space=pl.ANY)
WHOLE = pl.BlockSpec()
HBM = pl.BlockSpec(memory_space=pltpu.HBM)


def params(megabytes):
    return pltpu.CompilerParams(vmem_limit_bytes=megabytes << 20)


def constants():
    order = np.arange(1, CTRL + 1)
    basis = np.sqrt(2.0 / (CTRL + 1)) * np.sin(np.pi * np.outer(order, order) / (CTRL + 1))
    eigen = 1.0 + SMOOTHING * (2.0 - 2.0 * np.cos(np.pi * order / (CTRL + 1)))
    damp = 1.0 / eigen
    keep = 1.0 - damp
    powers = [keep**k * damp for k in range(3)]
    ends = [basis[:, 0], basis[:, CTRL - 1]]
    edge_rows = np.zeros((8, CTRL))
    scale_rows = np.zeros((8, CTRL))
    for k in range(3):
        for side in range(2):
            edge_rows[2 * k + side] = powers[k] * ends[side]
            scale_rows[2 * k + side] = powers[k]
    series = sum(np.outer(keep**k * damp, keep**k * damp) for k in range(4))

    def coupling(k):
        f = powers[k]
        lane = [0, 2, 1, 3]
        out = np.zeros((4 * CTRL, 4 * CTRL))
        for a, side_in in enumerate(lane):
            for b, side_out in enumerate(lane):
                q_in, q_out = ends[side_in % 2], ends[side_out % 2]
                if side_in // 2 == side_out // 2:
                    block = np.diag(f * np.sum(q_in * q_out * f))
                else:
                    block = np.outer(q_out * f, q_in * f)
                out[a * CTRL : (a + 1) * CTRL, b * CTRL : (b + 1) * CTRL] = SMOOTHING * block
        return out

    return dict(
        basis=np.float32(basis),
        basis_pair=np.float32(np.kron(np.eye(2), basis)),
        edge_rows=np.float32(edge_rows),
        scale_rows=np.float32(np.concatenate([scale_rows, scale_rows], 1)),
        series=np.float32(np.concatenate([series, series], 1)),
        coupling=np.float32(np.concatenate([coupling(0), coupling(1)], 1)),
    )


def split3(x):
    high = x.astype(BF16).astype(F32)
    rest = x - high
    mid = rest.astype(BF16).astype(F32)
    return high, mid, rest - mid


def nt(a, b, **kw):
    return lax.dot_general(a, b, (((1,), (1,)), ((), ())), preferred_element_type=F32, **kw)


def nn(a, b, **kw):
    return lax.dot_general(a, b, (((1,), (0,)), ((), ())), preferred_element_type=F32, **kw)


def tn(a, b, **kw):
    return lax.dot_general(a, b, (((0,), (0,)), ((), ())), preferred_element_type=F32, **kw)


def iota(shape, axis):
    return lax.broadcasted_iota(jnp.int32, shape, axis)


def halves(x):
    high = x.astype(BF16)
    return high, (x - high.astype(F32)).astype(BF16)


def two(x):
    return jnp.concatenate(halves(x), 1)


def fold(x):
    half = x.shape[1] // 2
    return x[:, :half] + x[:, half:]


def product(x, y):
    x_high, x_low = halves(x)
    y_high, y_low = halves(y)
    return nn(x_high, y_high) + (nn(x_low, y_high) + nn(x_high, y_low))


def nt_product(x, y):
    x_high, x_low = halves(x)
    y_high, y_low = halves(y)
    return nt(x_high, y_high) + (nt(x_low, y_high) + nt(x_high, y_low))


def fetch(pairs, sem):
    copies = [pltpu.make_async_copy(a, b, sem.at[i]) for i, (a, b) in enumerate(pairs)]
    for copy in copies:
        copy.start()
    for copy in copies:
        copy.wait()


def pack_kernel(
    capacity, geom_in, block_in, cell_in, near_in, far_in, request_ref, place_ref, slot_ref,
    geom_ref, block_ref, cell_ref, near_ref, far_ref, sem,
):
    fetch([(geom_in, geom_ref), (block_in, block_ref), (cell_in, cell_ref), (near_in, near_ref), (far_in, far_ref)], sem)
    near, far = near_ref[...].astype(F32), far_ref[...].astype(F32)
    slots = []
    last = jnp.full((1, 1), -1.0, F32)
    for _ in range(GROUP):
        a = jnp.min(jnp.where(near > last, near, NO_PATCH), axis=1, keepdims=True)
        b = jnp.min(jnp.where(far > last, far, NO_PATCH), axis=1, keepdims=True)
        last = jnp.minimum(a, b)
        slots.append(jnp.broadcast_to(last, (1, LANES)))
    slot_ref[...] = jnp.concatenate(slots + slots, 0)
    owners = request_ref.shape[0]
    count = geom_ref.shape[1]
    block = block_ref[...]
    owner_id = iota((owners, count), 0)
    chosen = jnp.where(owner_id == block, 1.0, 0.0).astype(F32)
    earlier = jnp.where(iota((count, count), 0) < iota((count, count), 1), 1.0, 0.0).astype(BF16)
    rank = nn(chosen.astype(BF16), earlier)
    place = jnp.sum(chosen * (rank + (capacity * owner_id).astype(F32)), axis=0, keepdims=True)
    place = place.astype(jnp.int32)
    place_ref[...] = place
    row = iota((8, count), 0)
    number = (iota((8, count), 1) + 1).astype(F32)
    values = jnp.where(row < 6, geom_ref[...], jnp.where(row == 6, cell_ref[...].astype(F32), number))
    high, mid, low = split3(values)
    parts = jnp.concatenate([high, mid, low], 0).astype(BF16)
    put = jnp.where(iota((owners * capacity, count), 0) == place, 1.0, 0.0).astype(BF16)
    packed = nt(parts, put)
    packed = (packed[16:24] + packed[8:16]) + packed[0:8]
    for owner in range(owners):
        request_ref[owner, 0:8, :] = packed[:, owner * capacity : (owner + 1) * capacity]
    if request_ref.shape[1] > 8:
        own = [in_rows(x) for x in (geom_ref[6:7, :], geom_ref[7:8, :], far)] + [slot_ref[0:GROUP, :]]
        own = jnp.concatenate(own, 0)
        for owner in range(owners):
            request_ref[owner, 8:, 0:LANES] = own
            request_ref[owner, 8:, LANES:] = jnp.zeros((own.shape[0], capacity - LANES), F32)


def pack_requests(far_geom, far_block, far_cell, near_patch, far_patch, owners, capacity, staged):
    count = far_geom.shape[1]
    return pl.pallas_call(
        functools.partial(pack_kernel, capacity),
        out_shape=(
            jax.ShapeDtypeStruct((owners, 8 + staged * (3 * LINES + GROUP), capacity), F32),
            jax.ShapeDtypeStruct((1, count), jnp.int32),
            jax.ShapeDtypeStruct((8, LANES), F32),
        ),
        in_specs=[HBM] * 5,
        out_specs=(VMEM, VMEM, VMEM),
        scratch_shapes=[
            pltpu.VMEM((8, count), F32),
            pltpu.VMEM((1, count), jnp.int32),
            pltpu.VMEM((1, count), jnp.int32),
            pltpu.VMEM(near_patch.shape, jnp.int32),
            pltpu.VMEM(far_patch.shape, jnp.int32),
            pltpu.SemaphoreType.DMA((5,)),
        ],
        compiler_params=params(60),
        name="pack_requests",
    )(far_geom, far_block, far_cell, near_patch, far_patch)


def gather_rows(cells, fields_ref, rows_ref, count):
    unroll = 64

    def step(i, carry):
        for u in range(unroll):
            p = i * unroll + u
            rows_ref[pl.ds(p, 1), :] = fields_ref[pl.ds(cells(p), 1), :]
        return carry

    lax.fori_loop(0, count // unroll, step, 0)


def bernstein(t):
    u = 1.0 - t
    uu, tt = u * u, t * t
    values = [uu * u, 3.0 * t * uu, 3.0 * tt * u, tt * t]
    tu = 6.0 * t * u
    slopes = [-3.0 * uu, 3.0 * uu - tu, tu - 3.0 * tt, 3.0 * tt]
    return values, slopes


def tile_density(columns, geom):
    row = iota((8, LANES), 0)
    wide = [jnp.broadcast_to(geom[r : r + 1], (8, LANES)) for r in range(3)]
    x_val, x_der = bernstein(wide[0])
    y_val, y_der = bernstein(wide[1])
    z_val, z_der = bernstein(wide[2])
    k = row % 4

    def by_k(v):
        return jnp.where(k == 0, v[0], jnp.where(k == 1, v[1], jnp.where(k == 2, v[2], v[3])))

    def by_j(v, m):
        return jnp.where(row < 4, v[2 * m], v[2 * m + 1])

    z_v, z_d = by_k(z_val), by_k(z_der)
    yz = [by_j(y_val, m) * z_v for m in range(2)]
    dyz = [by_j(y_der, m) * z_v for m in range(2)]
    ydz = [by_j(y_val, m) * z_d for m in range(2)]
    sums = []
    for half in range(2):
        total = [None] * 4
        for i in range(4):
            at = half * 64 + i * 16
            first, second = columns[at : at + 8], columns[at + 8 : at + 16]
            plain = first * yz[0] + second * yz[1]
            along_y = first * dyz[0] + second * dyz[1]
            along_z = first * ydz[0] + second * ydz[1]
            terms = [x_val[i] * plain, x_der[i] * plain, x_val[i] * along_y, x_val[i] * along_z]
            total = [t if s is None else s + t for s, t in zip(total, terms)]
        sums.append([jnp.sum(t, axis=0, keepdims=True) for t in total])
    state, adjoint = sums
    n = [geom[3 + r : 4 + r] for r in range(3)]
    normal_sq = n[0] * n[0] + n[1] * n[1] + n[2] * n[2]
    inner = state[1] * adjoint[1] + state[2] * adjoint[2] + state[3] * adjoint[3]
    along_s = state[1] * n[0] + state[2] * n[1] + state[3] * n[2]
    along_a = adjoint[1] * n[0] + adjoint[2] * n[1] + adjoint[3] * n[2]
    return normal_sq * inner - 2.0 * along_s * along_a + PENALTY * normal_sq * state[0] * adjoint[0]


def densities(rows_ref, geom_ref, out_ref, count):
    def step(tile, carry):
        at = pl.multiple_of(tile * LANES, LANES)
        columns = rows_ref[pl.ds(at, LANES), :].T
        out_ref[:, pl.ds(at, LANES)] = tile_density(columns, geom_ref[:, pl.ds(at, LANES)])
        return carry

    tiles = count // LANES
    lax.fori_loop(0, tiles, step, 0, unroll=next(n for n in (8, 5, 4, 2, 1) if tiles % n == 0))


def near_kernel(first, cell_in, fields_in, geom_in, out_ref, cell_ref, fields_ref, geom_ref, rows_ref, sem):
    count = out_ref.shape[1]
    part = pl.ds(first, count)
    fetch([(cell_in.at[part], cell_ref), (geom_in.at[:, part], geom_ref), (fields_in, fields_ref)], sem)
    gather_rows(lambda p: cell_ref[p], fields_ref, rows_ref, count)
    densities(rows_ref, geom_ref, out_ref, count)


def far_densities(request_in, fields_ref, request_ref, query_ref, cell_v, cell_s, rows_ref, dens_ref, sems, sem):
    owners, _, capacity = request_in.shape
    count = owners * capacity
    fetch([(request_in.at[:, pl.ds(0, 8), :], request_ref)], sems)
    for o in range(owners):
        query_ref[:, o * capacity : (o + 1) * capacity] = request_ref[o]
    cell_v[...] = query_ref[6:7, :].astype(jnp.int32)
    copy = pltpu.make_async_copy(cell_v, cell_s, sem)
    copy.start()
    copy.wait()
    gather_rows(lambda p: cell_s[0, p], fields_ref, rows_ref, count)
    densities(rows_ref, query_ref, dens_ref, count)


def far_kernel(request_in, fields_ref, out_ref, *scratch):
    owners, _, capacity = request_in.shape
    far_densities(request_in, fields_ref, *scratch)
    dens_ref = scratch[5]
    for o in range(owners):
        out_ref[o] = dens_ref[:, o * capacity : (o + 1) * capacity]


def in_rows(x):
    return jnp.concatenate([x[:, i : i + LANES] for i in range(0, x.shape[1], LANES)], 0)


def in_line(x):
    return jnp.concatenate([x[i : i + 1, :] for i in range(x.shape[0])], 1)


def far_spread_kernel(request_in, fields_ref, out_ref, *scratch):
    owners, _, capacity = request_in.shape
    far_densities(request_in, fields_ref, *scratch)
    query_ref, dens_ref = scratch[1], scratch[5]
    number = iota((LINES * LANES, capacity), 0) + 1
    found = []
    for o in range(owners):
        part = slice(o * capacity, (o + 1) * capacity)
        place = jnp.where(number == query_ref[7:8, part].astype(jnp.int32), 1.0, 0.0).astype(BF16)
        high, mid, low = split3(dens_ref[:, part])
        parts = jnp.concatenate([high, mid, low, jnp.zeros((5, capacity), F32)], 0).astype(BF16)
        got = nt(parts, place)
        found.append(in_rows((got[2:3] + got[1:2]) + got[0:1]))
    lines = [jnp.concatenate(found[y::2], 0) for y in range(2)]
    for o in range(owners):
        out_ref[o] = lines[o % 2]


def far_scratch(requests):
    owners, _, capacity = requests.shape
    count = owners * capacity
    return [
        pltpu.VMEM((owners, 8, capacity), F32),
        pltpu.VMEM((8, count), F32),
        pltpu.VMEM((1, count), jnp.int32),
        pltpu.SMEM((1, count), jnp.int32),
        pltpu.VMEM((count, LANES), F32),
        pltpu.VMEM((1, count), F32),
        pltpu.SemaphoreType.DMA((1,)),
        pltpu.SemaphoreType.DMA,
    ]


def far_answers(requests, fields):
    owners, _, capacity = requests.shape
    return pl.pallas_call(
        far_kernel,
        out_shape=jax.ShapeDtypeStruct((owners, 1, capacity), F32),
        in_specs=[ANY, VMEM],
        out_specs=VMEM,
        scratch_shapes=far_scratch(requests),
        compiler_params=params(24),
        name="far_answers",
    )(requests, fields)


def far_spread(requests, fields):
    owners = requests.shape[0]
    return pl.pallas_call(
        far_spread_kernel,
        out_shape=jax.ShapeDtypeStruct((owners, owners // 2 * LINES, LANES), F32),
        in_specs=[ANY, VMEM],
        out_specs=VMEM,
        scratch_shapes=far_scratch(requests),
        compiler_params=params(24),
        cost_estimate=pl.CostEstimate(flops=40_000_000, bytes_accessed=4_000_000, transcendentals=0),
        name="far_spread",
    )(requests, fields)


def spline_weights(param):
    scaled = param * float(CTRL - 3)
    start = jnp.clip(jnp.floor(scaled), 0.0, float(CTRL - 4))
    x = scaled - start
    u = 1.0 - x
    cubed, squared = x * x * x, x * x
    weights = [
        u * u * u * (1.0 / 6.0),
        (3.0 * cubed - 6.0 * squared + 4.0) * (1.0 / 6.0),
        (-3.0 * cubed + 3.0 * squared + 3.0 * x + 1.0) * (1.0 / 6.0),
        cubed * (1.0 / 6.0),
    ]
    return start.astype(jnp.int32), weights


def spline_columns(start, weights):
    off = iota((CTRL, start.shape[1]), 0) - start
    out = jnp.zeros(off.shape, F32)
    for m in range(4):
        out = jnp.where(off == m, weights[m], out)
    return out


def slot_grids(density, s, t, patch, slots):
    start, weights = spline_weights(t)
    right = spline_columns(start, [w * density for w in weights])
    return grids_of(spline_columns(*spline_weights(s)), right, patch, slots)


def grids_of(left, right, patch, slots):
    left_high, left_low = halves(left)
    right_high, right_low = halves(right)
    masks = [jnp.where(patch == slot, 1.0, 0.0).astype(BF16) for slot in slots]
    high = jnp.concatenate([left_high * m for m in masks], 0)
    low = jnp.concatenate([left_low * m for m in masks], 0)
    return fold(nt(high, jnp.concatenate([right_high, right_low], 0))) + nt(low, right_high)


def side_by_side(grids):
    return [
        jnp.concatenate([grids[a * CTRL : (a + 1) * CTRL], grids[(a + 1) * CTRL : (a + 2) * CTRL]], 1)
        for a in range(0, GROUP, 2)
    ]


def near_payload_kernel(
    cell_in, fields_in, geom_in, near_in, slot_in, out_ref,
    near_ref, slot_ref, dens_ref, cell_ref, fields_ref, geom_ref, rows_ref, more, sem,
):
    others = [(near_in, near_ref), (slot_in, slot_ref)]
    others = [pltpu.make_async_copy(a, b, more.at[i]) for i, (a, b) in enumerate(others)]
    for copy in others:
        copy.start()
    near_kernel(0, cell_in, fields_in, geom_in, dens_ref, cell_ref, fields_ref, geom_ref, rows_ref, sem)
    for copy in others:
        copy.wait()
    slots = [slot_ref[s : s + 1, 0:1] for s in range(GROUP)]
    near = near_ref[...].astype(F32)
    grids = slot_grids(dens_ref[...], geom_ref[6:7, :], geom_ref[7:8, :], near, slots)
    lane = iota((1, LANES), 1)
    names = jnp.zeros((1, LANES), F32)
    for s in range(GROUP):
        names = jnp.where(lane == s, slots[s], names)
    out_ref[...] = jnp.concatenate(side_by_side(grids) + [slot_ref[0:GROUP, :]] + [names] * GROUP, 0)


def near_payload(near_cell, fields, near_geom, near_patch, slots):
    count = near_geom.shape[1]
    return pl.pallas_call(
        near_payload_kernel,
        out_shape=jax.ShapeDtypeStruct((PAYLOAD_ROWS, LANES), F32),
        in_specs=[HBM] * 5,
        out_specs=VMEM,
        scratch_shapes=[
            pltpu.VMEM(near_patch.shape, jnp.int32),
            pltpu.VMEM(slots.shape, F32),
            pltpu.VMEM((1, count), F32),
            pltpu.SMEM((count,), jnp.int32),
            pltpu.VMEM(fields.shape, F32),
            pltpu.VMEM((8, count), F32),
            pltpu.VMEM((count, LANES), F32),
            pltpu.SemaphoreType.DMA((2,)),
            pltpu.SemaphoreType.DMA((3,)),
        ],
        compiler_params=params(60),
        cost_estimate=pl.CostEstimate(flops=100_000_000, bytes_accessed=4_000_000, transcendentals=0),
        name="near_payload",
    )(near_cell, fields, near_geom, near_patch, slots)


def to_spectral(blocks, basis, basis_pair):
    turned = product(blocks, basis_pair)
    parts = range(0, blocks.shape[0], CTRL)
    turned = product(basis, jnp.concatenate([turned[at : at + CTRL] for at in parts], 1))
    return jnp.concatenate([turned[:, 2 * at : 2 * at + LANES] for at in parts], 0)


def payload_kernel(
    reply_ref, place_ref, geom_ref, far_ref, slot_ref, near_ref, basis_ref, pair_ref, dens_ref, out_ref, flat_ref
):
    owners, _, capacity = reply_ref.shape
    count = geom_ref.shape[1]
    for o in range(owners):
        flat_ref[:, o * capacity : (o + 1) * capacity] = reply_ref[o]
    high, mid, low = split3(flat_ref[...])
    parts = jnp.concatenate([high, mid, low, jnp.zeros((5, owners * capacity), F32)], 0).astype(BF16)
    put = jnp.where(iota((owners * capacity, count), 0) == place_ref[...], 1.0, 0.0).astype(BF16)
    got = nn(parts, put)
    dens = (got[2:3] + got[1:2]) + got[0:1]
    dens_ref[...] = dens
    slots = [slot_ref[s : s + 1, 0:1] for s in range(GROUP)]
    grids = slot_grids(dens, geom_ref[6:7, :], geom_ref[7:8, :], far_ref[...].astype(F32), slots)
    out_ref[GRID_ROWS:PAYLOAD_ROWS, :] = near_ref[GRID_ROWS:PAYLOAD_ROWS, :]
    blocks = near_ref[0:GRID_ROWS, :] + jnp.concatenate(side_by_side(grids), 0)
    out_ref[0:GRID_ROWS, :] = to_spectral(blocks, basis_ref[...], pair_ref[...])


def make_payload(reply, place, far_geom, far_patch, slots, near, const):
    owners, _, capacity = reply.shape
    count = far_geom.shape[1]
    return pl.pallas_call(
        payload_kernel,
        out_shape=(
            jax.ShapeDtypeStruct((1, count), F32),
            jax.ShapeDtypeStruct((PAYLOAD_ROWS, LANES), F32),
        ),
        in_specs=[VMEM] * 6 + [WHOLE] * 2,
        out_specs=(VMEM, VMEM),
        scratch_shapes=[pltpu.VMEM((1, owners * capacity), F32)],
        compiler_params=params(24),
        name="make_payload",
    )(reply, place, far_geom, far_patch, slots, near, const["basis"], const["basis_pair"])


def pair_rows(edge):
    blank = jnp.zeros((8, CTRL), F32)
    return jnp.concatenate([jnp.concatenate([edge, blank], 1), jnp.concatenate([blank, edge], 1)], 0)


def absorb(first_own, y_at, per_owner, items, sums, groups, edge, scale, name_v, name_s, edges, where_to, name_sem):
    patches = groups.shape[1]
    low8 = iota((8, LANES), 1) < CTRL
    spare = per_owner + iota((1, LANES), 1) // 2 % 2
    at = 0
    for ref, parts, _, _ in items:
        for p in range(parts):
            last = (p + 1) * PAYLOAD_ROWS - 1
            patch = ref[last : last + 1, :].astype(jnp.int32) - first_own
            name_v[at : at + 1, :] = jnp.where((patch >= 0) & (patch < per_owner), patch, spare)
            at += 1
    names = pltpu.make_async_copy(name_v, name_s, name_sem)
    names.start()

    sums[...] = jnp.zeros(sums.shape, F32)
    edge_high, edge_low = halves(edge)
    edge_both = jnp.concatenate([edge_high, edge_low], 0)
    both_high, both_low = halves(pair_rows(edge))
    both_both = jnp.concatenate([both_high, both_low], 0)
    for dy in sorted({dy for _, _, dy, _ in items}):
        at = 0
        chunks = [(ref, p) for ref, parts, own, _ in items if own == dy for p in range(0, parts, 2)]
        for ref, start in chunks:
            blocks = []
            for p in (start, start + 1):
                row = p * PAYLOAD_ROWS
                blocks += [halves(ref[row + q * CTRL : row + (q + 1) * CTRL, :]) for q in range(GROUP // 2)]
                row += GRID_ROWS
                where_to[at + GROUP * (p - start) : at + GROUP * (p - start + 1), :] = ref[row : row + GROUP, :]
            high, low = [jnp.concatenate(x, 1) for x in zip(*blocks)]
            along_rows = nn(edge_both, high)
            along_rows = (along_rows[:8] + along_rows[8:]) + nn(edge_high, low)
            high, low = [jnp.concatenate(x, 0) for x in zip(*blocks)]
            along_cols = nt(both_both, high)
            along_cols = (along_cols[:16] + along_cols[16:]) + nt(both_high, low)
            for s in range(2 * GROUP):
                q = s // 2
                first = along_rows[:, q * LANES : (q + 1) * LANES]
                second = along_cols[8 * (s % 2) : 8 * (s % 2) + 8, q // 2 * LANES : (q // 2 + 1) * LANES]
                if s % 2:
                    first = pltpu.roll(first, CTRL, 1)
                if q % 2 == 0:
                    second = pltpu.roll(second, CTRL, 1)
                edges[8 * at : 8 * at + 8, :] = jnp.where(low8, first, second) * scale
                at += 1
        lane = iota((at, LANES), 1)
        place = jnp.where(lane == where_to[:at, :].astype(jnp.int32), 1.0, 0.0).T[:patches].astype(BF16)
        rows = jnp.concatenate([edges[pl.ds(r, at, stride=8), :] for r in range(6)], 1)
        groups[dy ^ y_at] = fold(nn(place, two(rows)))

    names.wait()

    def add_items(wanted):
        at = 0
        for ref, parts, dy, _ in items:

            def add_payload(p, carry, ref=ref, at=at):
                places = [pl.ds(pl.multiple_of(name_s[at + p, s] * CTRL, CTRL), CTRL) for s in range(GROUP)]
                first = pl.multiple_of(p * PAYLOAD_ROWS, 8)
                blocks = [ref[pl.ds(first + q * CTRL, CTRL), :] for q in range(GROUP // 2)]
                held = [sums[s % 2, places[s], :] + blocks[s // 2] for s in range(GROUP)]
                for s in range(GROUP):
                    sums[s % 2, places[s], :] = held[s]
                return carry

            if dy == wanted:
                lax.fori_loop(0, parts, add_payload, 0, unroll=2)
            at += parts

    @pl.when(y_at == 0)
    def _():
        add_items(0)
        add_items(1)

    @pl.when(y_at != 0)
    def _():
        add_items(1)
        add_items(0)


def smooth_kernel(
    items, per_owner, where_ref, adj_ref, coupling_ref, basis_ref, pair_ref, series_ref, edge_ref, scale_ref, *rest
):
    refs, rest = rest[: len(items)], rest[len(items) :]
    out_ref, sums, groups, halo_all, halo_rows, out_v, out_sem, *scratch = rest
    patches = adj_ref.shape[0]
    first_own = pl.multiple_of(where_ref[0] * per_owner, 8)
    items = [(ref, *item) for ref, item in zip(refs, items)]
    edge = edge_ref[...]
    scale = scale_ref[...]
    if len(items) == 1:
        groups[...] = jnp.zeros(groups.shape, F32)
    absorb(first_own, where_ref[1], per_owner, items, sums, groups, edge, scale, *scratch)
    base = groups[0] + groups[1]
    base = [base[:, 4 * CTRL * k : 4 * CTRL * (k + 1)] for k in range(3)]

    column = iota((patches, patches), 1)
    wide = 4 * CTRL

    def facing(adjacency):
        hits = [
            jnp.where(adjacency[:, s : s + 1] == column[: adjacency.shape[0]], 1.0, 0.0).astype(BF16)
            for s in range(4)
        ]
        return jnp.concatenate([hits[0], hits[2]], 0), jnp.concatenate([hits[1], hits[3]], 0)

    def halo(facing, edges):
        count = facing[0].shape[0] // 2
        low_lane = iota((count, LANES), 1) < CTRL
        first = fold(nn(facing[0], two(edges[:, LANES:])))
        second = fold(nn(facing[1], two(edges[:, :LANES])))
        return jnp.concatenate(
            [jnp.where(low_lane, x[:count], x[count:]) for x in (first, second)], 1
        )

    every = facing(adj_ref[...])
    halo0 = halo(every, base[0])
    effect0 = product(halo0, coupling_ref[...])
    edges1 = base[0] + base[1] + effect0[:, :wide]
    halo1 = halo(every, edges1)
    effect1 = product(halo1, coupling_ref[:, :wide])
    edges2 = base[0] + base[1] + base[2] + effect0[:, wide:] + effect1
    halo2 = halo(facing(adj_ref[pl.ds(first_own, per_owner), :]), edges2)
    halo_all[0] = halo1
    halo_all[1] = halo0
    for k in range(3):
        mine = halo2 if k == 0 else halo_all[k - 1, pl.ds(first_own, per_owner), :]
        factor = SMOOTHING * scale[2 * k : 2 * k + 1]
        for side in range(2):
            halo_rows[pl.ds(2 * k + side, per_owner, stride=8), :] = (
                mine[:, side * LANES : (side + 1) * LANES] * factor
            )
    zero = jnp.zeros((per_owner, LANES), F32)
    for r in (6, 7):
        halo_rows[pl.ds(r, per_owner, stride=8), :] = zero

    pairs = per_owner // 2
    both = pair_rows(edge)
    low8 = iota((8, LANES), 1) < CTRL
    along_rows, along_cols = [], []
    for pair in range(pairs):
        a = halo_rows[16 * pair : 16 * pair + 8, :]
        b = halo_rows[16 * pair + 8 : 16 * pair + 16, :]
        along_rows.append(jnp.where(low8, a, pltpu.roll(b, CTRL, 1)))
        low, high = (pltpu.roll(x, CTRL, 1) for x in (a, b)) if pair % 2 == 0 else (a, b)
        along_cols.append(jnp.concatenate([low, high], 0))
    from_rows = tn_product(edge, jnp.concatenate(along_rows, 1))
    low_half = iota((CTRL, LANES), 1) < CTRL
    basis_both = pair_ref[...]
    low16 = iota((16, LANES), 1) < CTRL
    along_cols = [jnp.where(low16, x, y) for x, y in zip(along_cols[::2], along_cols[1::2])]
    from_cols = tn_product(jnp.concatenate(along_cols, 1), both)
    step = pairs // CHUNKS if pairs % CHUNKS == 0 else pairs
    stores = []
    for start in range(0, pairs, step):
        turned = []
        for pair in range(start, start + step):
            a, b = [slice(patch * CTRL, (patch + 1) * CTRL) for patch in (2 * pair, 2 * pair + 1)]
            left = sums[0, a, :] + pltpu.roll(sums[1, a, :], CTRL, 1)
            right = pltpu.roll(sums[0, b, :], CTRL, 1) + sums[1, b, :]
            spectral = jnp.where(low_half, left, right) * series_ref[...]
            spectral = spectral + from_rows[:, pair * LANES : (pair + 1) * LANES]
            turned.append(spectral + from_cols[pair * CTRL : (pair + 1) * CTRL, :])
        turned = product(jnp.concatenate(turned, 0), basis_both)
        flat = jnp.concatenate([turned[at : at + CTRL] for at in range(0, step * CTRL, CTRL)], 1)
        done = product(basis_ref[...], flat)
        for pair in range(start, start + step):
            at = (pair - start) * LANES
            out_v[2 * pair] = done[:, at : at + CTRL]
            out_v[2 * pair + 1] = done[:, at + CTRL : at + LANES]
        part = pl.ds(2 * start, 2 * step)
        stores.append(pltpu.make_async_copy(out_v.at[part], out_ref.at[part], out_sem.at[len(stores)]))
        stores[-1].start()
    for store in stores:
        store.wait()


def tn_product(x, y):
    x_high, x_low = halves(x)
    y_high, y_low = halves(y)
    return tn(x_high, y_high) + (tn(x_low, y_high) + tn(x_high, y_low))


def smooth(payloads, items, where, adjacency, per_owner, const):
    patches = adjacency.shape[0]
    total = sum(item[0] for item in items)
    return pl.pallas_call(
        functools.partial(smooth_kernel, items, per_owner),
        out_shape=jax.ShapeDtypeStruct((per_owner, CTRL, CTRL), F32),
        in_specs=[SMEM] + [WHOLE] * 7 + [VMEM] * len(payloads),
        out_specs=HBM,
        scratch_shapes=[
            pltpu.VMEM((2, (per_owner + 2) * CTRL, LANES), F32),
            pltpu.VMEM((2, patches, 12 * CTRL), F32),
            pltpu.VMEM((2, patches, 4 * CTRL), F32),
            pltpu.VMEM((per_owner * 8, LANES), F32),
            pltpu.VMEM((per_owner, CTRL, CTRL), F32),
            pltpu.SemaphoreType.DMA((CHUNKS,)),
            pltpu.VMEM((total, LANES), jnp.int32),
            pltpu.SMEM((total, LANES), jnp.int32),
            pltpu.VMEM((total * GROUP * 8, LANES), F32),
            pltpu.VMEM((total * GROUP, LANES), F32),
            pltpu.SemaphoreType.DMA,
        ],
        compiler_params=params(32),
        name="smooth",
    )(
        where, adjacency, const["coupling"], const["basis"], const["basis_pair"], const["series"],
        const["edge_rows"], const["scale_rows"], *payloads,
    )


def far_line_kernel(where_ref, spread_ref, asked_ref, out_ref, own_ref, total_ref):
    owners = spread_ref.shape[0]
    line = owners // 2
    total = spread_ref[0]
    for o in range(1, owners):
        total = total + spread_ref[o]
    total_ref[...] = total
    own_ref[...] = total_ref[pl.ds(where_ref[2] // 2 * LINES, LINES), :]
    for z in range(line):
        dens = total[z * LINES : (z + 1) * LINES]
        held = asked_ref[2 * z + where_ref[1], 8:, 0:LANES]
        s, t, patch = [held[i * LINES : (i + 1) * LINES] for i in range(3)]
        start_s, weights_s = spline_weights(s)
        start_t, weights_t = spline_weights(t)
        left = spline_columns(in_line(start_s), [in_line(w) for w in weights_s])
        right = spline_columns(in_line(start_t), [in_line(w * dens) for w in weights_t])
        slots = [held[3 * LINES + i : 3 * LINES + i + 1, 0:1] for i in range(GROUP)]
        far = side_by_side(grids_of(left, right, in_line(patch), slots))
        out_ref[z * GRID_ROWS : (z + 1) * GRID_ROWS, :] = jnp.concatenate(far, 0)


def far_line(spread, asked, where):
    line = spread.shape[0] // 2
    return pl.pallas_call(
        far_line_kernel,
        out_shape=(
            jax.ShapeDtypeStruct((line * GRID_ROWS, LANES), F32),
            jax.ShapeDtypeStruct((LINES, LANES), F32),
        ),
        in_specs=[SMEM, VMEM, VMEM],
        out_specs=(VMEM, VMEM),
        scratch_shapes=[pltpu.VMEM((line * LINES, LANES), F32)],
        compiler_params=params(16),
        cost_estimate=pl.CostEstimate(flops=100_000_000, bytes_accessed=1_000_000, transcendentals=0),
        name="far_line",
    )(where, spread, asked)


def join_kernel(where_ref, far_ref, basis_ref, pair_ref, *refs):
    *parts, out_ref, near_ref = refs
    for k, part in enumerate(parts):
        near_ref[where_ref[2] // 2 ^ k] = part[...]
    blocks = [near_ref[z, 0:GRID_ROWS, :] + far_ref[z * GRID_ROWS : (z + 1) * GRID_ROWS, :] for z in range(len(parts))]
    blocks = to_spectral(jnp.concatenate(blocks, 0), basis_ref[...], pair_ref[...])
    for z in range(len(parts)):
        at = z * PAYLOAD_ROWS
        out_ref[at : at + GRID_ROWS, :] = blocks[z * GRID_ROWS : (z + 1) * GRID_ROWS]
        out_ref[at + GRID_ROWS : at + PAYLOAD_ROWS, :] = near_ref[z, GRID_ROWS:PAYLOAD_ROWS, :]


def join(parts, far, where, const):
    return pl.pallas_call(
        join_kernel,
        out_shape=jax.ShapeDtypeStruct((len(parts) * PAYLOAD_ROWS, LANES), F32),
        in_specs=[SMEM, VMEM, WHOLE, WHOLE] + [VMEM] * len(parts),
        out_specs=VMEM,
        scratch_shapes=[pltpu.VMEM((len(parts), PAYLOAD_ROWS, LANES), F32)],
        compiler_params=params(16),
        name="join",
    )(where, far, const["basis"], const["basis_pair"], *parts)


def over(axis, array, bit):
    count = lax.axis_size(axis)
    return lax.ppermute(array, axis, [(i, i ^ bit) for i in range(count)])


def gather_in_plane(here):
    half = here.shape[0] // 2
    beside_y = over("vol", here, 1)
    beside_x = over("dsg", here, 2)
    corner = [over("dsg", beside_y[:half], 2), over("vol", beside_x[half:], 1)]
    arrays = [here, beside_x, beside_y]
    arrays = [x for array in arrays for x in (array, over("dsg", array, 1))]
    arrays += corner + [over("dsg", c, 1) for c in corner]
    items = ((4, 0, 0), (4, 0, 0), (4, 0, 1), (4, 0, 1), (4, 1, 0), (4, 1, 0)) + ((2, 1, 1),) * 4
    return arrays, items


def per_device(
    fields, far_geom, far_block, far_cell, far_patch, near_geom, near_cell, near_patch, adjacency
):
    vol_count, dsg_count = lax.axis_size("vol"), lax.axis_size("dsg")
    far_count = far_cell.shape[0]
    capacity = 5 * far_count // (2 * vol_count)
    const = {name: jnp.asarray(value) for name, value in constants().items()}

    per_owner = adjacency.shape[0] // dsg_count
    staged = vol_count == 8 and dsg_count == 4 and far_count == LINES * LANES
    vol_at = lax.axis_index("vol")
    where = jnp.stack([lax.axis_index("dsg"), vol_at % 2 if staged else 0, vol_at]).astype(jnp.int32)
    near_patch, far_patch = near_patch.reshape(1, -1), far_patch.reshape(1, -1)
    request, place, slots = pack_requests(
        far_geom, far_block.reshape(1, -1), far_cell.reshape(1, -1), near_patch, far_patch, vol_count, capacity, staged
    )
    asked = lax.all_to_all(request, "vol", split_axis=0, concat_axis=0, tiled=True)
    near = near_payload(near_cell, fields, near_geom, near_patch, slots)
    asked, near = lax.optimization_barrier((asked, near))
    if staged:
        spread = far_spread(asked, fields)
        spread = lax.all_to_all(spread, "vol", split_axis=0, concat_axis=0, tiled=True)
        parts = [near] + [over("vol", near, 2 * k) for k in (1, 2, 3)]
        far, far_dens = far_line(spread, asked, where)
        here = join(parts, far, where, const)
        arrays, items = gather_in_plane(here)
    else:
        reply = lax.all_to_all(far_answers(asked, fields), "vol", split_axis=0, concat_axis=0, tiled=True)
        far_dens, payload = make_payload(reply, place, far_geom, far_patch, slots, near, const)
        arrays = [lax.all_gather(payload, ("vol", "dsg"), axis=0, tiled=True)]
        items = ((vol_count * dsg_count, 0, 0),)
    design = smooth(arrays, items, where, adjacency, per_owner, const)
    return far_dens.reshape(-1), design


def solution(mesh):
    return jax.shard_map(
        per_device,
        mesh=mesh,
        in_specs=(
            P("vol", None),
            P(None, ("vol", "dsg")),
            P(("vol", "dsg"), None),
            P(("vol", "dsg")),
            P(("vol", "dsg")),
            P(None, ("vol", "dsg")),
            P(("vol", "dsg")),
            P(("vol", "dsg")),
            P(),
        ),
        out_specs=(P(("vol", "dsg")), P("dsg", None, None)),
        check_vma=False,
    )
```

```python
import functools

import jax
import jax.numpy as jnp
import numpy as np
from jax import lax
from jax.experimental import pallas as pl
from jax.experimental.pallas import tpu as pltpu
from jax.sharding import PartitionSpec as P

CTRL = 64
GROUP = 4
LANES = 128
PENALTY = 4.0
SMOOTHING = 16.0
NO_PATCH = 1.0e6
GRID_ROWS = GROUP // 2 * CTRL
PAYLOAD_ROWS = GRID_ROWS + 2 * GROUP
LINES = 4
CHUNKS = 3
F32 = jnp.float32
BF16 = jnp.bfloat16
EXACT = lax.Precision.HIGHEST
VMEM = pl.BlockSpec(memory_space=pltpu.VMEM)
SMEM = pl.BlockSpec(memory_space=pltpu.SMEM)
ANY = pl.BlockSpec(memory_space=pl.ANY)
WHOLE = pl.BlockSpec()
HBM = pl.BlockSpec(memory_space=pltpu.HBM)


def params(megabytes):
    return pltpu.CompilerParams(vmem_limit_bytes=megabytes << 20)


def constants():
    order = np.arange(1, CTRL + 1)
    basis = np.sqrt(2.0 / (CTRL + 1)) * np.sin(np.pi * np.outer(order, order) / (CTRL + 1))
    eigen = 1.0 + SMOOTHING * (2.0 - 2.0 * np.cos(np.pi * order / (CTRL + 1)))
    damp = 1.0 / eigen
    keep = 1.0 - damp
    powers = [keep**k * damp for k in range(3)]
    ends = [basis[:, 0], basis[:, CTRL - 1]]
    edge_rows = np.zeros((8, CTRL))
    scale_rows = np.zeros((8, CTRL))
    for k in range(3):
        for side in range(2):
            edge_rows[2 * k + side] = powers[k] * ends[side]
            scale_rows[2 * k + side] = powers[k]
    series = sum(np.outer(keep**k * damp, keep**k * damp) for k in range(4))

    def coupling(k):
        f = powers[k]
        lane = [0, 2, 1, 3]
        out = np.zeros((4 * CTRL, 4 * CTRL))
        for a, side_in in enumerate(lane):
            for b, side_out in enumerate(lane):
                q_in, q_out = ends[side_in % 2], ends[side_out % 2]
                if side_in // 2 == side_out // 2:
                    block = np.diag(f * np.sum(q_in * q_out * f))
                else:
                    block = np.outer(q_out * f, q_in * f)
                out[a * CTRL : (a + 1) * CTRL, b * CTRL : (b + 1) * CTRL] = SMOOTHING * block
        return out

    return dict(
        basis=np.float32(basis),
        basis_pair=np.float32(np.kron(np.eye(2), basis)),
        edge_rows=np.float32(edge_rows),
        scale_rows=np.float32(np.concatenate([scale_rows, scale_rows], 1)),
        series=np.float32(np.concatenate([series, series], 1)),
        coupling=np.float32(np.concatenate([coupling(0), coupling(1)], 1)),
    )


def split3(x):
    high = x.astype(BF16).astype(F32)
    rest = x - high
    mid = rest.astype(BF16).astype(F32)
    return high, mid, rest - mid


def nt(a, b, **kw):
    return lax.dot_general(a, b, (((1,), (1,)), ((), ())), preferred_element_type=F32, **kw)


def nn(a, b, **kw):
    return lax.dot_general(a, b, (((1,), (0,)), ((), ())), preferred_element_type=F32, **kw)


def tn(a, b, **kw):
    return lax.dot_general(a, b, (((0,), (0,)), ((), ())), preferred_element_type=F32, **kw)


def iota(shape, axis):
    return lax.broadcasted_iota(jnp.int32, shape, axis)


def halves(x):
    high = x.astype(BF16)
    return high, (x - high.astype(F32)).astype(BF16)


def two(x):
    return jnp.concatenate(halves(x), 1)


def fold(x):
    half = x.shape[1] // 2
    return x[:, :half] + x[:, half:]


def product(x, y):
    x_high, x_low = halves(x)
    y_high, y_low = halves(y)
    return nn(x_high, y_high) + (nn(x_low, y_high) + nn(x_high, y_low))


def nt_product(x, y):
    x_high, x_low = halves(x)
    y_high, y_low = halves(y)
    return nt(x_high, y_high) + (nt(x_low, y_high) + nt(x_high, y_low))


def fetch(pairs, sem):
    copies = [pltpu.make_async_copy(a, b, sem.at[i]) for i, (a, b) in enumerate(pairs)]
    for copy in copies:
        copy.start()
    for copy in copies:
        copy.wait()


def pack_kernel(
    capacity, geom_in, block_in, cell_in, near_in, far_in, request_ref, place_ref, slot_ref,
    geom_ref, block_ref, cell_ref, near_ref, far_ref, sem,
):
    fetch([(geom_in, geom_ref), (block_in, block_ref), (cell_in, cell_ref), (near_in, near_ref), (far_in, far_ref)], sem)
    near, far = near_ref[...].astype(F32), far_ref[...].astype(F32)
    slots = []
    last = jnp.full((1, 1), -1.0, F32)
    for _ in range(GROUP):
        a = jnp.min(jnp.where(near > last, near, NO_PATCH), axis=1, keepdims=True)
        b = jnp.min(jnp.where(far > last, far, NO_PATCH), axis=1, keepdims=True)
        last = jnp.minimum(a, b)
        slots.append(jnp.broadcast_to(last, (1, LANES)))
    slot_ref[...] = jnp.concatenate(slots + slots, 0)
    owners = request_ref.shape[0]
    count = geom_ref.shape[1]
    block = block_ref[...]
    owner_id = iota((owners, count), 0)
    chosen = jnp.where(owner_id == block, 1.0, 0.0).astype(F32)
    earlier = jnp.where(iota((count, count), 0) < iota((count, count), 1), 1.0, 0.0).astype(BF16)
    rank = nn(chosen.astype(BF16), earlier)
    place = jnp.sum(chosen * (rank + (capacity * owner_id).astype(F32)), axis=0, keepdims=True)
    place = place.astype(jnp.int32)
    place_ref[...] = place
    row = iota((8, count), 0)
    number = (iota((8, count), 1) + 1).astype(F32)
    values = jnp.where(row < 6, geom_ref[...], jnp.where(row == 6, cell_ref[...].astype(F32), number))
    high, mid, low = split3(values)
    parts = jnp.concatenate([high, mid, low], 0).astype(BF16)
    put = jnp.where(iota((owners * capacity, count), 0) == place, 1.0, 0.0).astype(BF16)
    packed = nt(parts, put)
    packed = (packed[16:24] + packed[8:16]) + packed[0:8]
    for owner in range(owners):
        request_ref[owner, 0:8, :] = packed[:, owner * capacity : (owner + 1) * capacity]
    if request_ref.shape[1] > 8:
        own = [in_rows(x) for x in (geom_ref[6:7, :], geom_ref[7:8, :], far)] + [slot_ref[0:GROUP, :]]
        own = jnp.concatenate(own, 0)
        for owner in range(owners):
            request_ref[owner, 8:, 0:LANES] = own
            request_ref[owner, 8:, LANES:] = jnp.zeros((own.shape[0], capacity - LANES), F32)


def pack_requests(far_geom, far_block, far_cell, near_patch, far_patch, owners, capacity, staged):
    count = far_geom.shape[1]
    return pl.pallas_call(
        functools.partial(pack_kernel, capacity),
        out_shape=(
            jax.ShapeDtypeStruct((owners, 8 + staged * (3 * LINES + GROUP), capacity), F32),
            jax.ShapeDtypeStruct((1, count), jnp.int32),
            jax.ShapeDtypeStruct((8, LANES), F32),
        ),
        in_specs=[HBM] * 5,
        out_specs=(VMEM, VMEM, VMEM),
        scratch_shapes=[
            pltpu.VMEM((8, count), F32),
            pltpu.VMEM((1, count), jnp.int32),
            pltpu.VMEM((1, count), jnp.int32),
            pltpu.VMEM(near_patch.shape, jnp.int32),
            pltpu.VMEM(far_patch.shape, jnp.int32),
            pltpu.SemaphoreType.DMA((5,)),
        ],
        compiler_params=params(60),
        name="pack_requests",
    )(far_geom, far_block, far_cell, near_patch, far_patch)


def gather_rows(cells, fields_ref, rows_ref, count):
    unroll = 64

    def step(i, carry):
        for u in range(unroll):
            p = i * unroll + u
            rows_ref[pl.ds(p, 1), :] = fields_ref[pl.ds(cells(p), 1), :]
        return carry

    lax.fori_loop(0, count // unroll, step, 0)


def bernstein(t):
    u = 1.0 - t
    uu, tt = u * u, t * t
    values = [uu * u, 3.0 * t * uu, 3.0 * tt * u, tt * t]
    tu = 6.0 * t * u
    slopes = [-3.0 * uu, 3.0 * uu - tu, tu - 3.0 * tt, 3.0 * tt]
    return values, slopes


def tile_density(columns, geom):
    row = iota((8, LANES), 0)
    wide = [jnp.broadcast_to(geom[r : r + 1], (8, LANES)) for r in range(3)]
    x_val, x_der = bernstein(wide[0])
    y_val, y_der = bernstein(wide[1])
    z_val, z_der = bernstein(wide[2])
    k = row % 4

    def by_k(v):
        return jnp.where(k == 0, v[0], jnp.where(k == 1, v[1], jnp.where(k == 2, v[2], v[3])))

    def by_j(v, m):
        return jnp.where(row < 4, v[2 * m], v[2 * m + 1])

    z_v, z_d = by_k(z_val), by_k(z_der)
    yz = [by_j(y_val, m) * z_v for m in range(2)]
    dyz = [by_j(y_der, m) * z_v for m in range(2)]
    ydz = [by_j(y_val, m) * z_d for m in range(2)]
    sums = []
    for half in range(2):
        total = [None] * 4
        for i in range(4):
            at = half * 64 + i * 16
            first, second = columns[at : at + 8], columns[at + 8 : at + 16]
            plain = first * yz[0] + second * yz[1]
            along_y = first * dyz[0] + second * dyz[1]
            along_z = first * ydz[0] + second * ydz[1]
            terms = [x_val[i] * plain, x_der[i] * plain, x_val[i] * along_y, x_val[i] * along_z]
            total = [t if s is None else s + t for s, t in zip(total, terms)]
        sums.append([jnp.sum(t, axis=0, keepdims=True) for t in total])
    state, adjoint = sums
    n = [geom[3 + r : 4 + r] for r in range(3)]
    normal_sq = n[0] * n[0] + n[1] * n[1] + n[2] * n[2]
    inner = state[1] * adjoint[1] + state[2] * adjoint[2] + state[3] * adjoint[3]
    along_s = state[1] * n[0] + state[2] * n[1] + state[3] * n[2]
    along_a = adjoint[1] * n[0] + adjoint[2] * n[1] + adjoint[3] * n[2]
    return normal_sq * inner - 2.0 * along_s * along_a + PENALTY * normal_sq * state[0] * adjoint[0]


def densities(rows_ref, geom_ref, out_ref, count):
    def step(tile, carry):
        at = pl.multiple_of(tile * LANES, LANES)
        columns = rows_ref[pl.ds(at, LANES), :].T
        out_ref[:, pl.ds(at, LANES)] = tile_density(columns, geom_ref[:, pl.ds(at, LANES)])
        return carry

    tiles = count // LANES
    lax.fori_loop(0, tiles, step, 0, unroll=next(n for n in (16, 10, 8, 5, 4, 2, 1) if tiles % n == 0))


def near_kernel(first, cell_in, fields_in, geom_in, out_ref, cell_ref, fields_ref, geom_ref, rows_ref, sem):
    count = out_ref.shape[1]
    part = pl.ds(first, count)
    fetch([(cell_in.at[part], cell_ref), (geom_in.at[:, part], geom_ref), (fields_in, fields_ref)], sem)
    gather_rows(lambda p: cell_ref[p], fields_ref, rows_ref, count)
    densities(rows_ref, geom_ref, out_ref, count)


def far_densities(request_in, fields_ref, request_ref, query_ref, cell_v, cell_s, rows_ref, dens_ref, sems, sem):
    owners, _, capacity = request_in.shape
    count = owners * capacity
    fetch([(request_in.at[:, pl.ds(0, 8), :], request_ref)], sems)
    for o in range(owners):
        query_ref[:, o * capacity : (o + 1) * capacity] = request_ref[o]
    cell_v[...] = query_ref[6:7, :].astype(jnp.int32)
    copy = pltpu.make_async_copy(cell_v, cell_s, sem)
    copy.start()
    copy.wait()
    gather_rows(lambda p: cell_s[0, p], fields_ref, rows_ref, count)
    densities(rows_ref, query_ref, dens_ref, count)


def far_kernel(request_in, fields_ref, out_ref, *scratch):
    owners, _, capacity = request_in.shape
    far_densities(request_in, fields_ref, *scratch)
    dens_ref = scratch[5]
    for o in range(owners):
        out_ref[o] = dens_ref[:, o * capacity : (o + 1) * capacity]


def in_rows(x):
    return jnp.concatenate([x[:, i : i + LANES] for i in range(0, x.shape[1], LANES)], 0)


def in_line(x):
    return jnp.concatenate([x[i : i + 1, :] for i in range(x.shape[0])], 1)


def far_spread_kernel(request_in, fields_ref, out_ref, *scratch):
    owners, _, capacity = request_in.shape
    far_densities(request_in, fields_ref, *scratch)
    query_ref, dens_ref = scratch[1], scratch[5]
    number = iota((LINES * LANES, capacity), 0) + 1
    found = []
    for o in range(owners):
        part = slice(o * capacity, (o + 1) * capacity)
        place = jnp.where(number == query_ref[7:8, part].astype(jnp.int32), 1.0, 0.0).astype(BF16)
        high, mid, low = split3(dens_ref[:, part])
        parts = jnp.concatenate([high, mid, low, jnp.zeros((5, capacity), F32)], 0).astype(BF16)
        got = nt(parts, place)
        found.append(in_rows((got[2:3] + got[1:2]) + got[0:1]))
    lines = [jnp.concatenate(found[y::2], 0) for y in range(2)]
    for o in range(owners):
        out_ref[o] = lines[o % 2]


def far_scratch(requests):
    owners, _, capacity = requests.shape
    count = owners * capacity
    return [
        pltpu.VMEM((owners, 8, capacity), F32),
        pltpu.VMEM((8, count), F32),
        pltpu.VMEM((1, count), jnp.int32),
        pltpu.SMEM((1, count), jnp.int32),
        pltpu.VMEM((count, LANES), F32),
        pltpu.VMEM((1, count), F32),
        pltpu.SemaphoreType.DMA((1,)),
        pltpu.SemaphoreType.DMA,
    ]


def far_answers(requests, fields):
    owners, _, capacity = requests.shape
    return pl.pallas_call(
        far_kernel,
        out_shape=jax.ShapeDtypeStruct((owners, 1, capacity), F32),
        in_specs=[ANY, VMEM],
        out_specs=VMEM,
        scratch_shapes=far_scratch(requests),
        compiler_params=params(24),
        name="far_answers",
    )(requests, fields)


def far_spread(requests, fields):
    owners = requests.shape[0]
    return pl.pallas_call(
        far_spread_kernel,
        out_shape=jax.ShapeDtypeStruct((owners, owners // 2 * LINES, LANES), F32),
        in_specs=[ANY, VMEM],
        out_specs=VMEM,
        scratch_shapes=far_scratch(requests),
        compiler_params=params(24),
        cost_estimate=pl.CostEstimate(flops=40_000_000, bytes_accessed=4_000_000, transcendentals=0),
        name="far_spread",
    )(requests, fields)


def spline_weights(param):
    scaled = param * float(CTRL - 3)
    start = jnp.clip(jnp.floor(scaled), 0.0, float(CTRL - 4))
    x = scaled - start
    u = 1.0 - x
    cubed, squared = x * x * x, x * x
    weights = [
        u * u * u * (1.0 / 6.0),
        (3.0 * cubed - 6.0 * squared + 4.0) * (1.0 / 6.0),
        (-3.0 * cubed + 3.0 * squared + 3.0 * x + 1.0) * (1.0 / 6.0),
        cubed * (1.0 / 6.0),
    ]
    return start.astype(jnp.int32), weights


def spline_columns(start, weights):
    off = iota((CTRL, start.shape[1]), 0) - start
    out = jnp.zeros(off.shape, F32)
    for m in range(4):
        out = jnp.where(off == m, weights[m], out)
    return out


def slot_grids(density, s, t, patch, slots):
    start, weights = spline_weights(t)
    right = spline_columns(start, [w * density for w in weights])
    return grids_of(spline_columns(*spline_weights(s)), right, patch, slots)


def grids_of(left, right, patch, slots):
    left_high, left_low = halves(left)
    right_high, right_low = halves(right)
    masks = [jnp.where(patch == slot, 1.0, 0.0).astype(BF16) for slot in slots]
    high = jnp.concatenate([left_high * m for m in masks], 0)
    low = jnp.concatenate([left_low * m for m in masks], 0)
    return fold(nt(high, jnp.concatenate([right_high, right_low], 0))) + nt(low, right_high)


def side_by_side(grids):
    return [
        jnp.concatenate([grids[a * CTRL : (a + 1) * CTRL], grids[(a + 1) * CTRL : (a + 2) * CTRL]], 1)
        for a in range(0, GROUP, 2)
    ]


def near_payload_kernel(
    cell_in, fields_in, geom_in, near_in, slot_in, out_ref,
    near_ref, slot_ref, dens_ref, cell_ref, fields_ref, geom_ref, rows_ref, more, sem,
):
    others = [(near_in, near_ref), (slot_in, slot_ref)]
    others = [pltpu.make_async_copy(a, b, more.at[i]) for i, (a, b) in enumerate(others)]
    for copy in others:
        copy.start()
    near_kernel(0, cell_in, fields_in, geom_in, dens_ref, cell_ref, fields_ref, geom_ref, rows_ref, sem)
    for copy in others:
        copy.wait()
    slots = [slot_ref[s : s + 1, 0:1] for s in range(GROUP)]
    near = near_ref[...].astype(F32)
    grids = slot_grids(dens_ref[...], geom_ref[6:7, :], geom_ref[7:8, :], near, slots)
    lane = iota((1, LANES), 1)
    names = jnp.zeros((1, LANES), F32)
    for s in range(GROUP):
        names = jnp.where(lane == s, slots[s], names)
    out_ref[...] = jnp.concatenate(side_by_side(grids) + [slot_ref[0:GROUP, :]] + [names] * GROUP, 0)


def near_payload(near_cell, fields, near_geom, near_patch, slots):
    count = near_geom.shape[1]
    return pl.pallas_call(
        near_payload_kernel,
        out_shape=jax.ShapeDtypeStruct((PAYLOAD_ROWS, LANES), F32),
        in_specs=[HBM] * 5,
        out_specs=VMEM,
        scratch_shapes=[
            pltpu.VMEM(near_patch.shape, jnp.int32),
            pltpu.VMEM(slots.shape, F32),
            pltpu.VMEM((1, count), F32),
            pltpu.SMEM((count,), jnp.int32),
            pltpu.VMEM(fields.shape, F32),
            pltpu.VMEM((8, count), F32),
            pltpu.VMEM((count, LANES), F32),
            pltpu.SemaphoreType.DMA((2,)),
            pltpu.SemaphoreType.DMA((3,)),
        ],
        compiler_params=params(60),
        cost_estimate=pl.CostEstimate(flops=100_000_000, bytes_accessed=4_000_000, transcendentals=0),
        name="near_payload",
    )(near_cell, fields, near_geom, near_patch, slots)


def to_spectral(blocks, basis, basis_pair):
    turned = product(blocks, basis_pair)
    parts = range(0, blocks.shape[0], CTRL)
    turned = product(basis, jnp.concatenate([turned[at : at + CTRL] for at in parts], 1))
    return jnp.concatenate([turned[:, 2 * at : 2 * at + LANES] for at in parts], 0)


def payload_kernel(
    reply_ref, place_ref, geom_ref, far_ref, slot_ref, near_ref, basis_ref, pair_ref, dens_ref, out_ref, flat_ref
):
    owners, _, capacity = reply_ref.shape
    count = geom_ref.shape[1]
    for o in range(owners):
        flat_ref[:, o * capacity : (o + 1) * capacity] = reply_ref[o]
    high, mid, low = split3(flat_ref[...])
    parts = jnp.concatenate([high, mid, low, jnp.zeros((5, owners * capacity), F32)], 0).astype(BF16)
    put = jnp.where(iota((owners * capacity, count), 0) == place_ref[...], 1.0, 0.0).astype(BF16)
    got = nn(parts, put)
    dens = (got[2:3] + got[1:2]) + got[0:1]
    dens_ref[...] = dens
    slots = [slot_ref[s : s + 1, 0:1] for s in range(GROUP)]
    grids = slot_grids(dens, geom_ref[6:7, :], geom_ref[7:8, :], far_ref[...].astype(F32), slots)
    out_ref[GRID_ROWS:PAYLOAD_ROWS, :] = near_ref[GRID_ROWS:PAYLOAD_ROWS, :]
    blocks = near_ref[0:GRID_ROWS, :] + jnp.concatenate(side_by_side(grids), 0)
    out_ref[0:GRID_ROWS, :] = to_spectral(blocks, basis_ref[...], pair_ref[...])


def make_payload(reply, place, far_geom, far_patch, slots, near, const):
    owners, _, capacity = reply.shape
    count = far_geom.shape[1]
    return pl.pallas_call(
        payload_kernel,
        out_shape=(
            jax.ShapeDtypeStruct((1, count), F32),
            jax.ShapeDtypeStruct((PAYLOAD_ROWS, LANES), F32),
        ),
        in_specs=[VMEM] * 6 + [WHOLE] * 2,
        out_specs=(VMEM, VMEM),
        scratch_shapes=[pltpu.VMEM((1, owners * capacity), F32)],
        compiler_params=params(24),
        name="make_payload",
    )(reply, place, far_geom, far_patch, slots, near, const["basis"], const["basis_pair"])


def pair_rows(edge):
    blank = jnp.zeros((8, CTRL), F32)
    return jnp.concatenate([jnp.concatenate([edge, blank], 1), jnp.concatenate([blank, edge], 1)], 0)


def absorb(first_own, y_at, per_owner, items, sums, groups, edge, scale, name_v, name_s, edges, where_to, name_sem):
    patches = groups.shape[1]
    low8 = iota((8, LANES), 1) < CTRL
    spare = per_owner + iota((1, LANES), 1) // 2 % 2
    at = 0
    for ref, parts, _, _ in items:
        for p in range(parts):
            last = (p + 1) * PAYLOAD_ROWS - 1
            patch = ref[last : last + 1, :].astype(jnp.int32) - first_own
            name_v[at : at + 1, :] = jnp.where((patch >= 0) & (patch < per_owner), patch, spare)
            at += 1
    names = pltpu.make_async_copy(name_v, name_s, name_sem)
    names.start()

    sums[...] = jnp.zeros(sums.shape, F32)
    edge_high, edge_low = halves(edge)
    edge_both = jnp.concatenate([edge_high, edge_low], 0)
    both_high, both_low = halves(pair_rows(edge))
    both_both = jnp.concatenate([both_high, both_low], 0)
    for dy in sorted({dy for _, _, dy, _ in items}):
        at = 0
        chunks = [(ref, p) for ref, parts, own, _ in items if own == dy for p in range(0, parts, 2)]
        for ref, start in chunks:
            blocks = []
            for p in (start, start + 1):
                row = p * PAYLOAD_ROWS
                blocks += [halves(ref[row + q * CTRL : row + (q + 1) * CTRL, :]) for q in range(GROUP // 2)]
                row += GRID_ROWS
                where_to[at + GROUP * (p - start) : at + GROUP * (p - start + 1), :] = ref[row : row + GROUP, :]
            high, low = [jnp.concatenate(x, 1) for x in zip(*blocks)]
            along_rows = nn(edge_both, high)
            along_rows = (along_rows[:8] + along_rows[8:]) + nn(edge_high, low)
            high, low = [jnp.concatenate(x, 0) for x in zip(*blocks)]
            along_cols = nt(both_both, high)
            along_cols = (along_cols[:16] + along_cols[16:]) + nt(both_high, low)
            for s in range(2 * GROUP):
                q = s // 2
                first = along_rows[:, q * LANES : (q + 1) * LANES]
                second = along_cols[8 * (s % 2) : 8 * (s % 2) + 8, q // 2 * LANES : (q // 2 + 1) * LANES]
                if s % 2:
                    first = pltpu.roll(first, CTRL, 1)
                if q % 2 == 0:
                    second = pltpu.roll(second, CTRL, 1)
                edges[8 * at : 8 * at + 8, :] = jnp.where(low8, first, second) * scale
                at += 1
        lane = iota((at, LANES), 1)
        place = jnp.where(lane == where_to[:at, :].astype(jnp.int32), 1.0, 0.0).T[:patches].astype(BF16)
        rows = jnp.concatenate([edges[pl.ds(r, at, stride=8), :] for r in range(6)], 1)
        groups[dy ^ y_at] = fold(nn(place, two(rows)))

    names.wait()

    def add_items(wanted):
        at = 0
        for ref, parts, dy, _ in items:

            def add_payload(p, carry, ref=ref, at=at):
                places = [pl.ds(pl.multiple_of(name_s[at + p, s] * CTRL, CTRL), CTRL) for s in range(GROUP)]
                first = pl.multiple_of(p * PAYLOAD_ROWS, 8)
                blocks = [ref[pl.ds(first + q * CTRL, CTRL), :] for q in range(GROUP // 2)]
                held = [sums[s % 2, places[s], :] + blocks[s // 2] for s in range(GROUP)]
                for s in range(GROUP):
                    sums[s % 2, places[s], :] = held[s]
                return carry

            if dy == wanted:
                lax.fori_loop(0, parts, add_payload, 0, unroll=2)
            at += parts

    @pl.when(y_at == 0)
    def _():
        add_items(0)
        add_items(1)

    @pl.when(y_at != 0)
    def _():
        add_items(1)
        add_items(0)


def smooth_kernel(
    items, per_owner, where_ref, adj_ref, coupling_ref, basis_ref, pair_ref, series_ref, edge_ref, scale_ref, *rest
):
    refs, rest = rest[: len(items)], rest[len(items) :]
    out_ref, sums, groups, halo_all, halo_rows, out_v, out_sem, *scratch = rest
    patches = adj_ref.shape[0]
    first_own = pl.multiple_of(where_ref[0] * per_owner, 8)
    items = [(ref, *item) for ref, item in zip(refs, items)]
    edge = edge_ref[...]
    scale = scale_ref[...]
    if len(items) == 1:
        groups[...] = jnp.zeros(groups.shape, F32)
    absorb(first_own, where_ref[1], per_owner, items, sums, groups, edge, scale, *scratch)
    base = groups[0] + groups[1]
    base = [base[:, 4 * CTRL * k : 4 * CTRL * (k + 1)] for k in range(3)]

    column = iota((patches, patches), 1)
    wide = 4 * CTRL

    def facing(adjacency):
        hits = [
            jnp.where(adjacency[:, s : s + 1] == column[: adjacency.shape[0]], 1.0, 0.0).astype(BF16)
            for s in range(4)
        ]
        return jnp.concatenate([hits[0], hits[2]], 0), jnp.concatenate([hits[1], hits[3]], 0)

    def halo(facing, edges):
        count = facing[0].shape[0] // 2
        low_lane = iota((count, LANES), 1) < CTRL
        first = fold(nn(facing[0], two(edges[:, LANES:])))
        second = fold(nn(facing[1], two(edges[:, :LANES])))
        return jnp.concatenate(
            [jnp.where(low_lane, x[:count], x[count:]) for x in (first, second)], 1
        )

    every = facing(adj_ref[...])
    halo0 = halo(every, base[0])
    effect0 = product(halo0, coupling_ref[...])
    edges1 = base[0] + base[1] + effect0[:, :wide]
    halo1 = halo(every, edges1)
    effect1 = product(halo1, coupling_ref[:, :wide])
    edges2 = base[0] + base[1] + base[2] + effect0[:, wide:] + effect1
    halo2 = halo(facing(adj_ref[pl.ds(first_own, per_owner), :]), edges2)
    halo_all[0] = halo1
    halo_all[1] = halo0
    for k in range(3):
        mine = halo2 if k == 0 else halo_all[k - 1, pl.ds(first_own, per_owner), :]
        factor = SMOOTHING * scale[2 * k : 2 * k + 1]
        for side in range(2):
            halo_rows[pl.ds(2 * k + side, per_owner, stride=8), :] = (
                mine[:, side * LANES : (side + 1) * LANES] * factor
            )
    zero = jnp.zeros((per_owner, LANES), F32)
    for r in (6, 7):
        halo_rows[pl.ds(r, per_owner, stride=8), :] = zero

    pairs = per_owner // 2
    both = pair_rows(edge)
    low8 = iota((8, LANES), 1) < CTRL
    along_rows, along_cols = [], []
    for pair in range(pairs):
        a = halo_rows[16 * pair : 16 * pair + 8, :]
        b = halo_rows[16 * pair + 8 : 16 * pair + 16, :]
        along_rows.append(jnp.where(low8, a, pltpu.roll(b, CTRL, 1)))
        low, high = (pltpu.roll(x, CTRL, 1) for x in (a, b)) if pair % 2 == 0 else (a, b)
        along_cols.append(jnp.concatenate([low, high], 0))
    from_rows = tn_product(edge, jnp.concatenate(along_rows, 1))
    low_half = iota((CTRL, LANES), 1) < CTRL
    basis_both = pair_ref[...]
    low16 = iota((16, LANES), 1) < CTRL
    along_cols = [jnp.where(low16, x, y) for x, y in zip(along_cols[::2], along_cols[1::2])]
    from_cols = tn_product(jnp.concatenate(along_cols, 1), both)
    step = pairs // CHUNKS if pairs % CHUNKS == 0 else pairs
    stores = []
    for start in range(0, pairs, step):
        turned = []
        for pair in range(start, start + step):
            a, b = [slice(patch * CTRL, (patch + 1) * CTRL) for patch in (2 * pair, 2 * pair + 1)]
            left = sums[0, a, :] + pltpu.roll(sums[1, a, :], CTRL, 1)
            right = pltpu.roll(sums[0, b, :], CTRL, 1) + sums[1, b, :]
            spectral = jnp.where(low_half, left, right) * series_ref[...]
            spectral = spectral + from_rows[:, pair * LANES : (pair + 1) * LANES]
            turned.append(spectral + from_cols[pair * CTRL : (pair + 1) * CTRL, :])
        turned = product(jnp.concatenate(turned, 0), basis_both)
        flat = jnp.concatenate([turned[at : at + CTRL] for at in range(0, step * CTRL, CTRL)], 1)
        done = product(basis_ref[...], flat)
        for pair in range(start, start + step):
            at = (pair - start) * LANES
            out_v[2 * pair] = done[:, at : at + CTRL]
            out_v[2 * pair + 1] = done[:, at + CTRL : at + LANES]
        part = pl.ds(2 * start, 2 * step)
        stores.append(pltpu.make_async_copy(out_v.at[part], out_ref.at[part], out_sem.at[len(stores)]))
        stores[-1].start()
    for store in stores:
        store.wait()


def tn_product(x, y):
    x_high, x_low = halves(x)
    y_high, y_low = halves(y)
    return tn(x_high, y_high) + (tn(x_low, y_high) + tn(x_high, y_low))


def smooth(payloads, items, where, adjacency, per_owner, const):
    patches = adjacency.shape[0]
    total = sum(item[0] for item in items)
    return pl.pallas_call(
        functools.partial(smooth_kernel, items, per_owner),
        out_shape=jax.ShapeDtypeStruct((per_owner, CTRL, CTRL), F32),
        in_specs=[SMEM] + [WHOLE] * 7 + [VMEM] * len(payloads),
        out_specs=HBM,
        scratch_shapes=[
            pltpu.VMEM((2, (per_owner + 2) * CTRL, LANES), F32),
            pltpu.VMEM((2, patches, 12 * CTRL), F32),
            pltpu.VMEM((2, patches, 4 * CTRL), F32),
            pltpu.VMEM((per_owner * 8, LANES), F32),
            pltpu.VMEM((per_owner, CTRL, CTRL), F32),
            pltpu.SemaphoreType.DMA((CHUNKS,)),
            pltpu.VMEM((total, LANES), jnp.int32),
            pltpu.SMEM((total, LANES), jnp.int32),
            pltpu.VMEM((total * GROUP * 8, LANES), F32),
            pltpu.VMEM((total * GROUP, LANES), F32),
            pltpu.SemaphoreType.DMA,
        ],
        compiler_params=params(32),
        name="smooth",
    )(
        where, adjacency, const["coupling"], const["basis"], const["basis_pair"], const["series"],
        const["edge_rows"], const["scale_rows"], *payloads,
    )


def far_line_kernel(where_ref, spread_ref, asked_ref, out_ref, own_ref, total_ref):
    owners = spread_ref.shape[0]
    line = owners // 2
    total = spread_ref[0]
    for o in range(1, owners):
        total = total + spread_ref[o]
    total_ref[...] = total
    own_ref[...] = total_ref[pl.ds(where_ref[2] // 2 * LINES, LINES), :]
    for z in range(line):
        dens = total[z * LINES : (z + 1) * LINES]
        held = asked_ref[2 * z + where_ref[1], 8:, 0:LANES]
        s, t, patch = [held[i * LINES : (i + 1) * LINES] for i in range(3)]
        start_s, weights_s = spline_weights(s)
        start_t, weights_t = spline_weights(t)
        left = spline_columns(in_line(start_s), [in_line(w) for w in weights_s])
        right = spline_columns(in_line(start_t), [in_line(w * dens) for w in weights_t])
        slots = [held[3 * LINES + i : 3 * LINES + i + 1, 0:1] for i in range(GROUP)]
        far = side_by_side(grids_of(left, right, in_line(patch), slots))
        out_ref[z * GRID_ROWS : (z + 1) * GRID_ROWS, :] = jnp.concatenate(far, 0)


def far_line(spread, asked, where):
    line = spread.shape[0] // 2
    return pl.pallas_call(
        far_line_kernel,
        out_shape=(
            jax.ShapeDtypeStruct((line * GRID_ROWS, LANES), F32),
            jax.ShapeDtypeStruct((LINES, LANES), F32),
        ),
        in_specs=[SMEM, VMEM, VMEM],
        out_specs=(VMEM, VMEM),
        scratch_shapes=[pltpu.VMEM((line * LINES, LANES), F32)],
        compiler_params=params(16),
        cost_estimate=pl.CostEstimate(flops=100_000_000, bytes_accessed=1_000_000, transcendentals=0),
        name="far_line",
    )(where, spread, asked)


def join_kernel(where_ref, far_ref, basis_ref, pair_ref, *refs):
    *parts, out_ref, near_ref = refs
    for k, part in enumerate(parts):
        near_ref[where_ref[2] // 2 ^ k] = part[...]
    blocks = [near_ref[z, 0:GRID_ROWS, :] + far_ref[z * GRID_ROWS : (z + 1) * GRID_ROWS, :] for z in range(len(parts))]
    blocks = to_spectral(jnp.concatenate(blocks, 0), basis_ref[...], pair_ref[...])
    for z in range(len(parts)):
        at = z * PAYLOAD_ROWS
        out_ref[at : at + GRID_ROWS, :] = blocks[z * GRID_ROWS : (z + 1) * GRID_ROWS]
        out_ref[at + GRID_ROWS : at + PAYLOAD_ROWS, :] = near_ref[z, GRID_ROWS:PAYLOAD_ROWS, :]


def join(parts, far, where, const):
    return pl.pallas_call(
        join_kernel,
        out_shape=jax.ShapeDtypeStruct((len(parts) * PAYLOAD_ROWS, LANES), F32),
        in_specs=[SMEM, VMEM, WHOLE, WHOLE] + [VMEM] * len(parts),
        out_specs=VMEM,
        scratch_shapes=[pltpu.VMEM((len(parts), PAYLOAD_ROWS, LANES), F32)],
        compiler_params=params(16),
        name="join",
    )(where, far, const["basis"], const["basis_pair"], *parts)


def over(axis, array, bit):
    count = lax.axis_size(axis)
    return lax.ppermute(array, axis, [(i, i ^ bit) for i in range(count)])


def gather_in_plane(here):
    half = here.shape[0] // 2
    beside_y = over("vol", here, 1)
    beside_x = over("dsg", here, 2)
    corner = [over("dsg", beside_y[:half], 2), over("vol", beside_x[half:], 1)]
    arrays = [here, beside_x, beside_y]
    arrays = [x for array in arrays for x in (array, over("dsg", array, 1))]
    arrays += corner + [over("dsg", c, 1) for c in corner]
    items = ((4, 0, 0), (4, 0, 0), (4, 0, 1), (4, 0, 1), (4, 1, 0), (4, 1, 0)) + ((2, 1, 1),) * 4
    return arrays, items


def per_device(
    fields, far_geom, far_block, far_cell, far_patch, near_geom, near_cell, near_patch, adjacency
):
    vol_count, dsg_count = lax.axis_size("vol"), lax.axis_size("dsg")
    far_count = far_cell.shape[0]
    capacity = 5 * far_count // (2 * vol_count)
    const = {name: jnp.asarray(value) for name, value in constants().items()}

    per_owner = adjacency.shape[0] // dsg_count
    staged = vol_count == 8 and dsg_count == 4 and far_count == LINES * LANES
    vol_at = lax.axis_index("vol")
    where = jnp.stack([lax.axis_index("dsg"), vol_at % 2 if staged else 0, vol_at]).astype(jnp.int32)
    near_patch, far_patch = near_patch.reshape(1, -1), far_patch.reshape(1, -1)
    request, place, slots = pack_requests(
        far_geom, far_block.reshape(1, -1), far_cell.reshape(1, -1), near_patch, far_patch, vol_count, capacity, staged
    )
    asked = lax.all_to_all(request, "vol", split_axis=0, concat_axis=0, tiled=True)
    near = near_payload(near_cell, fields, near_geom, near_patch, slots)
    asked, near = lax.optimization_barrier((asked, near))
    if staged:
        spread = far_spread(asked, fields)
        spread = lax.all_to_all(spread, "vol", split_axis=0, concat_axis=0, tiled=True)
        parts = [near] + [over("vol", near, 2 * k) for k in (1, 2, 3)]
        far, far_dens = far_line(spread, asked, where)
        here = join(parts, far, where, const)
        arrays, items = gather_in_plane(here)
    else:
        reply = lax.all_to_all(far_answers(asked, fields), "vol", split_axis=0, concat_axis=0, tiled=True)
        far_dens, payload = make_payload(reply, place, far_geom, far_patch, slots, near, const)
        arrays = [lax.all_gather(payload, ("vol", "dsg"), axis=0, tiled=True)]
        items = ((vol_count * dsg_count, 0, 0),)
    design = smooth(arrays, items, where, adjacency, per_owner, const)
    return far_dens.reshape(-1), design


def solution(mesh):
    return jax.shard_map(
        per_device,
        mesh=mesh,
        in_specs=(
            P("vol", None),
            P(None, ("vol", "dsg")),
            P(("vol", "dsg"), None),
            P(("vol", "dsg")),
            P(("vol", "dsg")),
            P(None, ("vol", "dsg")),
            P(("vol", "dsg")),
            P(("vol", "dsg")),
            P(),
        ),
        out_specs=(P(("vol", "dsg")), P("dsg", None, None)),
        check_vma=False,
    )
```
